128 devices in a mesh: dp: 32 (over x, y, z_hi), tensor: 4 (over z_lo, core).
Axes of the slice: x: 4, y: 4, z: 4 (z_hi: 2, z_lo: 2; z = z_hi * 2 + z_lo), core: 2. Of those that a mesh axis runs over, the one named last changes fastest.
Arguments:
- image: bfloat16 [64, 256, 2048], P('dp'), may hold values from -6 to 6
- text: bfloat16 [64, 16, 4096], P('dp'), may hold values from -6 to 6
- masked: int32 [64, 256], P('dp'), may hold values 0 or 1
- text_len: int32 [64], P('dp'), may hold values from 1 to 16, as said below
- cotangent: bfloat16 [64, 256, 2048], P('dp'), may hold values from -6 to 6
- self_query: bfloat16 [2048, 2048], P(None, 'tensor'), may hold values from -0.1875 to 0.1875
- self_key: bfloat16 [2048, 2048], P(None, 'tensor'), may hold values from -0.1875 to 0.1875
- self_value: bfloat16 [2048, 2048], P(None, 'tensor'), may hold values from -0.125 to 0.125
- self_output: bfloat16 [2048, 2048], P('tensor'), may hold values from -0.25 to 0.25
- text_query: bfloat16 [2048, 2048], P(None, 'tensor'), may hold values from -0.1875 to 0.1875
- text_key: bfloat16 [4096, 2048], P(None, 'tensor'), may hold values from -0.125 to 0.125
- text_value: bfloat16 [4096, 2048], P(None, 'tensor'), may hold values from -0.09375 to 0.09375
- text_output: bfloat16 [2048, 2048], P('tensor'), may hold values from -0.25 to 0.25
- expand: bfloat16 [2048, 8192], P(None, 'tensor'), may hold values from -0.125 to 0.125
- contract: bfloat16 [8192, 2048], P('tensor'), may hold values from -0.09375 to 0.09375
- first_gain: float32 [2048], replicated, may hold values from 0.1 to 1.9
- second_gain: float32 [2048], replicated, may hold values from 0.1 to 1.9
- third_gain: float32 [2048], replicated, may hold values from 0.1 to 1.9
- mask_token: float32 [2048], replicated, may hold values from -6 to 6
Outputs:
- layer_out: bfloat16 [64, 256, 2048], P('dp')
- image_grad: bfloat16 [64, 256, 2048], P('dp')
- self_query_grad: float32 [2048, 2048], P('dp', 'tensor')
- self_key_grad: float32 [2048, 2048], P('dp', 'tensor')
- self_value_grad: float32 [2048, 2048], P('dp', 'tensor')
- self_output_grad: float32 [2048, 2048], P('tensor', 'dp')
- text_query_grad: float32 [2048, 2048], P('dp', 'tensor')
- text_key_grad: float32 [4096, 2048], P('dp', 'tensor')
- text_value_grad: float32 [4096, 2048], P('dp', 'tensor')
- text_output_grad: float32 [2048, 2048], P('tensor', 'dp')
- expand_grad: float32 [2048, 8192], P('dp', 'tensor')
- contract_grad: float32 [8192, 2048], P('tensor', 'dp')
- first_gain_grad: float32 [2048], P('dp')
- second_gain_grad: float32 [2048], P('dp')
- third_gain_grad: float32 [2048], P('dp')
- mask_token_grad: float32 [2048], P('dp')
The draws below stay inside these ranges and needn't reach their ends.
Inputs may be any that keep to these rules, and one draw needn't show every extreme that they name: One item, drawn from the seed, has text_len = 16.
All inputs are finite; a program needn't handle non-finite values. No bound on the sum of `masked` on one device may be relied on, other than what follows from the above.
Results may differ from the reference program's by a relative error of at most 0.025.
The reference program's roundings to bfloat16 on the way count: a program that leaves them out, or rounds other values in their place, can miss the bound.
Values sent between devices are 32-bit elements; how exact they have to be, the bound alone decides.
A program may use at most 320 MiB of HBM per device.

```python
import jax
import jax.numpy as jnp
from jax import lax

D = 2048
HEADS = 16
HEAD = 128
FF = 8192
TXT_D = 4096
IMG = 256
TEXT = 16
ITEMS = 64


def draw_text_len(key, part):
    key = jax.random.fold_in(key, 11)
    first_key, second_key = jax.random.split(key)
    lengths = jax.random.randint(first_key, (ITEMS,), 1, TEXT + 1)
    chosen = jax.random.randint(second_key, (), 0, ITEMS)
    return jnp.where(jnp.arange(ITEMS) == chosen, TEXT, lengths).astype(jnp.int32)


def with_ends(drawn, rng, low, high):
    dims = drawn.shape
    spot = [jax.random.randint(jax.random.fold_in(rng, axis), (), 0, dims[axis]) for axis in range(len(dims))]
    drawn = drawn.at[tuple(spot)].set(low)
    longest = dims.index(max(dims))
    spot[longest] = (spot[longest] + 1) % dims[longest]
    return drawn.at[tuple(spot)].set(high)


def block_scale(stream_key, dims, cuts, low, high):
    level, own = 1.0, jax.random.fold_in(stream_key, 6)
    for dim, parts in cuts:
        draws = jnp.exp(jax.random.uniform(jax.random.fold_in(own, dim), (parts,), jnp.float32, low / len(cuts), high / len(cuts)))
        level = level * jnp.repeat(draws, dims[dim] // parts).reshape([-1 if axis == dim else 1 for axis in range(len(dims))])
    return level


def noise(rng, extent, scale, reach, shards=(), kind=jnp.bfloat16):
    values = scale * jax.random.normal(rng, extent, jnp.float32)
    if shards:
        values = values * block_scale(rng, extent, shards, -0.22, 0.18)
    return jnp.clip(values, -reach, reach).astype(kind)


def setup_inputs(seed: int = 0) -> dict:
    streams_of = jax.random.split(jax.random.key(seed), 20)
    image = noise(streams_of[0], (ITEMS, IMG, D), 1.0, 6.0, ((0, 32),))
    text = noise(streams_of[1], (ITEMS, TEXT, TXT_D), 1.0, 6.0, ((0, 32),))
    masked = with_ends((jax.random.randint(streams_of[2], (ITEMS, IMG), 0, 2) < 1).astype(jnp.int32), jax.random.fold_in(streams_of[2], 1), 0, 1)
    text_len = draw_text_len(jax.random.fold_in(streams_of[19], 71), 0)
    cotangent = noise(streams_of[4], (ITEMS, IMG, D), 1.0, 6.0, ((0, 32),))
    self_query = noise(streams_of[5], (D, D), (D // 2) ** -0.5, 0.1875, ((1, 4),))
    self_key = noise(streams_of[6], (D, D), (D // 2) ** -0.5, 0.1875, ((1, 4),))
    self_value = noise(streams_of[7], (D, D), D ** -0.5, 0.125, ((1, 4),))
    self_output = noise(streams_of[8], (D, D), (D // 4) ** -0.5, 0.25, ((0, 4),))
    text_query = noise(streams_of[9], (D, D), (D // 2) ** -0.5, 0.1875, ((1, 4),))
    text_key = noise(streams_of[10], (TXT_D, D), (TXT_D // 2) ** -0.5, 0.125, ((1, 4),))
    text_value = noise(streams_of[11], (TXT_D, D), TXT_D ** -0.5, 0.09375, ((1, 4),))
    text_output = noise(streams_of[12], (D, D), (D // 4) ** -0.5, 0.25, ((0, 4),))
    expand = noise(streams_of[13], (D, FF), D ** -0.5, 0.125, ((1, 4),))
    contract = noise(streams_of[14], (FF, D), (FF // 2) ** -0.5, 0.09375, ((0, 4),))
    first_gain = jnp.clip(1.0 + 0.18 * jax.random.normal(streams_of[15], (D,), jnp.float32), 0.1, 1.9)
    second_gain = jnp.clip(1.0 + 0.18 * jax.random.normal(streams_of[16], (D,), jnp.float32), 0.1, 1.9)
    third_gain = jnp.clip(1.0 + 0.18 * jax.random.normal(streams_of[17], (D,), jnp.float32), 0.1, 1.9)
    mask_token = noise(streams_of[18], (D,), 1.0, 6.0, (), jnp.float32)
    return {"image": image, "text": text, "masked": masked, "text_len": text_len, "cotangent": cotangent, "self_query": self_query, "self_key": self_key, "self_value": self_value, "self_output": self_output, "text_query": text_query, "text_key": text_key, "text_value": text_value, "text_output": text_output, "expand": expand, "contract": contract, "first_gain": first_gain, "second_gain": second_gain, "third_gain": third_gain, "mask_token": mask_token}


@jax.custom_vjp
def low(v):
    return lax.optimization_barrier(v.astype(jnp.bfloat16)).astype(jnp.float32)

@jax.custom_vjp
def low_back(v):
    return v

def low_keep(v):
    return (low(v), None)

def low_pass(kept, grad):
    return (grad,)

def back_keep(v):
    return (v, None)

def back_low(kept, grad):
    return (low(grad),)
low.defvjp(low_keep, low_pass)
low_back.defvjp(back_keep, back_low)
PRECISE = lax.Precision.HIGHEST

def matmul(left, right):
    return jnp.dot(left, right, precision=PRECISE)

def rounded(value):
    return low_back(low(value))

def layer_norm(rows, gain):
    mean = lax.optimization_barrier(jnp.mean(rows, axis=-1, keepdims=True))
    centred = rows - mean
    spread = lax.optimization_barrier(jnp.mean(centred * centred, axis=-1, keepdims=True))
    return centred * lax.rsqrt(spread + 1e-05) * gain

def attend(query, keys, values, valid):
    heads_q = query.reshape(query.shape[0], HEADS, HEAD)
    heads_k = keys.reshape(keys.shape[0], HEADS, HEAD)
    heads_v = values.reshape(values.shape[0], HEADS, HEAD)
    scores = jnp.einsum('qhd,khd->hqk', heads_q, heads_k, precision=PRECISE) * HEAD ** (-0.5)
    scores = jnp.where(valid[None, None, :], low_back(scores), -1e+30)
    weights = low(jax.nn.softmax(scores, axis=-1))
    mixed = jnp.einsum('hqk,khd->qhd', weights, heads_v, precision=PRECISE)
    return rounded(mixed.reshape(query.shape[0], HEADS * HEAD))

def block(weights, smalls, rows, text_rows, masked_rows, length):
    w_sq, w_sk, w_sv, w_so, w_tq, w_tk, w_tv, w_to, w_up, w_down = weights
    gain_one, gain_two, gain_three, mask_vec = smalls
    start = jnp.where(masked_rows[:, None] == 1, mask_vec[None, :], rows)
    normed_one = low(layer_norm(start, gain_one))
    query = rounded(matmul(normed_one, w_sq))
    keys = rounded(matmul(normed_one, w_sk))
    values = rounded(matmul(normed_one, w_sv))
    every = jnp.arange(IMG) >= 0
    self_mixed = attend(query, keys, values, every)
    first = start + low_back(matmul(self_mixed, w_so))
    normed_two = low(layer_norm(first, gain_two))
    cross_query = rounded(matmul(normed_two, w_tq))
    cross_keys = rounded(matmul(text_rows, w_tk))
    cross_values = rounded(matmul(text_rows, w_tv))
    present = jnp.arange(TEXT) < length
    cross_mixed = attend(cross_query, cross_keys, cross_values, present)
    second = first + low_back(matmul(cross_mixed, w_to))
    normed_three = low(layer_norm(second, gain_three))
    raised = low_back(matmul(normed_three, w_up))
    active = low(jax.nn.gelu(raised))
    return second + low_back(matmul(active, w_down))

def reference(image, text, masked, text_len, cotangent, self_query, self_key, self_value, self_output, text_query, text_key, text_value, text_output, expand, contract, first_gain, second_gain, third_gain, mask_token):
    weights = tuple((w.astype(jnp.float32) for w in (self_query, self_key, self_value, self_output, text_query, text_key, text_value, text_output, expand, contract)))
    smalls = (first_gain, second_gain, third_gain, mask_token)

    def step(totals, item):
        rows, text_rows, masked_rows, length, upstream = item
        text_f = text_rows.astype(jnp.float32)

        def forward(w_all, s_all, x_rows):
            return block(w_all, s_all, x_rows, text_f, masked_rows, length)
        result, pull = jax.vjp(forward, weights, smalls, rows.astype(jnp.float32))
        grad_w, grad_s, grad_x = pull(upstream.astype(jnp.float32))
        totals = jax.tree.map(jnp.add, totals, (grad_w, grad_s))
        return (totals, (result.astype(jnp.bfloat16), grad_x.astype(jnp.bfloat16)))
    zeros = jax.tree.map(jnp.zeros_like, (weights, smalls))
    (grad_w, grad_s), (layer_out, image_grad) = lax.scan(step, zeros, (image, text, masked, text_len, cotangent))
    return (layer_out, image_grad, grad_w[0], grad_w[1], grad_w[2], grad_w[3], grad_w[4], grad_w[5], grad_w[6], grad_w[7], grad_w[8], grad_w[9], grad_s[0], grad_s[1], grad_s[2], grad_s[3])
```

```python
import jax
import jax.numpy as jnp
from jax import lax
from jax.sharding import PartitionSpec as P

HEAD = 128
EPS = 1e-05

CORE = [(t, t ^ 1) for t in range(4)]
ZLO = [(t, t ^ 2) for t in range(4)]
ZHI = [(d, d ^ 1) for d in range(32)]


def along_x(step):
    return [(d, ((d // 8 + step) % 4) * 8 + d % 8) for d in range(32)]


def along_y(step):
    return [(d, (d // 8) * 8 + ((d // 2 + step) % 4) * 2 + d % 2) for d in range(32)]


def product(left, right):
    return jnp.dot(left, right, preferred_element_type=jnp.float32)


def outer_sum(left, right):
    return lax.dot_general(
        left, right, (((0,), (0,)), ((), ())), preferred_element_type=jnp.float32
    )


def back_product(left, right):
    return lax.dot_general(
        left, right, (((1,), (1,)), ((), ())), preferred_element_type=jnp.float32
    )


def low(value):
    return value.astype(jnp.bfloat16)


def layer_norm(rows, gain):
    mean = jnp.mean(rows, axis=-1, keepdims=True)
    centred = rows - mean
    spread = jnp.mean(centred * centred, axis=-1, keepdims=True)
    return centred * lax.rsqrt(spread + EPS) * gain


def norm_back(rows, gain, grad):
    mean = jnp.mean(rows, axis=-1, keepdims=True)
    centred = rows - mean
    spread = jnp.mean(centred * centred, axis=-1, keepdims=True)
    root = lax.rsqrt(spread + EPS)
    xhat = centred * root
    scaled = grad * gain
    row_grad = root * (
        scaled
        - jnp.mean(scaled, axis=-1, keepdims=True)
        - xhat * jnp.mean(scaled * xhat, axis=-1, keepdims=True)
    )
    return row_grad, jnp.sum(grad * xhat, axis=0)


def heads_of(rows):
    return rows.reshape(rows.shape[0], rows.shape[1] // HEAD, HEAD)


def attend_scores(query, keys, valid):
    scores = jnp.einsum("qhd,khd->hqk", query, keys, preferred_element_type=jnp.float32)
    scores = scores * HEAD ** (-0.5)
    if valid is None:
        return scores
    return jnp.where(valid[None, None, :], scores, -1e30)


def attend_forward(query, keys, values, valid):
    query, keys, values = heads_of(query), heads_of(keys), heads_of(values)
    scores = attend_scores(query, keys, valid)
    total = jax.nn.logsumexp(scores, axis=-1, keepdims=True)
    weights_low = low(jnp.exp(scores - total))
    mixed = jnp.einsum("hqk,khd->qhd", weights_low, values, preferred_element_type=jnp.float32)
    return low(mixed).reshape(mixed.shape[0], -1), total


def attend_backward(query, keys, values, valid, total, upstream):
    query, keys, values = heads_of(query), heads_of(keys), heads_of(values)
    upstream = heads_of(upstream)
    scale = HEAD ** (-0.5)
    probs = jnp.exp(attend_scores(query, keys, valid) - total)
    grad_values = jnp.einsum(
        "hqk,qhd->khd", low(probs), upstream, preferred_element_type=jnp.float32
    )
    grad_probs = jnp.einsum("qhd,khd->hqk", upstream, values, preferred_element_type=jnp.float32)
    inner = jnp.sum(grad_probs * probs, axis=-1, keepdims=True)
    grad_scores = low(probs * (grad_probs - inner))
    grad_query = (
        jnp.einsum("hqk,khd->qhd", grad_scores, keys, preferred_element_type=jnp.float32) * scale
    )
    grad_keys = (
        jnp.einsum("hqk,qhd->khd", grad_scores, query, preferred_element_type=jnp.float32) * scale
    )
    flat = lambda v: low(v).reshape(v.shape[0], -1)
    return flat(grad_query), flat(grad_keys), flat(grad_values)


def core_swap(value):
    return lax.ppermute(value, "tensor", CORE)


def half_sum(part):
    half = part.shape[0] // 2
    mine = part[:half] + core_swap(part[half:])
    return mine + lax.ppermute(mine, "tensor", ZLO)


def whole(mine):
    other = core_swap(mine * 0.5) * 2.0
    return jnp.concatenate([mine, other], axis=0)


def ring_sum(piece, along):
    right = lambda v: lax.ppermute(v, "dp", along(1))
    left = lambda v: lax.ppermute(v, "dp", along(-1))
    far_right = right(piece(2, 0))
    far_left = left(piece(2, 1))
    near_right = right(piece(1, 1))
    near_left = left(piece(3, 0))
    last_right = right(piece(1, 0) + far_right)
    last_left = left(piece(3, 1) + far_left)
    return (
        piece(0, 0) + near_left + last_right,
        piece(0, 1) + near_right + last_left,
    )


class Place:
    def __init__(self):
        dp = lax.axis_index("dp")
        self.x, self.y, self.z = dp // 8, (dp // 2) % 4, dp % 2
        self.core = lax.axis_index("tensor") % 2

    def fold(self, left, right, x_first):
        rows, width = left.shape[0], right.shape[1]
        if x_first:
            blocks = left.reshape(rows, 8, 256).transpose(1, 0, 2)
            one, two, first, second = self.x, self.y, along_x, along_y
        else:
            blocks = (
                left.reshape(rows, 2, 2, 4, 128).transpose(3, 1, 0, 2, 4).reshape(8, rows, 256)
            )
            one, two, first, second = self.y, self.x, along_y, along_x

        def piece(k, h):
            index = ((one + k) % 4) * 2 + h
            block = lax.dynamic_index_in_dim(blocks, index, 0, keepdims=False)
            return outer_sum(block, right)

        halves = ring_sum(piece, first)
        return self.fold_second(jnp.concatenate(halves, axis=0), two, second)

    def fold_second(self, summed, two, second):
        unit = summed.shape[0] // 8

        def piece(k, h):
            return lax.dynamic_slice_in_dim(
                summed, ((two + k) % 4) * 2 * unit + h * unit, unit, axis=0
            )

        return self.fold_third(*ring_sum(piece, second))

    def fold_third(self, low_half, high_half):
        upper = self.z == 1
        keep = jnp.where(upper, high_half, low_half)
        send = jnp.where(upper, low_half, high_half)
        return keep + lax.ppermute(send, "dp", ZHI)

    def mine_first(self, rows):
        half = rows.shape[0] // 2
        first, second = rows[:half], rows[half:]
        odd = self.core == 1
        return jnp.concatenate(
            [jnp.where(odd, second, first), jnp.where(odd, first, second)], axis=0
        )


def everyone(value, along):
    return [value] + [lax.ppermute(value, "dp", along(k)) for k in (1, 2, 3)]


def exchange(blocks, place, along):
    pick = lambda k: lax.dynamic_index_in_dim(blocks, (place + k) % 4, 0, keepdims=False)
    return [pick(0)] + [lax.ppermute(pick(k), "dp", along(k)) for k in (1, 2, 3)]


def shards(
    image,
    text,
    masked,
    text_len,
    cotangent,
    self_query,
    self_key,
    self_value,
    self_output,
    text_query,
    text_key,
    text_value,
    text_output,
    expand,
    contract,
    first_gain,
    second_gain,
    third_gain,
    mask_token,
):
    items, length, width = image.shape
    words = text.shape[1]
    half = length // 2
    place = Place()
    every = range(items)
    wide = jnp.float32

    text_rows = text.reshape(items * words, text.shape[2])
    cross_keys = low(product(text_rows, text_key))
    cross_values = low(product(text_rows, text_value))

    blocks = (text_rows.astype(wide) * 0.5).reshape(items * words, 4, -1).transpose(1, 0, 2)
    mine = jnp.concatenate(exchange(blocks, place.x, along_x), axis=0)
    blocks = mine.reshape(mine.shape[0], 4, -1).transpose(1, 0, 2)
    mine = jnp.concatenate(exchange(blocks, place.y, along_y), axis=0)
    text_columns = low(mine * 2.0)

    hidden, start, normed_one = [], [], []
    query, keys, values, self_rows, self_total = [], [], [], [], []
    first, normed_two = [], []
    for i in every:
        hidden.append(place.mine_first(masked[i].reshape(length, 1)) == 1)
        rows = place.mine_first(image[i]).astype(wide)
        start.append(jnp.where(hidden[i], mask_token[None, :], rows))
        normed_one.append(low(layer_norm(start[i], first_gain)))
        query.append(low(product(normed_one[i], self_query)))
        keys.append(low(product(normed_one[i], self_key)))
        values.append(low(product(normed_one[i], self_value)))
        mixed, total = attend_forward(query[i], keys[i], values[i], None)
        self_rows.append(mixed)
        self_total.append(total)
        first.append(start[i][:half] + half_sum(product(mixed, self_output)))
        normed_two.append(low(whole(layer_norm(first[i], second_gain))))

    cross_query, cross_rows, cross_total, present = [], [], [], []
    second, normed_three = [], []
    picked = lambda v, i: v[i * words : (i + 1) * words]
    for i in every:
        cross_query.append(low(product(normed_two[i], text_query)))
        present.append(jnp.arange(words) < text_len[i])
        mixed, total = attend_forward(
            cross_query[i], picked(cross_keys, i), picked(cross_values, i), present[i]
        )
        cross_rows.append(mixed)
        cross_total.append(total)
        second.append(first[i] + half_sum(product(mixed, text_output)))
        normed_three.append(low(whole(layer_norm(second[i], third_gain))))

    upstream, active, grad_raised = [], [], []
    grad_second, cross_out_grad = [], []
    third = 0.0
    for i in every:
        upstream.append(place.mine_first(cotangent[i]))
        raised = product(normed_three[i], expand)
        gelu, pull = jax.vjp(jax.nn.gelu, raised)
        active.append(low(gelu))
        grad_raised.append(low(pull(back_product(upstream[i], contract))[0]))
        grad = half_sum(back_product(grad_raised[i], expand))
        row_grad, gain_grad = norm_back(second[i], third_gain, grad)
        third = third + gain_grad
        grad_second.append(upstream[i][:half].astype(wide) + row_grad)
        cross_out_grad.append(low(whole(grad_second[i])))

    both = lambda parts: jnp.concatenate(parts, axis=0)
    contract_t = place.fold(both(upstream), both(active), False)
    expand_grad = place.fold(both(normed_three), both(grad_raised), True)
    text_output_t = place.fold(both(cross_out_grad), both(cross_rows), True)

    grad_cq, text_kv, grad_first, self_out_grad = [], [], [], []
    second_sum = 0.0
    for i in every:
        grad_mixed = low(back_product(cross_out_grad[i], text_output))
        grad_q, grad_k, grad_v = attend_backward(
            cross_query[i],
            picked(cross_keys, i),
            picked(cross_values, i),
            present[i],
            cross_total[i],
            grad_mixed,
        )
        grad_cq.append(grad_q)
        text_kv.append(jnp.concatenate([grad_k, grad_v], axis=1))
        grad = half_sum(back_product(grad_q, text_query))
        row_grad, gain_grad = norm_back(first[i], second_gain, grad)
        second_sum = second_sum + gain_grad
        grad_first.append(grad_second[i] + row_grad)
        self_out_grad.append(low(whole(grad_first[i])))

    text_query_grad = place.fold(both(normed_two), both(grad_cq), False)
    self_output_t = place.fold(both(self_out_grad), both(self_rows), True)

    gathered = jnp.concatenate(everyone(both(text_kv).astype(wide) * 0.5, along_x), axis=0)
    gathered = jnp.concatenate(everyone(gathered, along_y), axis=0)
    gathered = low(gathered * 2.0)
    text_grads = outer_sum(text_columns, gathered)
    middle = text_grads.shape[0] // 2
    text_grads = place.fold_third(text_grads[:middle], text_grads[middle:])

    grad_qkv, grad_start = [], []
    first_sum, mask_sum = 0.0, 0.0
    for i in every:
        grad_mixed = low(back_product(self_out_grad[i], self_output))
        grad_q, grad_k, grad_v = attend_backward(
            query[i], keys[i], values[i], None, self_total[i], grad_mixed
        )
        grad_qkv.append((grad_q, grad_k, grad_v))
        shares = (
            back_product(grad_q, self_query)
            + back_product(grad_k, self_key)
            + back_product(grad_v, self_value)
        )
        grad = half_sum(shares)
        row_grad, gain_grad = norm_back(start[i][:half], first_gain, grad)
        first_sum = first_sum + gain_grad
        result = grad_first[i] + row_grad
        mask_sum = mask_sum + jnp.sum(jnp.where(hidden[i][:half], result, 0.0), axis=0)
        grad_start.append(jnp.where(hidden[i][:half], 0.0, result))

    normed = both(normed_one)
    grad_q, grad_k, grad_v = [both(list(parts)) for parts in zip(*grad_qkv)]
    middle = grad_k.shape[1] // 2
    qk = place.fold(normed, jnp.concatenate([grad_q, grad_k[:, :middle]], axis=1), True)
    kv = place.fold(normed, jnp.concatenate([grad_k[:, middle:], grad_v], axis=1), False)
    cut = grad_q.shape[1]
    self_query_grad = qk[:, :cut]
    self_key_grad = jnp.concatenate([qk[:, cut:], kv[:, :middle]], axis=1)
    self_value_grad = kv[:, middle:]

    small = jnp.stack([first_sum, second_sum, third, mask_sum])
    small = small + core_swap(small)
    small = sum(everyone(small, along_x))
    small = sum(everyone(small, along_y))
    small = small + lax.ppermute(small, "dp", ZHI)
    share = width // 32
    small = lax.dynamic_slice_in_dim(small, lax.axis_index("dp") * share, share, axis=1)

    def finished(value):
        both_halves = whole(value)
        return low(place.mine_first(both_halves))

    layer_out = []
    for i in every:
        total = half_sum(product(active[i], contract))
        layer_out.append(finished(second[i] + total))
    image_grad = [finished(g) for g in grad_start]

    cut = text_grads.shape[1] // 2
    return (
        jnp.stack(layer_out),
        jnp.stack(image_grad),
        self_query_grad,
        self_key_grad,
        self_value_grad,
        self_output_t.T,
        text_query_grad,
        text_grads[:, :cut],
        text_grads[:, cut:],
        text_output_t.T,
        expand_grad,
        contract_t.T,
        small[0],
        small[1],
        small[2],
        small[3],
    )


def solution(mesh):
    rows, split = P("dp", None, None), P(None, "tensor")
    turned, grads, grads_t = P("tensor", None), P("dp", "tensor"), P("tensor", "dp")
    return jax.shard_map(
        shards,
        mesh=mesh,
        in_specs=(
            rows,
            rows,
            P("dp", None),
            P("dp"),
            rows,
            split,
            split,
            split,
            turned,
            split,
            split,
            split,
            turned,
            split,
            turned,
            P(),
            P(),
            P(),
            P(),
        ),
        out_specs=(
            rows,
            rows,
            grads,
            grads,
            grads,
            grads_t,
            grads,
            grads,
            grads,
            grads_t,
            grads,
            grads_t,
            P("dp"),
            P("dp"),
            P("dp"),
            P("dp"),
        ),
        check_vma=False,
    )
```

```python
import functools

import jax
import jax.numpy as jnp
from jax import lax
from jax.experimental import pallas as pl
from jax.experimental.pallas import tpu as pltpu
from jax.sharding import PartitionSpec as P

HEAD = 128
EPS = 1e-05
MESH = pl.DeviceIdType.MESH
F32, BF16 = jnp.float32, jnp.bfloat16
CHUNK = 64
JOB = 512


def product(left, right):
    return jnp.dot(left, right, preferred_element_type=F32)


def outer_sum(left, right):
    return lax.dot_general(left, right, (((0,), (0,)), ((), ())), preferred_element_type=F32)


def back_product(left, right):
    return lax.dot_general(left, right, (((1,), (1,)), ((), ())), preferred_element_type=F32)


def low(value):
    return value.astype(BF16)


def layer_norm(rows, gain):
    mean = jnp.mean(rows, axis=-1, keepdims=True)
    centred = rows - mean
    spread = jnp.mean(centred * centred, axis=-1, keepdims=True)
    return centred * lax.rsqrt(spread + EPS) * gain


def norm_back(rows, gain, grad):
    mean = jnp.mean(rows, axis=-1, keepdims=True)
    centred = rows - mean
    spread = jnp.mean(centred * centred, axis=-1, keepdims=True)
    root = lax.rsqrt(spread + EPS)
    xhat = centred * root
    scaled = grad * gain
    row_grad = root * (
        scaled
        - jnp.mean(scaled, axis=-1, keepdims=True)
        - xhat * jnp.mean(scaled * xhat, axis=-1, keepdims=True)
    )
    return row_grad, grad * xhat


def attend_scores(query, keys, valid):
    scores = jnp.einsum("bqhd,bkhd->bhqk", query, keys, preferred_element_type=F32)
    scores = scores * HEAD ** (-0.5)
    if valid is None:
        return scores
    return jnp.where(valid[:, None, None, :], scores, -1e30)


def attend_forward(query, keys, values, valid):
    scores = attend_scores(query, keys, valid)
    total = jax.nn.logsumexp(scores, axis=-1, keepdims=True)
    weights_low = low(jnp.exp(scores - total))
    mixed = jnp.einsum("bhqk,bkhd->bqhd", weights_low, values, preferred_element_type=F32)
    return low(mixed), total


def attend_backward(query, keys, values, valid, total, upstream):
    scale = HEAD ** (-0.5)
    probs = jnp.exp(attend_scores(query, keys, valid) - total)
    grad_values = jnp.einsum("bhqk,bqhd->bkhd", low(probs), upstream, preferred_element_type=F32)
    grad_probs = jnp.einsum("bqhd,bkhd->bhqk", upstream, values, preferred_element_type=F32)
    inner = jnp.sum(grad_probs * probs, axis=-1, keepdims=True)
    grad_scores = low(probs * (grad_probs - inner))
    grad_query = jnp.einsum("bhqk,bkhd->bqhd", grad_scores, keys, preferred_element_type=F32)
    grad_keys = jnp.einsum("bhqk,bqhd->bkhd", grad_scores, query, preferred_element_type=F32)
    return low(grad_query * scale), low(grad_keys * scale), low(grad_values)


class Net:
    def __init__(self, send, recv, local):
        dp, tensor = lax.axis_index("dp"), lax.axis_index("tensor")
        self.x, self.y, self.z = dp // 8, (dp // 2) % 4, dp % 2
        self.tensor, self.core = tensor, tensor % 2
        self.send, self.recv, self.local = send, recv, local
        self.sent, self.loads = 0, 0

    def device(self, kind, step=1):
        x, y, z, tensor = self.x, self.y, self.z, self.tensor
        if kind == "x":
            x = (x + step + 4) % 4
        elif kind == "y":
            y = (y + step + 4) % 4
        elif kind == "zhi":
            z = 1 - z
        elif kind == "zlo":
            tensor = (tensor + 2) % 4
        else:
            tensor = tensor + 1 - 2 * self.core
        return (x * 8 + y * 2 + z, tensor)

    def greet(self, partners):
        barrier = pltpu.get_barrier_semaphore()
        for kind, step in partners:
            pl.semaphore_signal(
                barrier, inc=1, device_id=self.device(kind, step), device_id_type=MESH
            )
        pl.semaphore_wait(barrier, len(partners))

    def push(self, source, target, kind, step=1):
        copy = pltpu.make_async_remote_copy(
            src_ref=source,
            dst_ref=target,
            send_sem=self.send.at[self.sent],
            recv_sem=self.recv.at[self.sent],
            device_id=self.device(kind, step),
            device_id_type=MESH,
        )
        self.sent += 1
        copy.start()
        return copy

    def load(self, source, target):
        copy = pltpu.make_async_copy(source, target, self.local.at[self.loads])
        self.loads += 1
        copy.start()
        return copy


def add_rows(target, *sources):
    rows = target.shape[0]
    step = 16 if target.shape[1] > 1024 else 32

    def body(i, carry):
        at = pl.ds(pl.multiple_of(i * step, step), step)
        value = target[at, :]
        for source in sources:
            value = value + source[at, :]
        target[at, :] = value
        return carry

    lax.fori_loop(0, rows // step, body, 0)


class Ring:
    SCRATCH = (
        ((6, 2, 128, JOB), F32),
        ((2, 2, 128, JOB), F32),
        ((4, 128, JOB), F32),
        ((6, 64, JOB), F32),
        ((64, JOB), F32),
    )
    COPIES, LOADS = 13, 4

    def __init__(self, net, grad, column, x_first, out, scratch):
        self.net, self.grad, self.out = net, grad, out
        self.columns = pl.ds(column * JOB, JOB)
        self.x_first = x_first
        self.axes = ("x", "y") if x_first else ("y", "x")
        self.one, self.two = (net.x, net.y) if x_first else (net.y, net.x)
        self.got, self.turn, self.own, self.got_two, self.got_three = scratch

    def piece(self, step, half):
        at = (self.one + step) % 4
        pair = pl.ds(2 * half, 2)
        if self.x_first:
            return self.grad.at[at, pair, :, self.columns]
        return self.grad.at[pair, at, :, self.columns]

    def begin(self):
        net, axis = self.net, self.axes[0]
        self.far = [
            net.push(self.piece(2, 0), self.got.at[0], axis, 1),
            net.push(self.piece(2, 1), self.got.at[1], axis, -1),
        ]
        self.loading = [
            net.load(self.piece(1, 0), self.turn.at[0]),
            net.load(self.piece(3, 1), self.turn.at[1]),
            net.load(self.piece(0, 0), self.own.at[pl.ds(0, 2)]),
            net.load(self.piece(0, 1), self.own.at[pl.ds(2, 2)]),
        ]

    def relay(self):
        net, axis = self.net, self.axes[0]
        self.last = []
        for i, step in enumerate((1, -1)):
            self.loading[i].wait()
            self.far[i].wait_recv()
            for j in range(2):
                add_rows(self.turn.at[i, j], self.got.at[i, j])
            self.last.append(net.push(self.turn.at[i], self.got.at[2 + i], axis, step))
        self.near = [
            net.push(self.piece(1, 1), self.got.at[4], axis, 1),
            net.push(self.piece(3, 0), self.got.at[5], axis, -1),
        ]

    def second(self):
        net, axis, own = self.net, self.axes[1], self.own
        for copy in self.loading[2:]:
            copy.wait()
        for copy in self.last + self.near:
            copy.wait_recv()
        for j in range(2):
            add_rows(own.at[j], self.got.at[5, j], self.got.at[2, j])
            add_rows(own.at[2 + j], self.got.at[4, j], self.got.at[3, j])
        self.part = lambda k, h: own.at[(self.two + k) % 4, pl.ds(h * 64, 64), :]
        got = self.got_two
        self.far_two = [
            net.push(self.part(2, 0), got.at[0], axis, 1),
            net.push(self.part(2, 1), got.at[1], axis, -1),
        ]
        self.near_two = [
            net.push(self.part(1, 1), got.at[4], axis, 1),
            net.push(self.part(3, 0), got.at[5], axis, -1),
        ]

    def relay_two(self):
        net, axis = self.net, self.axes[1]
        self.last_two = []
        for i, (step, at) in enumerate(((1, (1, 0)), (-1, (3, 1)))):
            self.far_two[i].wait_recv()
            add_rows(self.part(*at), self.got_two.at[i])
            self.last_two.append(net.push(self.part(*at), self.got_two.at[2 + i], axis, step))

    def third(self):
        net, got = self.net, self.got_two
        for copy in self.near_two + self.last_two:
            copy.wait_recv()
        add_rows(self.part(0, 0), got.at[5], got.at[2])
        add_rows(self.part(0, 1), got.at[4], got.at[3])
        whole = self.own.at[self.two]
        self.other = whole.at[pl.ds(pl.multiple_of((1 - net.z) * 64, 64), 64)]
        self.mine = whole.at[pl.ds(pl.multiple_of(net.z * 64, 64), 64)]
        self.final = net.push(self.other, self.got_three, "zhi")

    def finish(self):
        self.final.wait_recv()
        self.out[...] = self.mine[...] + self.got_three[...]
        for copy in self.far + self.last + self.near:
            copy.wait_send()
        for copy in self.far_two + self.last_two + self.near_two + [self.final]:
            copy.wait_send()


class TensorSum:
    SCRATCH = tuple(((256 // CHUNK, CHUNK, 2048), F32) for _ in range(4))
    COPIES, LOADS = 3 * (256 // CHUNK), 256 // CHUNK

    def __init__(self, net, share, epilogue, whole, scratch):
        self.net, self.share, self.epilogue, self.whole = net, share, epilogue, whole
        self.mine, self.got_core, self.got_z, self.got_rows = scratch
        self.steps = range(256 // CHUNK)

    def rows(self, core, step):
        return pl.ds(pl.multiple_of(core * 256 + step * CHUNK, CHUNK), CHUNK)

    def begin(self):
        net = self.net
        self.swaps = [
            net.push(self.share.at[self.rows(1 - net.core, j)], self.got_core.at[j], "core")
            for j in self.steps
        ]
        self.loading = [
            net.load(self.share.at[self.rows(net.core, j)], self.mine.at[j]) for j in self.steps
        ]

    def exchange(self):
        self.over = []
        for j in self.steps:
            self.loading[j].wait()
            self.swaps[j].wait_recv()
            add_rows(self.mine.at[j], self.got_core.at[j])
            self.over.append(self.net.push(self.mine.at[j], self.got_z.at[j], "zlo"))

    def work(self):
        net = self.net
        self.spread = []
        for j in self.steps:
            self.over[j].wait_recv()

            def body(i, carry, j=j):
                at = pl.ds(pl.multiple_of(i * 8, 8), 8)
                rows = pl.ds(pl.multiple_of(j * CHUNK + i * 8, 8), 8)
                self.got_core[j, at, :] = self.epilogue(
                    rows, self.mine[j, at, :] + self.got_z[j, at, :]
                )
                return carry

            lax.fori_loop(0, CHUNK // 8, body, 0)
            self.spread.append(net.push(self.got_core.at[j], self.got_rows.at[j], "core"))
            self.round(self.got_core, j, net.core)

    def round(self, source, step, core):
        def body(i, carry):
            at = pl.ds(pl.multiple_of(i * 16, 16), 16)
            rows = pl.ds(pl.multiple_of(core * 256 + step * CHUNK + i * 16, 16), 16)
            self.whole[rows, :] = source[step, at, :].astype(BF16)
            return carry

        lax.fori_loop(0, CHUNK // 16, body, 0)

    def finish(self):
        for j in self.steps:
            self.spread[j].wait_recv()
            self.round(self.got_rows, j, 1 - self.net.core)
        for copy in self.swaps + self.over + self.spread:
            copy.wait_send()


NEAR = [("core", 1), ("zlo", 1)]
RING = [("x", 1), ("x", -1), ("y", 1), ("y", -1)]
ALL = [("x", 1), ("x", 2), ("x", 3), ("y", 1), ("y", 2), ("y", 3)]


def vmem(shapes):
    return [pltpu.VMEM(shape, kind) for shape, kind in shapes]


def call(body, ins, outs, scratch, copies, loads, number, name):
    spec = lambda inside: pl.BlockSpec(memory_space=pltpu.VMEM if inside else pl.ANY)
    return pl.pallas_call(
        body,
        name=name,
        out_shape=outs,
        in_specs=[spec(inside) for _, inside in ins],
        out_specs=[spec(True) for _ in outs],
        scratch_shapes=vmem(scratch)
        + [
            pltpu.SemaphoreType.DMA((copies,)),
            pltpu.SemaphoreType.DMA((copies,)),
            pltpu.SemaphoreType.DMA((max(loads, 1),)),
        ],
        compiler_params=pltpu.CompilerParams(
            collective_id=number, has_side_effects=True, vmem_limit_bytes=60 * 2**20
        ),
    )(*[array for array, _ in ins])


def shape(*dims, kind=F32):
    return jax.ShapeDtypeStruct(dims, kind)


def sum_and_norm(share, rows, gain, text_blocks, number):
    with_text = text_blocks is not None
    scratch = list(TensorSum.SCRATCH)
    ins = [(share, False), (rows, True), (gain, True)]
    outs = [shape(256, 2048), shape(512, 2048, kind=BF16)]
    copies, loads = TensorSum.COPIES, TensorSum.LOADS
    if with_text:
        ins.append((text_blocks, False))
        outs.append(shape(4, 4, 32, 256))
        scratch.append(((4, 32, 1024), F32))
        copies, loads = copies + 6, loads + 2

    def body(*refs):
        refs = list(refs)
        share_ref, rows_ref, gain_ref = refs[:3]
        text_ref = refs[3] if with_text else None
        outs_at = len(ins)
        total_ref, normed_ref = refs[outs_at : outs_at + 2]
        columns_ref = refs[outs_at + 2] if with_text else None
        scratch_at = outs_at + len(outs)
        net = Net(*refs[-3:])
        net.greet(NEAR + (ALL if with_text else []))

        def epilogue(at, total):
            total = rows_ref[at, :] + total
            total_ref[at, :] = total
            return layer_norm(total, gain_ref[...])

        work = TensorSum(net, share_ref, epilogue, normed_ref, refs[scratch_at : scratch_at + 4])
        work.begin()
        if with_text:
            got = refs[scratch_at + 4]
            own = net.load(text_ref.at[net.x], got.at[0])
            first = [
                net.push(text_ref.at[(net.x + k) % 4], got.at[k], "x", k) for k in (1, 2, 3)
            ]
        work.exchange()
        if with_text:
            own.wait()
            for copy in first:
                copy.wait_recv()
            cut = lambda y: pl.ds(pl.multiple_of(y * 256, 256), 256)
            kept = net.load(got.at[:, :, cut(net.y)], columns_ref.at[0])
            second = [
                net.push(got.at[:, :, cut((net.y + k) % 4)], columns_ref.at[k], "y", k)
                for k in (1, 2, 3)
            ]
        work.work()
        work.finish()
        if with_text:
            kept.wait()
            for copy in second:
                copy.wait_recv()
            for copy in first + second:
                copy.wait_send()

    return call(body, ins, outs, scratch, copies, loads, number, f"forward_sum_{number}")


def run_rings(rings, between):
    begin, first, second, third = between
    for ring in rings:
        ring.begin()
    begin()
    for ring in rings:
        ring.relay()
    first()
    for ring in rings:
        ring.second()
    second()
    for ring in rings:
        ring.relay_two()
    for ring in rings:
        ring.third()
    third()
    for ring in rings:
        ring.finish()


def ring_scratch(count):
    return [(s, k) for _ in range(count) for s, k in Ring.SCRATCH]


def take(refs, counts):
    out, at = [], 0
    for count in counts:
        out.append(refs[at : at + count])
        at += count
    return out


def backward_wide(share, x_rows, gain, extra, grad, number, more):
    grad = grad.reshape(4, 4, 128, 2048)
    ins = [(share, False), (x_rows, True), (gain, True), (extra, True), (grad, False)]
    outs = [shape(256, 2048), shape(512, 2048, kind=BF16), shape(8, 2048)]
    outs += [shape(64, JOB)] * 4
    scratch = ring_scratch(4) + list(TensorSum.SCRATCH)
    copies = 4 * Ring.COPIES + TensorSum.COPIES
    loads = 4 * Ring.LOADS + TensorSum.LOADS
    kind = more[0]
    if kind == "out":
        ins += [(more[1], False), (more[2], True)]
        outs.append(shape(512, 2048, kind=BF16))
        scratch += list(TensorSum.SCRATCH)
        copies, loads = copies + TensorSum.COPIES, loads + TensorSum.LOADS
        partners = NEAR + RING + [("zhi", 1)]
    else:
        ins += [(more[1], False)]
        outs.append(shape(4, 4, 32, 1024))
        copies, loads = copies + 6, loads + 1
        partners = NEAR + ALL + [("zhi", 1)]
    n_rings = len(ring_scratch(4))

    def body(*refs):
        refs = list(refs)
        n_in, n_out = len(ins), len(outs)
        in_refs, out_refs = refs[:n_in], refs[n_in : n_in + n_out]
        work_refs = refs[n_in + n_out : -3]
        net = Net(*refs[-3:])
        net.greet(partners)
        share_ref, x_ref, gain_ref, extra_ref, grad_ref = in_refs[:5]
        rows_ref, low_ref, gain_sum = out_refs[:3]
        gain_sum[...] = jnp.zeros_like(gain_sum)

        def epilogue(at, total):
            row_grad, terms = norm_back(x_ref[at, :], gain_ref[...], total)
            gain_sum[...] += terms
            result = extra_ref[at, :] + row_grad
            rows_ref[at, :] = result
            return result

        work = TensorSum(net, share_ref, epilogue, low_ref, work_refs[n_rings : n_rings + 4])
        sets = take(work_refs, [len(Ring.SCRATCH)] * 4)
        rings = [
            Ring(net, grad_ref, i, i % 2 == 0, out_refs[3 + i], sets[i]) for i in range(4)
        ]
        if kind == "out":
            more_ref, added_ref = in_refs[5:7]
            other = TensorSum(
                net,
                more_ref,
                lambda at, total: added_ref[at, :] + total,
                out_refs[-1],
                work_refs[n_rings + 4 : n_rings + 8],
            )

            def begin():
                work.exchange()
                other.begin()

            def first():
                work.work()
                other.exchange()
                work.finish()

            def second():
                pass

            def third():
                other.work()
                other.finish()

            work.begin()
            run_rings(rings, (begin, first, second, third))
            return
        small_ref, all_ref = in_refs[5], out_refs[-1]
        state = {}

        def begin():
            work.exchange()

        def first():
            state["own"].wait()
            for copy in state["x"]:
                copy.wait_recv()
            state["y"] = [net.push(all_ref.at[0], all_ref.at[k], "y", k) for k in (1, 2, 3)]
            work.work()

        def second():
            work.finish()

        def third():
            for copy in state["y"]:
                copy.wait_recv()
            for copy in state["x"] + state["y"]:
                copy.wait_send()

        work.begin()
        state["own"] = net.load(small_ref, all_ref.at[0, 0])
        state["x"] = [net.push(small_ref, all_ref.at[0, k], "x", k) for k in (1, 2, 3)]
        run_rings(rings, (begin, first, second, third))

    name = f"backward_sum_{number}"
    return call(body, ins, outs, scratch, copies, loads, number, name)


def backward_last(share, x_rows, gain, extra, keep, grads, text_grad, sums, number):
    grads = [grad.reshape(4, 4, 128, -1) for grad in grads]
    jobs = [(i, c) for i, grad in enumerate(grads) for c in range(grad.shape[3] // JOB)]
    count = len(jobs)
    ins = [(share, False), (x_rows, True), (gain, True), (extra, True), (keep, True)]
    ins += [(text_grad, True), (sums, True)]
    ins += [(grad, False) for grad in grads]
    outs = [shape(512, 2048, kind=BF16), shape(8, 2048), shape(128, 1024)]
    outs += [shape(64, JOB)] * count
    scratch = ring_scratch(count) + list(TensorSum.SCRATCH)
    n_rings = len(ring_scratch(count))
    scratch += [((16, 2048), F32), ((128, 1024), F32), ((9, 8, 2048), F32)]
    copies = count * Ring.COPIES + TensorSum.COPIES + 9
    loads = count * Ring.LOADS + TensorSum.LOADS
    partners = NEAR + ALL + [("zhi", 1)]

    def body(*refs):
        refs = list(refs)
        n_in, n_out = len(ins), len(outs)
        in_refs, out_refs = refs[:n_in], refs[n_in : n_in + n_out]
        work_refs = refs[n_in + n_out : -3]
        net = Net(*refs[-3:])
        net.greet(partners)
        share_ref, x_ref, gain_ref, extra_ref, keep_ref, text_ref, sums_ref = in_refs[:7]
        image_ref, small_ref, text_out = out_refs[:3]
        acc_ref, got_text, got_small = work_refs[n_rings + 4 :]
        acc_ref[...] = jnp.zeros_like(acc_ref)

        def epilogue(at, total):
            row_grad, terms = norm_back(x_ref[at, :], gain_ref[...], total)
            result = extra_ref[at, :] + row_grad
            kept = keep_ref[at, :] > 0.5
            acc_ref[0:8, :] += terms
            acc_ref[8:16, :] += jnp.where(kept, 0.0, result)
            return jnp.where(kept, result, 0.0)

        work = TensorSum(net, share_ref, epilogue, image_ref, work_refs[n_rings : n_rings + 4])
        sets = take(work_refs, [len(Ring.SCRATCH)] * count)
        rings = [
            Ring(net, in_refs[7 + g], c, i % 2 == 0, out_refs[3 + i], sets[i])
            for i, (g, c) in enumerate(jobs)
        ]
        state = {}

        def begin():
            work.exchange()

        def first():
            work.work()

        def second():
            small_ref[...] = sums_ref[...]
            small_ref[0:1, :] = jnp.sum(acc_ref[0:8, :], axis=0, keepdims=True)
            small_ref[3:4, :] = jnp.sum(acc_ref[8:16, :], axis=0, keepdims=True)
            got_small[0] = small_ref[...]
            state["core"] = net.push(got_small.at[0], got_small.at[1], "core")
            state["text"] = net.push(
                text_ref.at[pl.ds(pl.multiple_of((1 - net.z) * 128, 128), 128)], got_text, "zhi"
            )
            work.finish()
            state["core"].wait()
            got_small[0] += got_small[1]
            state["x"] = [net.push(got_small.at[0], got_small.at[1 + k], "x", k) for k in (1, 2, 3)]

        def third():
            for copy in state["x"]:
                copy.wait()
            got_small[0] += got_small[2] + got_small[3] + got_small[4]
            state["y"] = [net.push(got_small.at[0], got_small.at[4 + k], "y", k) for k in (1, 2, 3)]
            for copy in state["y"]:
                copy.wait()
            got_small[0] += got_small[5] + got_small[6] + got_small[7]
            final = net.push(got_small.at[0], got_small.at[8], "zhi")
            final.wait()
            small_ref[...] = got_small[0] + got_small[8]
            state["text"].wait()
            mine = text_ref[pl.ds(pl.multiple_of(net.z * 128, 128), 128), :]
            text_out[...] = mine + got_text[...]

        work.begin()
        run_rings(rings, (begin, first, second, third))

    return call(body, ins, outs, scratch, copies, loads, number, "backward_last")


def shards(
    image,
    text,
    masked,
    text_len,
    cotangent,
    self_query,
    self_key,
    self_value,
    self_output,
    text_query,
    text_key,
    text_value,
    text_output,
    expand,
    contract,
    first_gain,
    second_gain,
    third_gain,
    mask_token,
):
    items, length, width = image.shape
    words = text.shape[1]
    count = items * length
    core = lax.axis_index("tensor") % 2
    heads = self_query.shape[1] // HEAD
    split = lambda rows: rows.reshape(items, -1, heads, HEAD)
    flat = lambda value: value.reshape(-1, heads * HEAD)
    gains = [g.reshape(1, width) for g in (first_gain, second_gain, third_gain)]
    own = lambda rows: lax.dynamic_slice_in_dim(rows, core * length, length, axis=0)

    text_rows = text.reshape(items * words, text.shape[2])
    cross_keys = split(low(product(text_rows, text_key)))
    cross_values = split(low(product(text_rows, text_value)))
    text_blocks = text_rows.astype(F32).reshape(items * words, 4, -1).transpose(1, 0, 2)

    hidden = masked.reshape(count, 1) == 1
    start = jnp.where(hidden, mask_token[None, :], image.reshape(count, width).astype(F32))
    normed_one = low(layer_norm(start, first_gain))
    query = split(low(product(normed_one, self_query)))
    keys = split(low(product(normed_one, self_key)))
    values = split(low(product(normed_one, self_value)))
    self_mixed, self_total = attend_forward(query, keys, values, None)
    self_rows = flat(self_mixed)
    start_own = own(start)
    first, normed_two, text_columns = sum_and_norm(
        product(self_rows, self_output), start_own, gains[1], text_blocks, 0
    )
    text_columns = low(text_columns.reshape(-1, text_columns.shape[-1]))

    cross_query = split(low(product(normed_two, text_query)))
    present = jnp.arange(words)[None, :] < text_len[:, None]
    cross_mixed, cross_total = attend_forward(cross_query, cross_keys, cross_values, present)
    cross_rows = flat(cross_mixed)
    second, normed_three = sum_and_norm(
        product(cross_rows, text_output), first, gains[2], None, 1
    )

    upstream = cotangent.reshape(count, width)
    raised = product(normed_three, expand)
    gelu, pull = jax.vjp(jax.nn.gelu, raised)
    active = low(gelu)
    grad_raised = low(pull(back_product(upstream, contract))[0])
    grad_second, cross_out_grad, third_sum, *contract_t, layer_out = backward_wide(
        back_product(grad_raised, expand),
        second,
        gains[2],
        own(upstream).astype(F32),
        outer_sum(upstream, active),
        2,
        ("out", product(active, contract), second),
    )

    grad_mixed = split(low(back_product(cross_out_grad, text_output)))
    grad_q, grad_k, grad_v = attend_backward(
        cross_query, cross_keys, cross_values, present, cross_total, grad_mixed
    )
    grad_cq = flat(grad_q)
    text_kv = jnp.concatenate([flat(grad_k), flat(grad_v)], axis=1).astype(F32)
    grad_first, self_out_grad, second_sum, *expand_grad, gathered = backward_wide(
        back_product(grad_cq, text_query),
        first,
        gains[1],
        grad_second,
        outer_sum(normed_three, grad_raised),
        3,
        ("text", text_kv),
    )
    gathered = low(gathered.reshape(-1, gathered.shape[-1]))
    text_grads = outer_sum(text_columns, gathered)

    grad_mixed = split(low(back_product(self_out_grad, self_output)))
    grad_q, grad_k, grad_v = map(
        flat, attend_backward(query, keys, values, None, self_total, grad_mixed)
    )
    shares = (
        back_product(grad_q, self_query)
        + back_product(grad_k, self_key)
        + back_product(grad_v, self_value)
    )
    sums = jnp.zeros((8, width), F32)
    sums = sums.at[1].set(jnp.sum(second_sum, axis=0)).at[2].set(jnp.sum(third_sum, axis=0))
    grads = [
        outer_sum(cross_out_grad, cross_rows),
        outer_sum(normed_two, grad_cq),
        outer_sum(self_out_grad, self_rows),
        outer_sum(normed_one, grad_q),
        outer_sum(normed_one, grad_k),
        outer_sum(normed_one, grad_v),
    ]
    keep = 1.0 - own(masked.reshape(count, 1)).astype(F32)
    image_grad, small, text_grads, to, tq, so, sq, sk, sv = backward_last(
        shares, start_own, gains[0], grad_first, keep, grads, text_grads, sums, 4
    )

    share = width // 32
    small = lax.dynamic_slice_in_dim(small, lax.axis_index("dp") * share, share, axis=1)
    cut = text_grads.shape[1] // 2
    joined = lambda parts: jnp.concatenate(parts, axis=1)
    return (
        layer_out.reshape(image.shape),
        image_grad.reshape(image.shape),
        sq,
        sk,
        sv,
        so.T,
        tq,
        text_grads[:, :cut],
        text_grads[:, cut:],
        to.T,
        joined(expand_grad),
        joined(contract_t).T,
        small[0],
        small[1],
        small[2],
        small[3],
    )


def solution(mesh):
    rows, split = P("dp", None, None), P(None, "tensor")
    turned, grads, grads_t = P("tensor", None), P("dp", "tensor"), P("tensor", "dp")
    ins = (rows, rows, P("dp", None), P("dp"), rows, split, split, split, turned)
    ins += (split, split, split, turned, split, turned, P(), P(), P(), P())
    outs = (rows, rows, grads, grads, grads, grads_t, grads, grads, grads, grads_t)
    outs += (grads, grads_t, P("dp"), P("dp"), P("dp"), P("dp"))
    return jax.shard_map(shards, mesh=mesh, in_specs=ins, out_specs=outs, check_vma=False)
```

```python
import functools

import jax
import jax.numpy as jnp
from jax import lax
from jax.experimental import pallas as pl
from jax.experimental.pallas import tpu as pltpu
from jax.sharding import PartitionSpec as P

HEAD = 128
EPS = 1e-05
MESH = pl.DeviceIdType.MESH
F32, BF16 = jnp.float32, jnp.bfloat16
CHUNK = 64
JOB = 512


def product(left, right):
    return jnp.dot(left, right, preferred_element_type=F32)


def outer_sum(left, right):
    return lax.dot_general(left, right, (((0,), (0,)), ((), ())), preferred_element_type=F32)


def back_product(left, right):
    return lax.dot_general(left, right, (((1,), (1,)), ((), ())), preferred_element_type=F32)


def low(value):
    return value.astype(BF16)


def layer_norm(rows, gain):
    mean = jnp.mean(rows, axis=-1, keepdims=True)
    centred = rows - mean
    spread = jnp.mean(centred * centred, axis=-1, keepdims=True)
    return centred * lax.rsqrt(spread + EPS) * gain


def norm_back(rows, gain, grad):
    mean = jnp.mean(rows, axis=-1, keepdims=True)
    centred = rows - mean
    spread = jnp.mean(centred * centred, axis=-1, keepdims=True)
    root = lax.rsqrt(spread + EPS)
    xhat = centred * root
    scaled = grad * gain
    row_grad = root * (
        scaled
        - jnp.mean(scaled, axis=-1, keepdims=True)
        - xhat * jnp.mean(scaled * xhat, axis=-1, keepdims=True)
    )
    return row_grad, grad * xhat


def attend_scores(query, keys, valid):
    scores = jnp.einsum("bqhd,bkhd->bhqk", query, keys, preferred_element_type=F32)
    scores = scores * HEAD ** (-0.5)
    if valid is None:
        return scores
    return jnp.where(valid[:, None, None, :], scores, -1e30)


def attend_forward(query, keys, values, valid):
    scores = attend_scores(query, keys, valid)
    total = jax.nn.logsumexp(scores, axis=-1, keepdims=True)
    weights_low = low(jnp.exp(scores - total))
    mixed = jnp.einsum("bhqk,bkhd->bqhd", weights_low, values, preferred_element_type=F32)
    return low(mixed), total


def attend_backward(query, keys, values, valid, total, upstream):
    scale = HEAD ** (-0.5)
    probs = jnp.exp(attend_scores(query, keys, valid) - total)
    grad_values = jnp.einsum("bhqk,bqhd->bkhd", low(probs), upstream, preferred_element_type=F32)
    grad_probs = jnp.einsum("bqhd,bkhd->bhqk", upstream, values, preferred_element_type=F32)
    inner = jnp.sum(grad_probs * probs, axis=-1, keepdims=True)
    grad_scores = low(probs * (grad_probs - inner))
    grad_query = jnp.einsum("bhqk,bkhd->bqhd", grad_scores, keys, preferred_element_type=F32)
    grad_keys = jnp.einsum("bhqk,bqhd->bkhd", grad_scores, query, preferred_element_type=F32)
    return low(grad_query * scale), low(grad_keys * scale), low(grad_values)


class Net:
    def __init__(self, send, recv, local):
        dp, tensor = lax.axis_index("dp"), lax.axis_index("tensor")
        self.x, self.y, self.z = dp // 8, (dp // 2) % 4, dp % 2
        self.tensor, self.core = tensor, tensor % 2
        self.send, self.recv, self.local = send, recv, local
        self.sent, self.loads = 0, 0

    def device(self, kind, step=1):
        x, y, z, tensor = self.x, self.y, self.z, self.tensor
        if kind == "x":
            x = (x + step + 4) % 4
        elif kind == "y":
            y = (y + step + 4) % 4
        elif kind == "zhi":
            z = 1 - z
        elif kind == "zlo":
            tensor = (tensor + 2) % 4
        else:
            tensor = tensor + 1 - 2 * self.core
        return (x * 8 + y * 2 + z, tensor)

    def greet(self, partners):
        barrier = pltpu.get_barrier_semaphore()
        for kind, step in partners:
            pl.semaphore_signal(
                barrier, inc=1, device_id=self.device(kind, step), device_id_type=MESH
            )
        pl.semaphore_wait(barrier, len(partners))

    def push(self, source, target, kind, step=1):
        copy = pltpu.make_async_remote_copy(
            src_ref=source,
            dst_ref=target,
            send_sem=self.send.at[self.sent],
            recv_sem=self.recv.at[self.sent],
            device_id=self.device(kind, step),
            device_id_type=MESH,
        )
        self.sent += 1
        copy.start()
        return copy

    def load(self, source, target):
        copy = pltpu.make_async_copy(source, target, self.local.at[self.loads])
        self.loads += 1
        copy.start()
        return copy


def add_rows(target, *sources):
    rows = target.shape[0]
    step = 16 if target.shape[1] > 1024 else 32

    def body(i, carry):
        at = pl.ds(pl.multiple_of(i * step, step), step)
        value = target[at, :]
        for source in sources:
            value = value + source[at, :]
        target[at, :] = value
        return carry

    lax.fori_loop(0, rows // step, body, 0)


class Ring:
    SCRATCH = (
        ((2, 2, 128, JOB), F32),
        ((2, 2, 128, JOB), F32),
        ((2, 2, 128, JOB), F32),
        ((4, 128, JOB), F32),
        ((6, 64, JOB), F32),
        ((64, JOB), F32),
    )
    COPIES = 13

    def __init__(self, net, left, right, column, x_first, out, scratch):
        self.net, self.left, self.right, self.out = net, left, right, out
        self.column = column * JOB
        self.x_first = x_first
        self.axes = ("x", "y") if x_first else ("y", "x")
        self.one, self.two = (net.x, net.y) if x_first else (net.y, net.x)
        self.sending, self.got, self.beside, self.own, self.got_two, self.got_three = scratch

    def piece(self, step, half, target, add=False):
        at = (self.one + step) % 4
        if self.x_first:
            left = self.left[:, pl.ds(pl.multiple_of(at * 512 + half * 256, 256), 256)]
        else:
            cut = lambda x: self.left[:, pl.ds(pl.multiple_of(x * 512 + at * 128, 128), 128)]
            left = jnp.concatenate([cut(2 * half), cut(2 * half + 1)], axis=1)
        for n in range(JOB // 256):
            value = outer_sum(left, self.right[:, pl.ds(self.column + n * 256, 256)])
            for j in range(2):
                part = value[j * 128 : (j + 1) * 128]
                if add:
                    part = part + target[j, :, pl.ds(n * 256, 256)]
                target[j, :, pl.ds(n * 256, 256)] = part

    def begin(self):
        net, axis = self.net, self.axes[0]
        self.far = []
        for half, step in enumerate((1, -1)):
            self.piece(2, half, self.sending.at[half])
            self.far.append(net.push(self.sending.at[half], self.got.at[half], axis, step))

    def relay(self):
        net, axis = self.net, self.axes[0]
        self.last, self.near = [], []
        for i, (step, at) in enumerate(((1, 1), (-1, 3))):
            self.far[i].wait_recv()
            self.piece(at, i, self.got.at[i], True)
            self.last.append(net.push(self.got.at[i], self.own.at[pl.ds(2 * i, 2)], axis, step))
        for i, (step, at) in enumerate(((1, 1), (-1, 3))):
            self.far[i].wait_send()
            self.piece(at, 1 - i, self.sending.at[i])
            self.near.append(net.push(self.sending.at[i], self.beside.at[1 - i], axis, step))

    def second(self):
        net, axis, own = self.net, self.axes[1], self.own
        for half in range(2):
            self.near[1 - half].wait_recv()
            self.piece(0, half, self.beside.at[half], True)
        for half in range(2):
            self.last[half].wait_recv()
            for j in range(2):
                add_rows(own.at[2 * half + j], self.beside.at[half, j])
        self.part = lambda k, h: own.at[(self.two + k) % 4, pl.ds(h * 64, 64), :]
        got = self.got_two
        self.far_two = [
            net.push(self.part(2, 0), got.at[0], axis, 1),
            net.push(self.part(2, 1), got.at[1], axis, -1),
        ]
        self.near_two = [
            net.push(self.part(1, 1), got.at[4], axis, 1),
            net.push(self.part(3, 0), got.at[5], axis, -1),
        ]

    def relay_two(self):
        net, axis = self.net, self.axes[1]
        self.last_two = []
        for i, (step, at) in enumerate(((1, (1, 0)), (-1, (3, 1)))):
            self.far_two[i].wait_recv()
            add_rows(self.part(*at), self.got_two.at[i])
            self.last_two.append(net.push(self.part(*at), self.got_two.at[2 + i], axis, step))

    def third(self):
        net, got = self.net, self.got_two
        for copy in self.near_two + self.last_two:
            copy.wait_recv()
        add_rows(self.part(0, 0), got.at[5], got.at[2])
        add_rows(self.part(0, 1), got.at[4], got.at[3])
        whole = self.own.at[self.two]
        self.other = whole.at[pl.ds(pl.multiple_of((1 - net.z) * 64, 64), 64)]
        self.mine = whole.at[pl.ds(pl.multiple_of(net.z * 64, 64), 64)]
        self.final = net.push(self.other, self.got_three, "zhi")

    def finish(self):
        self.final.wait_recv()
        self.out[...] = self.mine[...] + self.got_three[...]
        for copy in self.last + self.near:
            copy.wait_send()
        for copy in self.far_two + self.last_two + self.near_two + [self.final]:
            copy.wait_send()


class TensorSum:
    SCRATCH = tuple(((256 // CHUNK, CHUNK, 2048), F32) for _ in range(4))
    COPIES, LOADS = 3 * (256 // CHUNK), 256 // CHUNK

    def __init__(self, net, share, epilogue, whole, scratch):
        self.net, self.share, self.epilogue, self.whole = net, share, epilogue, whole
        self.mine, self.got_core, self.got_z, self.got_rows = scratch
        self.steps = range(256 // CHUNK)

    def rows(self, core, step):
        return pl.ds(pl.multiple_of(core * 256 + step * CHUNK, CHUNK), CHUNK)

    def begin(self):
        net = self.net
        self.swaps = [
            net.push(self.share.at[self.rows(1 - net.core, j)], self.got_core.at[j], "core")
            for j in self.steps
        ]
        self.loading = [
            net.load(self.share.at[self.rows(net.core, j)], self.mine.at[j]) for j in self.steps
        ]

    def exchange(self):
        self.over = []
        for j in self.steps:
            self.loading[j].wait()
            self.swaps[j].wait_recv()
            add_rows(self.mine.at[j], self.got_core.at[j])
            self.over.append(self.net.push(self.mine.at[j], self.got_z.at[j], "zlo"))

    def work(self):
        net = self.net
        self.spread = []
        for j in self.steps:
            self.over[j].wait_recv()

            def body(i, carry, j=j):
                at = pl.ds(pl.multiple_of(i * 8, 8), 8)
                rows = pl.ds(pl.multiple_of(j * CHUNK + i * 8, 8), 8)
                self.got_core[j, at, :] = self.epilogue(
                    rows, self.mine[j, at, :] + self.got_z[j, at, :]
                )
                return carry

            lax.fori_loop(0, CHUNK // 8, body, 0)
            self.spread.append(net.push(self.got_core.at[j], self.got_rows.at[j], "core"))
            self.round(self.got_core, j, net.core)

    def round(self, source, step, core):
        def body(i, carry):
            at = pl.ds(pl.multiple_of(i * 16, 16), 16)
            rows = pl.ds(pl.multiple_of(core * 256 + step * CHUNK + i * 16, 16), 16)
            self.whole[rows, :] = source[step, at, :].astype(BF16)
            return carry

        lax.fori_loop(0, CHUNK // 16, body, 0)

    def finish(self):
        for j in self.steps:
            self.spread[j].wait_recv()
            self.round(self.got_rows, j, 1 - self.net.core)
        for copy in self.swaps + self.over + self.spread:
            copy.wait_send()


NEAR = [("core", 1), ("zlo", 1)]
RING = [("x", 1), ("x", -1), ("y", 1), ("y", -1)]
ALL = [("x", 1), ("x", 2), ("x", 3), ("y", 1), ("y", 2), ("y", 3)]


def vmem(shapes):
    return [pltpu.VMEM(shape, kind) for shape, kind in shapes]


def call(body, ins, outs, scratch, copies, loads, number, name):
    spec = lambda inside: pl.BlockSpec(memory_space=pltpu.VMEM if inside else pl.ANY)
    return pl.pallas_call(
        body,
        name=name,
        out_shape=outs,
        in_specs=[spec(inside) for _, inside in ins],
        out_specs=[spec(True) for _ in outs],
        scratch_shapes=vmem(scratch)
        + [
            pltpu.SemaphoreType.DMA((copies,)),
            pltpu.SemaphoreType.DMA((copies,)),
            pltpu.SemaphoreType.DMA((max(loads, 1),)),
        ],
        compiler_params=pltpu.CompilerParams(
            collective_id=number, has_side_effects=True, vmem_limit_bytes=60 * 2**20
        ),
    )(*[array for array, _ in ins])


def shape(*dims, kind=F32):
    return jax.ShapeDtypeStruct(dims, kind)


def sum_and_norm(share, rows, gain, text_blocks, number):
    with_text = text_blocks is not None
    scratch = list(TensorSum.SCRATCH)
    ins = [(share, False), (rows, True), (gain, True)]
    outs = [shape(256, 2048), shape(512, 2048, kind=BF16)]
    copies, loads = TensorSum.COPIES, TensorSum.LOADS
    if with_text:
        ins.append((text_blocks, False))
        outs.append(shape(4, 4, 32, 256))
        scratch.append(((4, 32, 1024), F32))
        copies, loads = copies + 6, loads + 2

    def body(*refs):
        refs = list(refs)
        share_ref, rows_ref, gain_ref = refs[:3]
        text_ref = refs[3] if with_text else None
        outs_at = len(ins)
        total_ref, normed_ref = refs[outs_at : outs_at + 2]
        columns_ref = refs[outs_at + 2] if with_text else None
        scratch_at = outs_at + len(outs)
        net = Net(*refs[-3:])
        net.greet(NEAR + (ALL if with_text else []))

        def epilogue(at, total):
            total = rows_ref[at, :] + total
            total_ref[at, :] = total
            return layer_norm(total, gain_ref[...])

        work = TensorSum(net, share_ref, epilogue, normed_ref, refs[scratch_at : scratch_at + 4])
        work.begin()
        if with_text:
            got = refs[scratch_at + 4]
            own = net.load(text_ref.at[net.x], got.at[0])
            first = [
                net.push(text_ref.at[(net.x + k) % 4], got.at[k], "x", k) for k in (1, 2, 3)
            ]
        work.exchange()
        if with_text:
            own.wait()
            for copy in first:
                copy.wait_recv()
            cut = lambda y: pl.ds(pl.multiple_of(y * 256, 256), 256)
            kept = net.load(got.at[:, :, cut(net.y)], columns_ref.at[0])
            second = [
                net.push(got.at[:, :, cut((net.y + k) % 4)], columns_ref.at[k], "y", k)
                for k in (1, 2, 3)
            ]
        work.work()
        work.finish()
        if with_text:
            kept.wait()
            for copy in second:
                copy.wait_recv()
            for copy in first + second:
                copy.wait_send()

    return call(body, ins, outs, scratch, copies, loads, number, f"forward_sum_{number}")


def run_rings(rings, between):
    begin, first, second, third = between
    for ring in rings:
        ring.begin()
    begin()
    for ring in rings:
        ring.relay()
    first()
    for ring in rings:
        ring.second()
    second()
    for ring in rings:
        ring.relay_two()
    for ring in rings:
        ring.third()
    third()
    for ring in rings:
        ring.finish()


def ring_scratch(count):
    return [(s, k) for _ in range(count) for s, k in Ring.SCRATCH]


def take(refs, counts):
    out, at = [], 0
    for count in counts:
        out.append(refs[at : at + count])
        at += count
    return out


def backward_wide(share, x_rows, gain, extra, left, right, number, more):
    ins = [(share, False), (x_rows, True), (gain, True), (extra, True)]
    ins += [(left, True), (right, True)]
    outs = [shape(256, 2048), shape(512, 2048, kind=BF16), shape(8, 2048)]
    outs += [shape(64, JOB)] * 4
    scratch = ring_scratch(4) + list(TensorSum.SCRATCH)
    copies = 4 * Ring.COPIES + TensorSum.COPIES
    loads = TensorSum.LOADS
    kind = more[0]
    if kind == "out":
        ins += [(more[1], False), (more[2], True)]
        outs.append(shape(512, 2048, kind=BF16))
        scratch += list(TensorSum.SCRATCH)
        copies, loads = copies + TensorSum.COPIES, loads + TensorSum.LOADS
        partners = NEAR + RING + [("zhi", 1)]
    else:
        ins += [(more[1], False)]
        outs.append(shape(4, 4, 32, 1024))
        copies, loads = copies + 6, loads + 1
        partners = NEAR + ALL + [("zhi", 1)]
    n_rings = len(ring_scratch(4))

    def body(*refs):
        refs = list(refs)
        n_in, n_out = len(ins), len(outs)
        in_refs, out_refs = refs[:n_in], refs[n_in : n_in + n_out]
        work_refs = refs[n_in + n_out : -3]
        net = Net(*refs[-3:])
        net.greet(partners)
        share_ref, x_ref, gain_ref, extra_ref, left_ref, right_ref = in_refs[:6]
        rows_ref, low_ref, gain_sum = out_refs[:3]
        gain_sum[...] = jnp.zeros_like(gain_sum)

        def epilogue(at, total):
            row_grad, terms = norm_back(x_ref[at, :], gain_ref[...], total)
            gain_sum[...] += terms
            result = extra_ref[at, :] + row_grad
            rows_ref[at, :] = result
            return result

        work = TensorSum(net, share_ref, epilogue, low_ref, work_refs[n_rings : n_rings + 4])
        sets = take(work_refs, [len(Ring.SCRATCH)] * 4)
        rings = [
            Ring(net, left_ref, right_ref, i, i % 2 == 0, out_refs[3 + i], sets[i])
            for i in range(4)
        ]
        if kind == "out":
            more_ref, added_ref = in_refs[6:8]
            other = TensorSum(
                net,
                more_ref,
                lambda at, total: added_ref[at, :] + total,
                out_refs[-1],
                work_refs[n_rings + 4 : n_rings + 8],
            )

            def begin():
                work.exchange()
                other.begin()

            def first():
                work.work()
                other.exchange()
                work.finish()

            def second():
                pass

            def third():
                other.work()
                other.finish()

            work.begin()
            run_rings(rings, (begin, first, second, third))
            return
        small_ref, all_ref = in_refs[6], out_refs[-1]
        state = {}

        def begin():
            work.exchange()

        def first():
            state["own"].wait()
            for copy in state["x"]:
                copy.wait_recv()
            state["y"] = [net.push(all_ref.at[0], all_ref.at[k], "y", k) for k in (1, 2, 3)]
            work.work()

        def second():
            work.finish()

        def third():
            for copy in state["y"]:
                copy.wait_recv()
            for copy in state["x"] + state["y"]:
                copy.wait_send()

        work.begin()
        state["own"] = net.load(small_ref, all_ref.at[0, 0])
        state["x"] = [net.push(small_ref, all_ref.at[0, k], "x", k) for k in (1, 2, 3)]
        run_rings(rings, (begin, first, second, third))

    name = f"backward_sum_{number}"
    return call(body, ins, outs, scratch, copies, loads, number, name)


def backward_last(share, x_rows, gain, extra, keep, grads, text_grad, sums, number):
    lefts = []
    for left, _ in grads:
        if not any(left is other for other in lefts):
            lefts.append(left)
    where = [[left is other for other in lefts].index(True) for left, _ in grads]
    count = len(grads)
    ins = [(share, False), (x_rows, True), (gain, True), (extra, True), (keep, True)]
    ins += [(text_grad, True), (sums, True)]
    ins += [(left, True) for left in lefts] + [(right, True) for _, right in grads]
    outs = [shape(512, 2048, kind=BF16), shape(8, 2048), shape(128, 1024)]
    outs += [shape(64, JOB)] * count
    scratch = ring_scratch(count) + list(TensorSum.SCRATCH)
    n_rings = len(ring_scratch(count))
    scratch += [((16, 2048), F32), ((128, 1024), F32), ((9, 8, 2048), F32)]
    copies = count * Ring.COPIES + TensorSum.COPIES + 9
    loads = TensorSum.LOADS
    partners = NEAR + ALL + [("zhi", 1)]

    def body(*refs):
        refs = list(refs)
        n_in, n_out = len(ins), len(outs)
        in_refs, out_refs = refs[:n_in], refs[n_in : n_in + n_out]
        work_refs = refs[n_in + n_out : -3]
        net = Net(*refs[-3:])
        net.greet(partners)
        share_ref, x_ref, gain_ref, extra_ref, keep_ref, text_ref, sums_ref = in_refs[:7]
        image_ref, small_ref, text_out = out_refs[:3]
        acc_ref, got_text, got_small = work_refs[n_rings + 4 :]
        acc_ref[...] = jnp.zeros_like(acc_ref)

        def epilogue(at, total):
            row_grad, terms = norm_back(x_ref[at, :], gain_ref[...], total)
            result = extra_ref[at, :] + row_grad
            kept = keep_ref[at, :] > 0.5
            acc_ref[0:8, :] += terms
            acc_ref[8:16, :] += jnp.where(kept, 0.0, result)
            return jnp.where(kept, result, 0.0)

        work = TensorSum(net, share_ref, epilogue, image_ref, work_refs[n_rings : n_rings + 4])
        sets = take(work_refs, [len(Ring.SCRATCH)] * count)
        rings = [
            Ring(
                net,
                in_refs[7 + where[i]],
                in_refs[7 + len(lefts) + i],
                0,
                i % 2 == 0,
                out_refs[3 + i],
                sets[i],
            )
            for i in range(count)
        ]
        state = {}

        def begin():
            work.exchange()

        def first():
            work.work()

        def second():
            small_ref[...] = sums_ref[...]
            small_ref[0:1, :] = jnp.sum(acc_ref[0:8, :], axis=0, keepdims=True)
            small_ref[3:4, :] = jnp.sum(acc_ref[8:16, :], axis=0, keepdims=True)
            got_small[0] = small_ref[...]
            state["core"] = net.push(got_small.at[0], got_small.at[1], "core")
            state["text"] = net.push(
                text_ref.at[pl.ds(pl.multiple_of((1 - net.z) * 128, 128), 128)], got_text, "zhi"
            )
            work.finish()
            state["core"].wait()
            got_small[0] += got_small[1]
            state["x"] = [net.push(got_small.at[0], got_small.at[1 + k], "x", k) for k in (1, 2, 3)]

        def third():
            for copy in state["x"]:
                copy.wait()
            got_small[0] += got_small[2] + got_small[3] + got_small[4]
            state["y"] = [net.push(got_small.at[0], got_small.at[4 + k], "y", k) for k in (1, 2, 3)]
            for copy in state["y"]:
                copy.wait()
            got_small[0] += got_small[5] + got_small[6] + got_small[7]
            final = net.push(got_small.at[0], got_small.at[8], "zhi")
            final.wait()
            small_ref[...] = got_small[0] + got_small[8]
            state["text"].wait()
            mine = text_ref[pl.ds(pl.multiple_of(net.z * 128, 128), 128), :]
            text_out[...] = mine + got_text[...]

        work.begin()
        run_rings(rings, (begin, first, second, third))

    return call(body, ins, outs, scratch, copies, loads, number, "backward_last")


def shards(
    image,
    text,
    masked,
    text_len,
    cotangent,
    self_query,
    self_key,
    self_value,
    self_output,
    text_query,
    text_key,
    text_value,
    text_output,
    expand,
    contract,
    first_gain,
    second_gain,
    third_gain,
    mask_token,
):
    items, length, width = image.shape
    words = text.shape[1]
    count = items * length
    core = lax.axis_index("tensor") % 2
    heads = self_query.shape[1] // HEAD
    split = lambda rows: rows.reshape(items, -1, heads, HEAD)
    flat = lambda value: value.reshape(-1, heads * HEAD)
    gains = [g.reshape(1, width) for g in (first_gain, second_gain, third_gain)]
    own = lambda rows: lax.dynamic_slice_in_dim(rows, core * length, length, axis=0)

    text_rows = text.reshape(items * words, text.shape[2])
    cross_keys = split(low(product(text_rows, text_key)))
    cross_values = split(low(product(text_rows, text_value)))
    text_blocks = text_rows.astype(F32).reshape(items * words, 4, -1).transpose(1, 0, 2)

    hidden = masked.reshape(count, 1) == 1
    start = jnp.where(hidden, mask_token[None, :], image.reshape(count, width).astype(F32))
    normed_one = low(layer_norm(start, first_gain))
    query = split(low(product(normed_one, self_query)))
    keys = split(low(product(normed_one, self_key)))
    values = split(low(product(normed_one, self_value)))
    self_mixed, self_total = attend_forward(query, keys, values, None)
    self_rows = flat(self_mixed)
    start_own = own(start)
    first, normed_two, text_columns = sum_and_norm(
        product(self_rows, self_output), start_own, gains[1], text_blocks, 0
    )
    text_columns = low(text_columns.reshape(-1, text_columns.shape[-1]))

    cross_query = split(low(product(normed_two, text_query)))
    present = jnp.arange(words)[None, :] < text_len[:, None]
    cross_mixed, cross_total = attend_forward(cross_query, cross_keys, cross_values, present)
    cross_rows = flat(cross_mixed)
    second, normed_three = sum_and_norm(
        product(cross_rows, text_output), first, gains[2], None, 1
    )

    upstream = cotangent.reshape(count, width)
    raised = product(normed_three, expand)
    gelu, pull = jax.vjp(jax.nn.gelu, raised)
    active = low(gelu)
    grad_raised = low(pull(back_product(upstream, contract))[0])
    grad_second, cross_out_grad, third_sum, *contract_t, layer_out = backward_wide(
        back_product(grad_raised, expand),
        second,
        gains[2],
        own(upstream).astype(F32),
        upstream,
        active,
        2,
        ("out", product(active, contract), second),
    )

    grad_mixed = split(low(back_product(cross_out_grad, text_output)))
    grad_q, grad_k, grad_v = attend_backward(
        cross_query, cross_keys, cross_values, present, cross_total, grad_mixed
    )
    grad_cq = flat(grad_q)
    text_kv = jnp.concatenate([flat(grad_k), flat(grad_v)], axis=1).astype(F32)
    grad_first, self_out_grad, second_sum, *expand_grad, gathered = backward_wide(
        back_product(grad_cq, text_query),
        first,
        gains[1],
        grad_second,
        normed_three,
        grad_raised,
        3,
        ("text", text_kv),
    )
    gathered = low(gathered.reshape(-1, gathered.shape[-1]))
    text_grads = outer_sum(text_columns, gathered)

    grad_mixed = split(low(back_product(self_out_grad, self_output)))
    grad_q, grad_k, grad_v = map(
        flat, attend_backward(query, keys, values, None, self_total, grad_mixed)
    )
    shares = (
        back_product(grad_q, self_query)
        + back_product(grad_k, self_key)
        + back_product(grad_v, self_value)
    )
    sums = jnp.zeros((8, width), F32)
    sums = sums.at[1].set(jnp.sum(second_sum, axis=0)).at[2].set(jnp.sum(third_sum, axis=0))
    grads = [
        (cross_out_grad, cross_rows),
        (normed_two, grad_cq),
        (self_out_grad, self_rows),
        (normed_one, grad_q),
        (normed_one, grad_k),
        (normed_one, grad_v),
    ]
    keep = 1.0 - own(masked.reshape(count, 1)).astype(F32)
    image_grad, small, text_grads, to, tq, so, sq, sk, sv = backward_last(
        shares, start_own, gains[0], grad_first, keep, grads, text_grads, sums, 4
    )

    share = width // 32
    small = lax.dynamic_slice_in_dim(small, lax.axis_index("dp") * share, share, axis=1)
    cut = text_grads.shape[1] // 2
    joined = lambda parts: jnp.concatenate(parts, axis=1)
    return (
        layer_out.reshape(image.shape),
        image_grad.reshape(image.shape),
        sq,
        sk,
        sv,
        so.T,
        tq,
        text_grads[:, :cut],
        text_grads[:, cut:],
        to.T,
        joined(expand_grad),
        joined(contract_t).T,
        small[0],
        small[1],
        small[2],
        small[3],
    )


def solution(mesh):
    rows, split = P("dp", None, None), P(None, "tensor")
    turned, grads, grads_t = P("tensor", None), P("dp", "tensor"), P("tensor", "dp")
    ins = (rows, rows, P("dp", None), P("dp"), rows, split, split, split, turned)
    ins += (split, split, split, turned, split, turned, P(), P(), P(), P())
    outs = (rows, rows, grads, grads, grads, grads_t, grads, grads, grads, grads_t)
    outs += (grads, grads_t, P("dp"), P("dp"), P("dp"), P("dp"))
    return jax.shard_map(shards, mesh=mesh, in_specs=ins, out_specs=outs, check_vma=False)
```

```python
import functools

import jax
import jax.numpy as jnp
from jax import lax
from jax.experimental import pallas as pl
from jax.experimental.pallas import tpu as pltpu
from jax.sharding import PartitionSpec as P

HEAD = 128
EPS = 1e-05
MESH = pl.DeviceIdType.MESH
F32, BF16 = jnp.float32, jnp.bfloat16
CHUNK = 64
JOB = 512


def product(left, right):
    return jnp.dot(left, right, preferred_element_type=F32)


def outer_sum(left, right):
    return lax.dot_general(left, right, (((0,), (0,)), ((), ())), preferred_element_type=F32)


def back_product(left, right):
    return lax.dot_general(left, right, (((1,), (1,)), ((), ())), preferred_element_type=F32)


def low(value):
    return value.astype(BF16)


def layer_norm(rows, gain):
    mean = jnp.mean(rows, axis=-1, keepdims=True)
    centred = rows - mean
    spread = jnp.mean(centred * centred, axis=-1, keepdims=True)
    return centred * lax.rsqrt(spread + EPS) * gain


def norm_back(rows, gain, grad):
    mean = jnp.mean(rows, axis=-1, keepdims=True)
    centred = rows - mean
    spread = jnp.mean(centred * centred, axis=-1, keepdims=True)
    root = lax.rsqrt(spread + EPS)
    xhat = centred * root
    scaled = grad * gain
    row_grad = root * (
        scaled
        - jnp.mean(scaled, axis=-1, keepdims=True)
        - xhat * jnp.mean(scaled * xhat, axis=-1, keepdims=True)
    )
    return row_grad, grad * xhat


def attend_scores(query, keys, valid):
    scores = jnp.einsum("bqhd,bkhd->bhqk", query, keys, preferred_element_type=F32)
    scores = scores * HEAD ** (-0.5)
    if valid is None:
        return scores
    return jnp.where(valid[:, None, None, :], scores, -1e30)


def attend_forward(query, keys, values, valid):
    scores = attend_scores(query, keys, valid)
    total = jax.nn.logsumexp(scores, axis=-1, keepdims=True)
    weights_low = low(jnp.exp(scores - total))
    mixed = jnp.einsum("bhqk,bkhd->bqhd", weights_low, values, preferred_element_type=F32)
    return low(mixed), total


def attend_backward(query, keys, values, valid, total, upstream):
    scale = HEAD ** (-0.5)
    probs = jnp.exp(attend_scores(query, keys, valid) - total)
    grad_values = jnp.einsum("bhqk,bqhd->bkhd", low(probs), upstream, preferred_element_type=F32)
    grad_probs = jnp.einsum("bqhd,bkhd->bhqk", upstream, values, preferred_element_type=F32)
    inner = jnp.sum(grad_probs * probs, axis=-1, keepdims=True)
    grad_scores = low(probs * (grad_probs - inner))
    grad_query = jnp.einsum("bhqk,bkhd->bqhd", grad_scores, keys, preferred_element_type=F32)
    grad_keys = jnp.einsum("bhqk,bqhd->bkhd", grad_scores, query, preferred_element_type=F32)
    return low(grad_query * scale), low(grad_keys * scale), low(grad_values)


class Net:
    def __init__(self, send, recv, local, free):
        dp, tensor = lax.axis_index("dp"), lax.axis_index("tensor")
        self.x, self.y, self.z = dp // 8, (dp // 2) % 4, dp % 2
        self.tensor, self.core = tensor, tensor % 2
        self.send, self.recv, self.local, self.free = send, recv, local, free
        self.sent, self.loads, self.stores = 0, 0, []

    def device(self, kind, step=1):
        x, y, z, tensor = self.x, self.y, self.z, self.tensor
        if kind == "x":
            x = (x + step + 4) % 4
        elif kind == "y":
            y = (y + step + 4) % 4
        elif kind == "zhi":
            z = 1 - z
        elif kind == "zlo":
            tensor = (tensor + 2) % 4
        else:
            tensor = tensor + 1 - 2 * self.core
        return (x * 8 + y * 2 + z, tensor)

    def greet(self, partners):
        barrier = pltpu.get_barrier_semaphore()
        for kind, step in partners:
            pl.semaphore_signal(
                barrier, inc=1, device_id=self.device(kind, step), device_id_type=MESH
            )
        pl.semaphore_wait(barrier, len(partners))

    def release(self, kind):
        pl.semaphore_signal(self.free, inc=1, device_id=self.device(kind), device_id_type=MESH)

    def await_release(self):
        pl.semaphore_wait(self.free, 1)

    def push(self, source, target, kind, step=1):
        copy = pltpu.make_async_remote_copy(
            src_ref=source,
            dst_ref=target,
            send_sem=self.send.at[self.sent],
            recv_sem=self.recv.at[self.sent],
            device_id=self.device(kind, step),
            device_id_type=MESH,
        )
        self.sent += 1
        copy.start()
        return copy

    def load(self, source, target):
        copy = pltpu.make_async_copy(source, target, self.local.at[self.loads])
        self.loads += 1
        copy.start()
        return copy

    def store(self, out):
        self.stores.append(self.load(out.vmem, out.hbm))


class Late:
    def __init__(self, net, hbm, vmem):
        self.net, self.hbm, self.vmem, self.copy, self.here = net, hbm, vmem, None, False

    def start(self):
        self.copy = self.net.load(self.hbm, self.vmem)

    def ref(self):
        if self.copy is None:
            self.start()
        if not self.here:
            self.copy.wait()
            self.here = True
        return self.vmem


class Out:
    def __init__(self, hbm, vmem):
        self.hbm, self.vmem = hbm, vmem


def add_rows(target, *sources):
    rows = target.shape[0]
    step = 16 if target.shape[1] > 1024 else 32

    def body(i, carry):
        at = pl.ds(pl.multiple_of(i * step, step), step)
        value = target[at, :]
        for source in sources:
            value = value + source[at, :]
        target[at, :] = value
        return carry

    lax.fori_loop(0, rows // step, body, 0)


class RingOne:
    SCRATCH = (
        ((2, 2, 128, JOB), F32),
        ((2, 2, 128, JOB), F32),
        ((2, 2, 128, JOB), F32),
    )
    COPIES = 6

    def __init__(self, net, left, right, column, x_first, own, scratch):
        self.net, self.left, self.right, self.own = net, left, right, own
        self.column = column * JOB
        self.x_first = x_first
        self.axis, self.one = ("x", net.x) if x_first else ("y", net.y)
        self.sending, self.got, self.beside = scratch

    def piece(self, step, half, target, add=False):
        at = (self.one + step) % 4
        if self.x_first:
            left = self.left[:, pl.ds(pl.multiple_of(at * 512 + half * 256, 256), 256)]
        else:
            cut = lambda x: self.left[:, pl.ds(pl.multiple_of(x * 512 + at * 128, 128), 128)]
            left = jnp.concatenate([cut(2 * half), cut(2 * half + 1)], axis=1)
        for n in range(JOB // 256):
            value = outer_sum(left, self.right[:, pl.ds(self.column + n * 256, 256)])
            for j in range(2):
                part = value[j * 128 : (j + 1) * 128]
                if add:
                    part = part + target[j, :, pl.ds(n * 256, 256)]
                target[j, :, pl.ds(n * 256, 256)] = part

    def begin(self):
        self.far = []
        for half, step in enumerate((1, -1)):
            self.piece(2, half, self.sending.at[half])
            self.far.append(
                self.net.push(self.sending.at[half], self.got.at[half], self.axis, step)
            )

    def relay(self):
        net, axis = self.net, self.axis
        self.last, self.near = [], []
        for i, (step, at) in enumerate(((1, 1), (-1, 3))):
            self.far[i].wait_recv()
            self.piece(at, i, self.got.at[i], True)
            self.last.append(net.push(self.got.at[i], self.own.at[pl.ds(2 * i, 2)], axis, step))
        for i, (step, at) in enumerate(((1, 1), (-1, 3))):
            self.far[i].wait_send()
            self.piece(at, 1 - i, self.sending.at[i])
            self.near.append(net.push(self.sending.at[i], self.beside.at[1 - i], axis, step))

    def close(self):
        for half in range(2):
            self.near[1 - half].wait_recv()
            self.piece(0, half, self.beside.at[half], True)
        for half in range(2):
            self.last[half].wait_recv()
            for j in range(2):
                add_rows(self.own.at[2 * half + j], self.beside.at[half, j])

    def done(self):
        for copy in self.last + self.near:
            copy.wait_send()


class RingTwo:
    SCRATCH = (((6, 64, JOB), F32), ((64, JOB), F32))
    PARTS = (((4, 64, JOB), F32),)
    COPIES, LOADS = 7, 4

    def __init__(self, net, own, x_first, out, scratch, parts=None):
        self.net, self.own, self.out, self.parts = net, own, out, parts
        self.axis, self.two = ("y", net.y) if x_first else ("x", net.x)
        self.got, self.got_last = scratch

    def part(self, step, half):
        return self.own.at[(self.two + step) % 4, pl.ds(half * 64, 64), :]

    def begin(self):
        net, axis, got = self.net, self.axis, self.got
        self.far = [
            net.push(self.part(2, 0), got.at[0], axis, 1),
            net.push(self.part(2, 1), got.at[1], axis, -1),
        ]
        self.near = [
            net.push(self.part(1, 1), got.at[4], axis, 1),
            net.push(self.part(3, 0), got.at[5], axis, -1),
        ]
        self.read = [self.part(*at) for at in ((1, 0), (3, 1), (0, 0), (0, 1))]
        self.loading = []
        if self.parts is not None:
            self.loading = [net.load(ref, self.parts.at[i]) for i, ref in enumerate(self.read)]
            self.read = [self.parts.at[i] for i in range(4)]

    def relay(self):
        net, axis, got = self.net, self.axis, self.got
        self.last = []
        for copy in self.loading:
            copy.wait()
        for i, step in enumerate((1, -1)):
            self.far[i].wait_recv()
            add_rows(got.at[i], self.read[i])
            self.last.append(net.push(got.at[i], got.at[2 + i], axis, step))

    def third(self):
        net, got = self.net, self.got
        for copy in self.near + self.last:
            copy.wait_recv()
        add_rows(got.at[5], got.at[2], self.read[2])
        add_rows(got.at[4], got.at[3], self.read[3])
        self.final = net.push(got.at[4 + net.z], self.got_last, "zhi")

    def finish(self):
        self.final.wait_recv()
        self.out[...] = self.got[5 - self.net.z] + self.got_last[...]
        for copy in self.far + self.near + self.last + [self.final]:
            copy.wait_send()


class TensorSum:
    SCRATCH = tuple(((256 // CHUNK, CHUNK, 2048), F32) for _ in range(4))
    COPIES, LOADS = 3 * (256 // CHUNK), 256 // CHUNK

    def __init__(self, net, share, epilogue, whole, scratch):
        self.net, self.share, self.epilogue, self.whole = net, share, epilogue, whole
        self.mine, self.got_core, self.got_z, self.got_rows = scratch
        self.steps = range(256 // CHUNK)

    def rows(self, core, step):
        return pl.ds(pl.multiple_of(core * 256 + step * CHUNK, CHUNK), CHUNK)

    def begin(self):
        net = self.net
        self.swaps = [
            net.push(self.share.at[self.rows(1 - net.core, j)], self.got_core.at[j], "core")
            for j in self.steps
        ]
        self.loading = [
            net.load(self.share.at[self.rows(net.core, j)], self.mine.at[j]) for j in self.steps
        ]

    def exchange(self):
        self.over = []
        for j in self.steps:
            self.loading[j].wait()
            self.swaps[j].wait_recv()
            add_rows(self.mine.at[j], self.got_core.at[j])
            self.over.append(self.net.push(self.mine.at[j], self.got_z.at[j], "zlo"))

    def work(self):
        net = self.net
        self.spread = []
        for j in self.steps:
            self.over[j].wait_recv()

            def body(i, carry, j=j):
                at = pl.ds(pl.multiple_of(i * 8, 8), 8)
                rows = pl.ds(pl.multiple_of(j * CHUNK + i * 8, 8), 8)
                self.got_core[j, at, :] = self.epilogue(
                    rows, self.mine[j, at, :] + self.got_z[j, at, :]
                )
                return carry

            lax.fori_loop(0, CHUNK // 8, body, 0)
            self.spread.append(net.push(self.got_core.at[j], self.got_rows.at[j], "core"))
            self.round(self.got_core, j, net.core)

    def round(self, source, step, core):
        def body(i, carry):
            at = pl.ds(pl.multiple_of(i * 16, 16), 16)
            rows = pl.ds(pl.multiple_of(core * 256 + step * CHUNK + i * 16, 16), 16)
            self.whole[rows, :] = source[step, at, :].astype(BF16)
            return carry

        lax.fori_loop(0, CHUNK // 16, body, 0)

    def finish(self):
        for j in self.steps:
            self.spread[j].wait_recv()
            self.round(self.got_rows, j, 1 - self.net.core)
        for copy in self.swaps + self.over + self.spread:
            copy.wait_send()


NEAR = [("core", 1), ("zlo", 1)]
RING = [("x", 1), ("x", -1), ("y", 1), ("y", -1)]
ALL = [("x", 1), ("x", 2), ("x", 3), ("y", 1), ("y", 2), ("y", 3)]


def vmem(shapes):
    return [pltpu.VMEM(shape, kind) for shape, kind in shapes]


def call(body, ins, outs, scratch, copies, loads, number, name):
    spec = lambda how: pl.BlockSpec(memory_space=pltpu.VMEM if how == "vmem" else pl.ANY)
    late = [(a.shape, a.dtype) for a, how in ins if how == "load"]
    kept = [(o.shape, o.dtype) for o, how in outs if how == "store"]

    def kernel(*refs):
        refs, net = Refs(refs[:-4]), Net(*refs[-4:])
        in_refs, out_refs = refs.some(len(ins)), refs.some(len(outs))
        late_refs, kept_refs = refs.some(len(late)), refs.some(len(kept))
        in_refs = [
            Late(net, ref, late_refs.pop(0)) if how == "load" else ref
            for ref, (_, how) in zip(in_refs, ins)
        ]
        out_refs = [
            Out(ref, kept_refs.pop(0)) if how == "store" else ref
            for ref, (_, how) in zip(out_refs, outs)
        ]
        body(net, Refs(in_refs), Refs(out_refs), refs)
        for copy in net.stores:
            copy.wait()

    return pl.pallas_call(
        kernel,
        name=name,
        out_shape=[o for o, _ in outs],
        in_specs=[spec(how) for _, how in ins],
        out_specs=[spec(how) for _, how in outs],
        scratch_shapes=vmem(late + kept + list(scratch))
        + [
            pltpu.SemaphoreType.DMA((copies,)),
            pltpu.SemaphoreType.DMA((copies,)),
            pltpu.SemaphoreType.DMA((loads + len(late) + len(kept),)),
            pltpu.SemaphoreType.REGULAR,
        ],
        compiler_params=pltpu.CompilerParams(
            collective_id=number, has_side_effects=True, vmem_limit_bytes=60 * 2**20
        ),
    )(*[array for array, _ in ins])


def shape(*dims, kind=F32):
    return jax.ShapeDtypeStruct(dims, kind)


def blocks(count, width, body):
    def step(i, carry):
        body(pl.ds(pl.multiple_of(i * width, width), width))
        return carry

    lax.fori_loop(0, count, step, 0)


class Refs:
    def __init__(self, refs):
        self.refs = list(refs)

    def one(self):
        return self.refs.pop(0)

    def some(self, count):
        return [self.refs.pop(0) for _ in range(count)]


def forward_self(share, rows, gain, text_blocks, text_rows, text_key, text_value):
    ins = [(share, "hbm"), (rows, "load"), (gain, "vmem"), (text_blocks, "hbm")]
    ins += [(text_rows, "load"), (text_key, "load"), (text_value, "load")]
    outs = [(shape(256, 2048), "store"), (shape(512, 2048, kind=BF16), "store")]
    outs += [(shape(4, 4, 32, 256), "vmem")] + [(shape(32, 512, kind=BF16), "vmem")] * 2
    scratch = list(TensorSum.SCRATCH) + [((4, 32, 1024), F32)]

    def body(net, in_refs, out_refs, refs):
        share_ref, late_rows, gain_ref, text_ref, *late_text = in_refs.some(7)
        total, normed, columns_ref, *text_outs = out_refs.some(5)
        sum_scratch, got = refs.some(4), refs.one()
        net.greet(NEAR + ALL)
        rows_ref, total_ref = late_rows.vmem, total.vmem

        def epilogue(at, value):
            value = rows_ref[at, :] + value
            total_ref[at, :] = value
            return layer_norm(value, gain_ref[...])

        work = TensorSum(net, share_ref, epilogue, normed.vmem, sum_scratch)
        work.begin()
        own = net.load(text_ref.at[net.x], got.at[0])
        first = [net.push(text_ref.at[(net.x + k) % 4], got.at[k], "x", k) for k in (1, 2, 3)]
        late_rows.start()
        every(late_text, "start")
        work.exchange()
        own.wait()
        for copy in first:
            copy.wait_recv()
        cut = lambda y: pl.ds(pl.multiple_of(y * 256, 256), 256)
        kept = net.load(got.at[:, :, cut(net.y)], columns_ref.at[0])
        second = [
            net.push(got.at[:, :, cut((net.y + k) % 4)], columns_ref.at[k], "y", k)
            for k in (1, 2, 3)
        ]
        text_rows_ref = late_text[0].ref()
        for weight, out in zip(late_text[1:], text_outs):
            out[...] = low(product(text_rows_ref[...], weight.ref()[...]))
        late_rows.ref()
        work.work()
        net.store(total)
        work.finish()
        net.store(normed)
        kept.wait()
        for copy in second:
            copy.wait_recv()
        for copy in first + second:
            copy.wait_send()

    copies, loads = TensorSum.COPIES + 6, TensorSum.LOADS + 2
    return call(body, ins, outs, scratch, copies, loads, 0, "forward_self")


def forward_cross(share, rows, gain, upstream, contract):
    ins = [(share, "hbm"), (rows, "load"), (gain, "vmem"), (upstream, "load"), (contract, "load")]
    outs = [(shape(256, 2048), "store"), (shape(512, 2048, kind=BF16), "store")]
    outs += [(shape(512, 2048), "store")]
    scratch = list(TensorSum.SCRATCH)

    def body(net, in_refs, out_refs, refs):
        share_ref, late_rows, gain_ref, late_upstream, late_contract = in_refs.some(5)
        total, normed, grad = out_refs.some(3)
        net.greet(NEAR)
        rows_ref, total_ref = late_rows.vmem, total.vmem

        def epilogue(at, value):
            value = rows_ref[at, :] + value
            total_ref[at, :] = value
            return layer_norm(value, gain_ref[...])

        work = TensorSum(net, share_ref, epilogue, normed.vmem, refs.some(4))
        work.begin()
        every([late_upstream, late_contract, late_rows], "start")
        work.exchange()
        upstream_ref, contract_ref = late_upstream.ref(), late_contract.ref()

        def part(at):
            grad.vmem[:, at] = back_product(upstream_ref[...], contract_ref[at, :])

        blocks(8, 256, part)
        net.store(grad)
        late_rows.ref()
        work.work()
        net.store(total)
        work.finish()
        net.store(normed)

    return call(
        body, ins, outs, scratch, TensorSum.COPIES, TensorSum.LOADS, 1, "forward_cross"
    )


def norm_back_sum(net, share_ref, x_ref, gain_ref, extra_ref, rows_ref, low_ref, gain_sum, scratch):
    gain_sum[...] = jnp.zeros_like(gain_sum)

    def epilogue(at, total):
        row_grad, terms = norm_back(x_ref[at, :], gain_ref[...], total)
        gain_sum[...] += terms
        result = extra_ref[at, :] + row_grad
        rows_ref[at, :] = result
        return result

    return TensorSum(net, share_ref, epilogue, low_ref, scratch)


def every(parts, step):
    for part in parts:
        getattr(part, step)()


def backward_first(share, x_rows, gain, extra, left, right, contract):
    ins = [(share, "hbm"), (x_rows, "load"), (gain, "vmem"), (extra, "load"), (left, "load")]
    ins += [(right, "load"), (contract, "load")]
    outs = [(shape(256, 2048), "store"), (shape(512, 2048, kind=BF16), "store")]
    outs += [(shape(8, 2048), "vmem"), (shape(512, 2048), "store")]
    outs += [(shape(4, 128, JOB), "store")] * 4
    scratch = list(TensorSum.SCRATCH) + list(RingOne.SCRATCH) * 4

    def body(net, in_refs, out_refs, refs):
        share_ref, late_x, gain_ref, late_extra, late_left, late_right = in_refs.some(6)
        late_contract = in_refs.one()
        rows, lows, gain_sum, out_share, *owns = out_refs.some(8)
        sum_scratch = refs.some(4)
        rings = [
            RingOne(net, late_left.vmem, late_right.vmem, i, i % 2 == 0, owns[i].vmem, refs.some(3))
            for i in range(4)
        ]
        every([late_left, late_right], "start")
        net.greet(NEAR + RING)
        x_ref = late_x.vmem
        work = norm_back_sum(
            net, share_ref, x_ref, gain_ref, late_extra.vmem, rows.vmem, lows.vmem, gain_sum, sum_scratch
        )
        work.begin()
        every([late_contract, late_x, late_extra], "start")
        late_left.ref(), late_right.ref()
        every(rings, "begin")
        work.exchange()
        every(rings, "relay")
        right_ref, contract_ref = late_right.ref(), late_contract.ref()

        def part(at):
            out_share.vmem[:, at] = product(right_ref[...], contract_ref[:, at])

        blocks(8, 256, part)
        late_x.ref(), late_extra.ref()
        joins = jnp.where(net.tensor < 2, 1.0, 0.0)

        def join(i, carry):
            at = pl.ds(pl.multiple_of(i * 16, 16), 16)
            to = pl.ds(pl.multiple_of(net.core * 256 + i * 16, 16), 16)
            out_share.vmem[to, :] += x_ref[at, :] * joins
            return carry

        lax.fori_loop(0, 16, join, 0)
        net.store(out_share)
        work.work()
        net.store(rows)
        work.finish()
        net.store(lows)
        for ring, own in zip(rings, owns):
            ring.close()
            net.store(own)
        every(rings, "done")

    copies, loads = TensorSum.COPIES + 4 * RingOne.COPIES, TensorSum.LOADS
    return call(body, ins, outs, scratch, copies, loads, 2, "backward_first")


def grouped(pairs):
    lefts = []
    for left, _ in pairs:
        if not any(left is other for other in lefts):
            lefts.append(left)
    return lefts, [[left is other for other in lefts].index(True) for left, _ in pairs]


def backward_second(share, x_rows, gain, extra, owns, wide, narrow, text, out_share):
    pairs = [wide] + narrow
    ones = [(0, i, i % 2 == 0) for i in range(4)]
    ones += [(1 + i, 0, i % 2 == 0) for i in range(len(narrow))]
    ins = [(share, "hbm"), (x_rows, "load"), (gain, "vmem"), (extra, "load"), (text, "hbm")]
    ins += [(out_share, "hbm")] + [(own, "hbm") for own in owns]
    ins += [(array, "load") for pair in pairs for array in pair]
    outs = [(shape(256, 2048), "store"), (shape(512, 2048, kind=BF16), "store")]
    outs += [(shape(8, 2048), "vmem"), (shape(4, 4, 32, 1024), "vmem")]
    outs += [(shape(512, 2048, kind=BF16), "hbm")]
    outs += [(shape(64, JOB), "vmem")] * len(owns)
    outs += [(shape(4, 128, JOB), "store")] * len(ones)
    scratch = list(TensorSum.SCRATCH) + [TensorSum.SCRATCH[0]]
    scratch += list(RingTwo.SCRATCH + RingTwo.PARTS) * len(owns)
    scratch += list(RingOne.SCRATCH) * len(ones)

    def body(net, in_refs, out_refs, refs):
        share_ref, late_x, gain_ref, late_extra, text_ref, out_share_ref = in_refs.some(6)
        own_refs, late_pairs = in_refs.some(len(owns)), [in_refs.some(2) for _ in pairs]
        rows, lows, gain_sum, all_ref, layer_out = out_refs.some(5)
        final_refs, nexts = out_refs.some(len(owns)), out_refs.some(len(ones))
        mine, got_core, got_z, got_rows = refs.some(4)
        got_z_two = refs.one()
        twos = [
            RingTwo(net, own, i % 2 == 0, final_refs[i], refs.some(2), refs.one())
            for i, own in enumerate(own_refs)
        ]
        rings = [
            RingOne(
                net, *[late.vmem for late in late_pairs[p]], c, x_first, nexts[i].vmem, refs.some(3)
            )
            for i, (p, c, x_first) in enumerate(ones)
        ]
        for pair in late_pairs:
            every(pair, "start")
        net.greet(NEAR + ALL + [("zhi", 1)])
        work = norm_back_sum(
            net,
            share_ref,
            late_x.vmem,
            gain_ref,
            late_extra.vmem,
            rows.vmem,
            lows.vmem,
            gain_sum,
            (mine, got_core, got_z, got_rows),
        )
        layer = TensorSum(
            net,
            out_share_ref,
            lambda at, total: total,
            lows.vmem,
            (mine, got_core, got_z_two, got_rows),
        )
        work.begin()
        kept = net.load(text_ref, all_ref.at[0, 0])
        by_x = [net.push(text_ref, all_ref.at[0, k], "x", k) for k in (1, 2, 3)]
        every([late_x, late_extra], "start")
        for pair in late_pairs:
            every(pair, "ref")
        every(twos, "begin")
        every(rings, "begin")
        work.exchange()
        every(twos, "relay")
        every(rings, "relay")
        kept.wait()
        for copy in by_x:
            copy.wait_recv()
        by_y = [net.push(all_ref.at[0], all_ref.at[k], "y", k) for k in (1, 2, 3)]
        every([late_x, late_extra], "ref")
        work.work()
        net.store(rows)
        work.finish()
        net.release("core")
        lows_copy = net.load(lows.vmem, lows.hbm)
        net.await_release()
        layer.begin()
        layer.exchange()
        every(twos, "third")
        for ring, own in zip(rings[:2] + rings[4:], nexts[:2] + nexts[4:]):
            ring.close()
            net.store(own)
        every(twos, "finish")
        lows_copy.wait()
        layer.work()
        layer.finish()
        net.stores.append(net.load(lows.vmem, layer_out))
        for ring, own in zip(rings[2:4], nexts[2:4]):
            ring.close()
            net.store(own)
        for copy in by_y:
            copy.wait_recv()
        for copy in by_x + by_y:
            copy.wait_send()
        every(rings, "done")

    copies = 2 * TensorSum.COPIES + 6 + len(owns) * RingTwo.COPIES + len(ones) * RingOne.COPIES
    loads = 2 * TensorSum.LOADS + 2 + len(owns) * RingTwo.LOADS
    return call(body, ins, outs, scratch, copies, loads, 3, "backward_second")


def backward_last(share, x_rows, gain, extra, keep, owns, narrow, text_grad, sums):
    lefts, where = grouped(narrow)
    count = len(narrow)
    ins = [(share, "hbm"), (x_rows, "load"), (gain, "vmem"), (extra, "load"), (keep, "vmem")]
    ins += [(text_grad, "vmem"), (sums, "vmem")] + [(own, "hbm") for own in owns]
    ins += [(left, "load") for left in lefts] + [(right, "load") for _, right in narrow]
    outs = [(shape(512, 2048, kind=BF16), "store"), (shape(8, 2048), "vmem")]
    outs += [(shape(128, 1024), "vmem")] + [(shape(64, JOB), "vmem")] * (len(owns) + count)
    scratch = list(TensorSum.SCRATCH)
    scratch += [((16, 2048), F32), ((128, 1024), F32), ((9, 8, 2048), F32)]
    scratch += list(RingTwo.SCRATCH + RingTwo.PARTS) * len(owns)
    scratch += (list(RingTwo.SCRATCH + RingOne.SCRATCH) + [((4, 128, JOB), F32)]) * count

    def body(net, in_refs, out_refs, refs):
        share_ref, late_x, gain_ref, late_extra, keep_ref, text_ref, sums_ref = in_refs.some(7)
        own_refs = in_refs.some(len(owns))
        late_lefts, late_rights = in_refs.some(len(lefts)), in_refs.some(count)
        image, small_ref, text_out = out_refs.some(3)
        old_refs, new_refs = out_refs.some(len(owns)), out_refs.some(count)
        sum_scratch = refs.some(4)
        acc_ref, got_text, got_small = refs.some(3)
        old = [
            RingTwo(net, own, i % 2 == 0, old_refs[i], refs.some(2), refs.one())
            for i, own in enumerate(own_refs)
        ]
        ones, twos = [], []
        for i in range(count):
            two_scratch, one_scratch, own = refs.some(2), refs.some(3), refs.one()
            left, right = late_lefts[where[i]].vmem, late_rights[i].vmem
            ones.append(RingOne(net, left, right, 0, i % 2 == 0, own, one_scratch))
            twos.append(RingTwo(net, own, i % 2 == 0, new_refs[i], two_scratch))
        every(late_lefts + late_rights, "start")
        net.greet(NEAR + ALL + [("zhi", 1)])
        acc_ref[...] = jnp.zeros_like(acc_ref)
        x_ref, extra_ref = late_x.vmem, late_extra.vmem

        def epilogue(at, total):
            row_grad, terms = norm_back(x_ref[at, :], gain_ref[...], total)
            result = extra_ref[at, :] + row_grad
            kept = keep_ref[at, :] > 0.5
            acc_ref[0:8, :] += terms
            acc_ref[8:16, :] += jnp.where(kept, 0.0, result)
            return jnp.where(kept, result, 0.0)

        work = TensorSum(net, share_ref, epilogue, image.vmem, sum_scratch)
        work.begin()
        every([late_x, late_extra], "start")
        every(late_lefts + late_rights, "ref")
        every(old, "begin")
        every(ones, "begin")
        work.exchange()
        every(old, "relay")
        every(ones, "relay")
        every([late_x, late_extra], "ref")
        work.work()
        got_small[0] = sums_ref[...]
        got_small[0, 0:1, :] = jnp.sum(acc_ref[0:8, :], axis=0, keepdims=True)
        got_small[0, 3:4, :] = jnp.sum(acc_ref[8:16, :], axis=0, keepdims=True)
        by_core = net.push(got_small.at[0], got_small.at[1], "core")
        text_copy = net.push(
            text_ref.at[pl.ds(pl.multiple_of((1 - net.z) * 128, 128), 128)], got_text, "zhi"
        )
        work.finish()
        net.store(image)
        by_core.wait()
        got_small[0] += got_small[1]
        by_x = [net.push(got_small.at[0], got_small.at[1 + k], "x", k) for k in (1, 2, 3)]
        every(old, "third")
        for one, two in zip(ones, twos):
            one.close()
            two.begin()
        every(old, "finish")
        for copy in by_x:
            copy.wait()
        got_small[0] += got_small[2] + got_small[3] + got_small[4]
        by_y = [net.push(got_small.at[0], got_small.at[4 + k], "y", k) for k in (1, 2, 3)]
        every(twos, "relay")
        for copy in by_y:
            copy.wait()
        got_small[0] += got_small[5] + got_small[6] + got_small[7]
        by_z = net.push(got_small.at[0], got_small.at[8], "zhi")
        every(twos, "third")
        text_copy.wait()
        mine_text = text_ref[pl.ds(pl.multiple_of(net.z * 128, 128), 128), :]
        text_out[...] = mine_text + got_text[...]
        by_z.wait()
        small_ref[...] = got_small[0] + got_small[8]
        every(twos, "finish")
        every(ones, "done")

    copies = TensorSum.COPIES + 9 + (len(owns) + count) * RingTwo.COPIES + count * RingOne.COPIES
    loads = TensorSum.LOADS + len(owns) * RingTwo.LOADS
    return call(body, ins, outs, scratch, copies, loads, 4, "backward_last")


def shards(
    image,
    text,
    masked,
    text_len,
    cotangent,
    self_query,
    self_key,
    self_value,
    self_output,
    text_query,
    text_key,
    text_value,
    text_output,
    expand,
    contract,
    first_gain,
    second_gain,
    third_gain,
    mask_token,
):
    items, length, width = image.shape
    words = text.shape[1]
    count = items * length
    core = lax.axis_index("tensor") % 2
    heads = self_query.shape[1] // HEAD
    split = lambda rows: rows.reshape(items, -1, heads, HEAD)
    flat = lambda value: value.reshape(-1, heads * HEAD)
    gains = [g.reshape(1, width) for g in (first_gain, second_gain, third_gain)]
    own = lambda rows: lax.dynamic_slice_in_dim(rows, core * length, length, axis=0)

    text_rows = text.reshape(items * words, text.shape[2])
    text_blocks = text_rows.astype(F32).reshape(items * words, 4, -1).transpose(1, 0, 2)
    upstream = cotangent.reshape(count, width)

    hidden = masked.reshape(count, 1) == 1
    start = jnp.where(hidden, mask_token[None, :], image.reshape(count, width).astype(F32))
    normed_one = low(layer_norm(start, first_gain))
    query = split(low(product(normed_one, self_query)))
    keys = split(low(product(normed_one, self_key)))
    values = split(low(product(normed_one, self_value)))
    self_mixed, self_total = attend_forward(query, keys, values, None)
    self_rows = flat(self_mixed)
    start_own = own(start)
    first, normed_two, text_columns, cross_keys, cross_values = forward_self(
        product(self_rows, self_output),
        start_own,
        gains[1],
        text_blocks,
        text_rows,
        text_key,
        text_value,
    )
    cross_keys, cross_values = split(cross_keys), split(cross_values)
    text_columns = low(text_columns.reshape(-1, text_columns.shape[-1]))

    cross_query = split(low(product(normed_two, text_query)))
    present = jnp.arange(words)[None, :] < text_len[:, None]
    cross_mixed, cross_total = attend_forward(cross_query, cross_keys, cross_values, present)
    cross_rows = flat(cross_mixed)
    second, normed_three, grad_active = forward_cross(
        product(cross_rows, text_output), first, gains[2], upstream, contract
    )

    raised = product(normed_three, expand)
    gelu, pull = jax.vjp(jax.nn.gelu, raised)
    active = low(gelu)
    grad_raised = low(pull(grad_active)[0])
    grad_second, cross_out_grad, third_sum, out_share, *owns = backward_first(
        back_product(grad_raised, expand),
        second,
        gains[2],
        own(upstream).astype(F32),
        upstream,
        active,
        contract,
    )

    grad_mixed = split(low(back_product(cross_out_grad, text_output)))
    grad_q, grad_k, grad_v = attend_backward(
        cross_query, cross_keys, cross_values, present, cross_total, grad_mixed
    )
    grad_cq = flat(grad_q)
    text_kv = jnp.concatenate([flat(grad_k), flat(grad_v)], axis=1).astype(F32)
    grad_first, self_out_grad, second_sum, gathered, layer_out, *rest = backward_second(
        back_product(grad_cq, text_query),
        first,
        gains[1],
        grad_second,
        owns,
        (normed_three, grad_raised),
        [(cross_out_grad, cross_rows), (normed_two, grad_cq)],
        text_kv,
        out_share,
    )
    contract_t, owns = rest[:4], rest[4:]
    gathered = low(gathered.reshape(-1, gathered.shape[-1]))
    text_grads = outer_sum(text_columns, gathered)

    grad_mixed = split(low(back_product(self_out_grad, self_output)))
    grad_q, grad_k, grad_v = map(
        flat, attend_backward(query, keys, values, None, self_total, grad_mixed)
    )
    shares = (
        back_product(grad_q, self_query)
        + back_product(grad_k, self_key)
        + back_product(grad_v, self_value)
    )
    sums = jnp.zeros((8, width), F32)
    sums = sums.at[1].set(jnp.sum(second_sum, axis=0)).at[2].set(jnp.sum(third_sum, axis=0))
    keep = 1.0 - own(masked.reshape(count, 1)).astype(F32)
    image_grad, small, text_grads, *rest = backward_last(
        shares,
        start_own,
        gains[0],
        grad_first,
        keep,
        owns,
        [
            (self_out_grad, self_rows),
            (normed_one, grad_q),
            (normed_one, grad_k),
            (normed_one, grad_v),
        ],
        text_grads,
        sums,
    )
    expand_grad, (to, tq, so, sq, sk, sv) = rest[:4], rest[4:]

    share = width // 32
    small = lax.dynamic_slice_in_dim(small, lax.axis_index("dp") * share, share, axis=1)
    cut = text_grads.shape[1] // 2
    joined = lambda parts: jnp.concatenate(parts, axis=1)
    return (
        layer_out.reshape(image.shape),
        image_grad.reshape(image.shape),
        sq,
        sk,
        sv,
        so.T,
        tq,
        text_grads[:, :cut],
        text_grads[:, cut:],
        to.T,
        joined(expand_grad),
        joined(contract_t).T,
        small[0],
        small[1],
        small[2],
        small[3],
    )


def solution(mesh):
    rows, split = P("dp", None, None), P(None, "tensor")
    turned, grads, grads_t = P("tensor", None), P("dp", "tensor"), P("tensor", "dp")
    ins = (rows, rows, P("dp", None), P("dp"), rows, split, split, split, turned)
    ins += (split, split, split, turned, split, turned, P(), P(), P(), P())
    outs = (rows, rows, grads, grads, grads, grads_t, grads, grads, grads, grads_t)
    outs += (grads, grads_t, P("dp"), P("dp"), P("dp"), P("dp"))
    return jax.shard_map(shards, mesh=mesh, in_specs=ins, out_specs=outs, check_vma=False)
```

```python
import functools

import jax
import jax.numpy as jnp
from jax import lax
from jax.experimental import pallas as pl
from jax.experimental.pallas import tpu as pltpu
from jax.sharding import PartitionSpec as P

HEAD = 128
EPS = 1e-05
MESH = pl.DeviceIdType.MESH
F32, BF16 = jnp.float32, jnp.bfloat16
CHUNK = 64
JOB = 512


def product(left, right):
    return jnp.dot(left, right, preferred_element_type=F32)


def outer_sum(left, right):
    return lax.dot_general(left, right, (((0,), (0,)), ((), ())), preferred_element_type=F32)


def back_product(left, right):
    return lax.dot_general(left, right, (((1,), (1,)), ((), ())), preferred_element_type=F32)


def low(value):
    return value.astype(BF16)


def layer_norm(rows, gain):
    mean = jnp.mean(rows, axis=-1, keepdims=True)
    centred = rows - mean
    spread = jnp.mean(centred * centred, axis=-1, keepdims=True)
    return centred * lax.rsqrt(spread + EPS) * gain


def norm_back(rows, gain, grad):
    mean = jnp.mean(rows, axis=-1, keepdims=True)
    centred = rows - mean
    spread = jnp.mean(centred * centred, axis=-1, keepdims=True)
    root = lax.rsqrt(spread + EPS)
    xhat = centred * root
    scaled = grad * gain
    row_grad = root * (
        scaled
        - jnp.mean(scaled, axis=-1, keepdims=True)
        - xhat * jnp.mean(scaled * xhat, axis=-1, keepdims=True)
    )
    return row_grad, grad * xhat


def attend_probs(query, keys, valid):
    scores = back_product(query, keys) * HEAD ** (-0.5)
    if valid is not None:
        scores = jnp.where(valid > 0.5, scores, -1e30)
    raised = jnp.exp(scores - jnp.max(scores, axis=-1, keepdims=True))
    return raised / jnp.sum(raised, axis=-1, keepdims=True)


def attend_backward(query, keys, values, valid, upstream):
    scale = HEAD ** (-0.5)
    probs = attend_probs(query, keys, valid)
    grad_values = outer_sum(low(probs), upstream)
    grad_probs = back_product(upstream, values)
    inner = jnp.sum(grad_probs * probs, axis=-1, keepdims=True)
    grad_scores = low(probs * (grad_probs - inner))
    grad_query = product(grad_scores, keys) * scale
    grad_keys = outer_sum(grad_scores, query) * scale
    return low(grad_query), low(grad_keys), low(grad_values)


class Net:
    def __init__(self, send, recv, local, free):
        dp, tensor = lax.axis_index("dp"), lax.axis_index("tensor")
        self.x, self.y, self.z = dp // 8, (dp // 2) % 4, dp % 2
        self.tensor, self.core = tensor, tensor % 2
        self.send, self.recv, self.local, self.free = send, recv, local, free
        self.sent, self.loads, self.stores = 0, 0, []

    def device(self, kind, step=1):
        x, y, z, tensor = self.x, self.y, self.z, self.tensor
        if kind == "x":
            x = (x + step + 4) % 4
        elif kind == "y":
            y = (y + step + 4) % 4
        elif kind == "zhi":
            z = 1 - z
        elif kind == "zlo":
            tensor = (tensor + 2) % 4
        else:
            tensor = tensor + 1 - 2 * self.core
        return (x * 8 + y * 2 + z, tensor)

    def greet(self, partners):
        barrier = pltpu.get_barrier_semaphore()
        for kind, step in partners:
            pl.semaphore_signal(
                barrier, inc=1, device_id=self.device(kind, step), device_id_type=MESH
            )
        pl.semaphore_wait(barrier, len(partners))

    def release(self, kind):
        pl.semaphore_signal(self.free, inc=1, device_id=self.device(kind), device_id_type=MESH)

    def await_release(self):
        pl.semaphore_wait(self.free, 1)

    def push(self, source, target, kind, step=1):
        copy = pltpu.make_async_remote_copy(
            src_ref=source,
            dst_ref=target,
            send_sem=self.send.at[self.sent],
            recv_sem=self.recv.at[self.sent],
            device_id=self.device(kind, step),
            device_id_type=MESH,
        )
        self.sent += 1
        copy.start()
        return copy

    def load(self, source, target):
        copy = pltpu.make_async_copy(source, target, self.local.at[self.loads])
        self.loads += 1
        copy.start()
        return copy

    def store(self, out):
        self.stores.append(self.load(out.vmem, out.hbm))


class Late:
    def __init__(self, net, hbm, vmem):
        self.net, self.hbm, self.vmem, self.copy, self.here = net, hbm, vmem, None, False

    def start(self):
        self.copy = self.net.load(self.hbm, self.vmem)

    def ref(self):
        if self.copy is None:
            self.start()
        if not self.here:
            self.copy.wait()
            self.here = True
        return self.vmem


class Out:
    def __init__(self, hbm, vmem):
        self.hbm, self.vmem = hbm, vmem


def add_rows(target, *sources):
    rows = target.shape[0]
    step = 16 if target.shape[1] > 1024 else 32

    def body(i, carry):
        at = pl.ds(pl.multiple_of(i * step, step), step)
        value = target[at, :]
        for source in sources:
            value = value + source[at, :]
        target[at, :] = value
        return carry

    lax.fori_loop(0, rows // step, body, 0)


def each_head(rows, other_rows):
    for item in range(2):
        for head in range(4):
            columns = pl.ds(head * HEAD, HEAD)
            yield (
                item,
                (pl.ds(item * rows, rows), columns),
                (pl.ds(item * other_rows, other_rows), columns),
            )


class RingOne:
    SCRATCH = (
        ((2, 2, 128, JOB), F32),
        ((2, 2, 128, JOB), F32),
        ((2, 2, 128, JOB), F32),
    )
    COPIES = 6

    def __init__(self, net, left, right, column, x_first, own, scratch):
        self.net, self.left, self.right, self.own = net, left, right, own
        self.column = column * JOB
        self.x_first = x_first
        self.axis, self.one = ("x", net.x) if x_first else ("y", net.y)
        self.sending, self.got, self.beside = scratch

    def piece(self, step, half, target, add=False):
        at = (self.one + step) % 4
        if self.x_first:
            left = self.left[:, pl.ds(pl.multiple_of(at * 512 + half * 256, 256), 256)]
        else:
            cut = lambda x: self.left[:, pl.ds(pl.multiple_of(x * 512 + at * 128, 128), 128)]
            left = jnp.concatenate([cut(2 * half), cut(2 * half + 1)], axis=1)
        for n in range(JOB // 256):
            value = outer_sum(left, self.right[:, pl.ds(self.column + n * 256, 256)])
            for j in range(2):
                part = value[j * 128 : (j + 1) * 128]
                if add:
                    part = part + target[j, :, pl.ds(n * 256, 256)]
                target[j, :, pl.ds(n * 256, 256)] = part

    def begin(self):
        self.far = []
        for half, step in enumerate((1, -1)):
            self.piece(2, half, self.sending.at[half])
            self.far.append(
                self.net.push(self.sending.at[half], self.got.at[half], self.axis, step)
            )

    def relay(self):
        net, axis = self.net, self.axis
        self.last, self.near = [], []
        for i, (step, at) in enumerate(((1, 1), (-1, 3))):
            self.far[i].wait_recv()
            self.piece(at, i, self.got.at[i], True)
            self.last.append(net.push(self.got.at[i], self.own.at[pl.ds(2 * i, 2)], axis, step))
        for i, (step, at) in enumerate(((1, 1), (-1, 3))):
            self.far[i].wait_send()
            self.piece(at, 1 - i, self.sending.at[i])
            self.near.append(net.push(self.sending.at[i], self.beside.at[1 - i], axis, step))

    def close(self):
        for half in range(2):
            self.near[1 - half].wait_recv()
            self.piece(0, half, self.beside.at[half], True)
        for half in range(2):
            self.last[half].wait_recv()
            for j in range(2):
                add_rows(self.own.at[2 * half + j], self.beside.at[half, j])

    def done(self):
        for copy in self.last + self.near:
            copy.wait_send()


class RingTwo:
    SCRATCH = (((6, 64, JOB), F32), ((64, JOB), F32))
    PARTS = (((4, 64, JOB), F32),)
    COPIES, LOADS = 7, 4

    def __init__(self, net, own, x_first, out, scratch, parts=None):
        self.net, self.own, self.out, self.parts = net, own, out, parts
        self.axis, self.two = ("y", net.y) if x_first else ("x", net.x)
        self.got, self.got_last = scratch

    def part(self, step, half):
        return self.own.at[(self.two + step) % 4, pl.ds(half * 64, 64), :]

    def begin(self):
        net, axis, got = self.net, self.axis, self.got
        self.far = [
            net.push(self.part(2, 0), got.at[0], axis, 1),
            net.push(self.part(2, 1), got.at[1], axis, -1),
        ]
        self.near = [
            net.push(self.part(1, 1), got.at[4], axis, 1),
            net.push(self.part(3, 0), got.at[5], axis, -1),
        ]
        self.read = [self.part(*at) for at in ((1, 0), (3, 1), (0, 0), (0, 1))]
        self.loading = []
        if self.parts is not None:
            self.loading = [net.load(ref, self.parts.at[i]) for i, ref in enumerate(self.read)]
            self.read = [self.parts.at[i] for i in range(4)]

    def relay(self):
        net, axis, got = self.net, self.axis, self.got
        self.last = []
        for copy in self.loading:
            copy.wait()
        for i, step in enumerate((1, -1)):
            self.far[i].wait_recv()
            add_rows(got.at[i], self.read[i])
            self.last.append(net.push(got.at[i], got.at[2 + i], axis, step))

    def third(self):
        net, got = self.net, self.got
        for copy in self.near + self.last:
            copy.wait_recv()
        add_rows(got.at[5], got.at[2], self.read[2])
        add_rows(got.at[4], got.at[3], self.read[3])
        self.final = net.push(got.at[4 + net.z], self.got_last, "zhi")

    def finish(self):
        self.final.wait_recv()
        self.out[...] = self.got[5 - self.net.z] + self.got_last[...]
        for copy in self.far + self.near + self.last + [self.final]:
            copy.wait_send()


class TensorSum:
    SCRATCH = tuple(((256 // CHUNK, CHUNK, 2048), F32) for _ in range(4))
    COPIES, LOADS = 3 * (256 // CHUNK), 256 // CHUNK

    HALF = (((256, 2048), F32),)

    def __init__(self, net, share, epilogue, whole, scratch, half=None):
        self.net, self.share, self.epilogue, self.whole = net, share, epilogue, whole
        self.half = half
        self.mine, self.got_core, self.got_z, self.got_rows = scratch
        self.steps = range(256 // CHUNK)

    def rows(self, core, step):
        return pl.ds(pl.multiple_of(core * 256 + step * CHUNK, CHUNK), CHUNK)

    def free_half(self):
        for copy in self.swaps:
            copy.wait_send()
        self.swaps_sent = True

    def begin(self):
        net = self.net
        self.loading, self.swaps_sent = [], False
        if self.half is not None:
            for n in range(4):
                self.half[:, pl.ds(n * 512, 512)] = self.share(1 - net.core, n)
            self.swaps = [
                net.push(self.half.at[pl.ds(j * CHUNK, CHUNK)], self.got_core.at[j], "core")
                for j in self.steps
            ]
            for n in range(4):
                value = self.share(net.core, n)
                for j in self.steps:
                    rows = value[j * CHUNK : (j + 1) * CHUNK]
                    self.mine[j, :, pl.ds(n * 512, 512)] = rows
            return
        self.swaps = [
            net.push(self.share.at[self.rows(1 - net.core, j)], self.got_core.at[j], "core")
            for j in self.steps
        ]
        self.loading = [
            net.load(self.share.at[self.rows(net.core, j)], self.mine.at[j]) for j in self.steps
        ]

    def exchange(self):
        self.over = []
        for copy in self.loading:
            copy.wait()
        for j in self.steps:
            self.swaps[j].wait_recv()
            add_rows(self.mine.at[j], self.got_core.at[j])
            self.over.append(self.net.push(self.mine.at[j], self.got_z.at[j], "zlo"))

    def work(self):
        net = self.net
        self.spread = []
        for j in self.steps:
            self.over[j].wait_recv()

            def body(i, carry, j=j):
                at = pl.ds(pl.multiple_of(i * 8, 8), 8)
                rows = pl.ds(pl.multiple_of(j * CHUNK + i * 8, 8), 8)
                self.got_core[j, at, :] = self.epilogue(
                    rows, self.mine[j, at, :] + self.got_z[j, at, :]
                )
                return carry

            lax.fori_loop(0, CHUNK // 8, body, 0)
            self.spread.append(net.push(self.got_core.at[j], self.got_rows.at[j], "core"))
            self.round(self.got_core, j, net.core)

    def round(self, source, step, core):
        def body(i, carry):
            at = pl.ds(pl.multiple_of(i * 16, 16), 16)
            rows = pl.ds(pl.multiple_of(core * 256 + step * CHUNK + i * 16, 16), 16)
            self.whole[rows, :] = source[step, at, :].astype(BF16)
            return carry

        lax.fori_loop(0, CHUNK // 16, body, 0)

    def finish(self):
        for j in self.steps:
            self.spread[j].wait_recv()
            self.round(self.got_rows, j, 1 - self.net.core)
        for copy in ([] if self.swaps_sent else self.swaps) + self.over + self.spread:
            copy.wait_send()


NEAR = [("core", 1), ("zlo", 1)]
RING = [("x", 1), ("x", -1), ("y", 1), ("y", -1)]
ALL = [("x", 1), ("x", 2), ("x", 3), ("y", 1), ("y", 2), ("y", 3)]


def vmem(shapes):
    return [pltpu.VMEM(shape, kind) for shape, kind in shapes]


def call(body, ins, outs, scratch, copies, loads, number, name):
    spec = lambda how: pl.BlockSpec(memory_space=pltpu.VMEM if how == "vmem" else pl.ANY)
    late = [(a.shape, a.dtype) for a, how in ins if how == "load"]
    kept = [(o.shape, o.dtype) for o, how in outs if how == "store"]

    def kernel(*refs):
        refs, net = Refs(refs[:-4]), Net(*refs[-4:])
        in_refs, out_refs = refs.some(len(ins)), refs.some(len(outs))
        late_refs, kept_refs = refs.some(len(late)), refs.some(len(kept))
        in_refs = [
            Late(net, ref, late_refs.pop(0)) if how == "load" else ref
            for ref, (_, how) in zip(in_refs, ins)
        ]
        out_refs = [
            Out(ref, kept_refs.pop(0)) if how == "store" else ref
            for ref, (_, how) in zip(out_refs, outs)
        ]
        body(net, Refs(in_refs), Refs(out_refs), refs)
        for copy in net.stores:
            copy.wait()

    return pl.pallas_call(
        kernel,
        name=name,
        out_shape=[o for o, _ in outs],
        in_specs=[spec(how) for _, how in ins],
        out_specs=[spec(how) for _, how in outs],
        scratch_shapes=vmem(late + kept + list(scratch))
        + [
            pltpu.SemaphoreType.DMA((copies,)),
            pltpu.SemaphoreType.DMA((copies,)),
            pltpu.SemaphoreType.DMA((loads + len(late) + len(kept),)),
            pltpu.SemaphoreType.REGULAR,
        ],
        compiler_params=pltpu.CompilerParams(
            collective_id=number, has_side_effects=True, vmem_limit_bytes=60 * 2**20
        ),
    )(*[array for array, _ in ins])


def shape(*dims, kind=F32):
    return jax.ShapeDtypeStruct(dims, kind)


def blocks(count, width, body):
    def step(i, carry):
        body(pl.ds(pl.multiple_of(i * width, width), width))
        return carry

    lax.fori_loop(0, count, step, 0)


class Refs:
    def __init__(self, refs):
        self.refs = list(refs)

    def one(self):
        return self.refs.pop(0)

    def some(self, count):
        return [self.refs.pop(0) for _ in range(count)]


def own_rows(core):
    return pl.ds(pl.multiple_of(core * 256, 256), 256)


def forward_self(normed, weights, rows, gain, text_blocks, text_rows, text_key, text_value):
    ins = [(normed, "load")] + [(weight, "load") for weight in weights]
    ins += [(rows, "load"), (gain, "vmem"), (text_blocks, "hbm")]
    ins += [(text_rows, "load"), (text_key, "load"), (text_value, "load")]
    outs = [(shape(256, 2048), "store"), (shape(512, 2048, kind=BF16), "store")]
    outs += [(shape(4, 4, 32, 256), "vmem")] + [(shape(32, 512, kind=BF16), "vmem")] * 2
    outs += [(shape(512, 512, kind=BF16), "store")] * 4
    scratch = list(TensorSum.SCRATCH + TensorSum.HALF) + [((4, 32, 1024), F32)]

    def body(net, in_refs, out_refs, refs):
        late_normed, late_weights = in_refs.one(), in_refs.some(4)
        late_rows, gain_ref, text_ref, *late_text = in_refs.some(6)
        total, normed, columns_ref, *text_outs = out_refs.some(5)
        attention = out_refs.some(4)
        sum_scratch, half, got = refs.some(4), refs.one(), refs.one()
        every([late_normed] + late_weights, "start")
        net.greet(NEAR + ALL)
        own = net.load(text_ref.at[net.x], got.at[0])
        first = [net.push(text_ref.at[(net.x + k) % 4], got.at[k], "x", k) for k in (1, 2, 3)]
        normed_in = late_normed.ref()
        for late, out in zip(late_weights[:3], attention):
            out.vmem[...] = low(product(normed_in[...], late.ref()[...]))
        query_ref, keys_ref, values_ref, mixed_ref = [out.vmem for out in attention]
        for _, at, to in each_head(256, 256):
            probs = attend_probs(query_ref[at], keys_ref[to], None)
            mixed_ref[at] = low(product(low(probs), values_ref[to]))
        for out in attention:
            net.store(out)
        output_ref = late_weights[3].ref()
        share = lambda core, n: product(
            mixed_ref[own_rows(core), :], output_ref[:, pl.ds(n * 512, 512)]
        )
        rows_ref, total_ref = late_rows.vmem, total.vmem

        def epilogue(at, value):
            value = rows_ref[at, :] + value
            total_ref[at, :] = value
            return layer_norm(value, gain_ref[...])

        work = TensorSum(net, share, epilogue, normed.vmem, sum_scratch, half)
        work.begin()
        late_rows.start()
        every(late_text, "start")
        work.exchange()
        own.wait()
        for copy in first:
            copy.wait_recv()
        cut = lambda y: pl.ds(pl.multiple_of(y * 256, 256), 256)
        kept = net.load(got.at[:, :, cut(net.y)], columns_ref.at[0])
        second = [
            net.push(got.at[:, :, cut((net.y + k) % 4)], columns_ref.at[k], "y", k)
            for k in (1, 2, 3)
        ]
        text_rows_ref = late_text[0].ref()
        for weight, out in zip(late_text[1:], text_outs):
            out[...] = low(product(text_rows_ref[...], weight.ref()[...]))
        late_rows.ref()
        work.work()
        net.store(total)
        work.finish()
        net.store(normed)
        kept.wait()
        for copy in second:
            copy.wait_recv()
        for copy in first + second:
            copy.wait_send()

    copies, loads = TensorSum.COPIES + 6, TensorSum.LOADS + 2
    return call(body, ins, outs, scratch, copies, loads, 0, "forward_self")


def forward_cross(normed, weights, keys, values, present, rows, gain, upstream, contract):
    ins = [(normed, "load")] + [(weight, "load") for weight in weights]
    ins += [(keys, "vmem"), (values, "vmem"), (present, "vmem")]
    ins += [(rows, "load"), (gain, "vmem"), (upstream, "load"), (contract, "load")]
    outs = [(shape(256, 2048), "store"), (shape(512, 2048, kind=BF16), "store")]
    outs += [(shape(512, 2048), "store")] + [(shape(512, 512, kind=BF16), "store")] * 2
    scratch = list(TensorSum.SCRATCH + TensorSum.HALF)

    def body(net, in_refs, out_refs, refs):
        late_normed, late_query, late_output = in_refs.some(3)
        keys_ref, values_ref, present_ref = in_refs.some(3)
        late_rows, gain_ref, late_upstream, late_contract = in_refs.some(4)
        total, normed, grad, query, mixed = out_refs.some(5)
        every([late_normed, late_query, late_output], "start")
        net.greet(NEAR)
        query_ref, mixed_ref = query.vmem, mixed.vmem
        query_ref[...] = low(product(late_normed.ref()[...], late_query.ref()[...]))
        for item, at, to in each_head(256, 16):
            probs = attend_probs(query_ref[at], keys_ref[to], present_ref[pl.ds(item, 1), :])
            mixed_ref[at] = low(product(low(probs), values_ref[to]))
        net.store(query)
        net.store(mixed)
        output_ref = late_output.ref()
        share = lambda core, n: product(
            mixed_ref[own_rows(core), :], output_ref[:, pl.ds(n * 512, 512)]
        )
        rows_ref, total_ref = late_rows.vmem, total.vmem

        def epilogue(at, value):
            value = rows_ref[at, :] + value
            total_ref[at, :] = value
            return layer_norm(value, gain_ref[...])

        work = TensorSum(net, share, epilogue, normed.vmem, refs.some(4), refs.one())
        work.begin()
        every([late_upstream, late_contract, late_rows], "start")
        work.exchange()
        upstream_ref, contract_ref = late_upstream.ref(), late_contract.ref()

        def part(at):
            grad.vmem[:, at] = back_product(upstream_ref[...], contract_ref[at, :])

        blocks(8, 256, part)
        net.store(grad)
        late_rows.ref()
        work.work()
        net.store(total)
        work.finish()
        net.store(normed)

    return call(
        body, ins, outs, scratch, TensorSum.COPIES, TensorSum.LOADS, 1, "forward_cross"
    )


def norm_back_sum(net, share_ref, x_ref, gain_ref, extra_ref, rows_ref, low_ref, gain_sum, scratch):
    gain_sum[...] = jnp.zeros_like(gain_sum)

    def epilogue(at, total):
        row_grad, terms = norm_back(x_ref[at, :], gain_ref[...], total)
        gain_sum[...] += terms
        result = extra_ref[at, :] + row_grad
        rows_ref[at, :] = result
        return result

    return TensorSum(net, share_ref, epilogue, low_ref, scratch)


def every(parts, step):
    for part in parts:
        getattr(part, step)()


def backward_first(share, x_rows, gain, extra, left, right, contract):
    ins = [(share, "hbm"), (x_rows, "load"), (gain, "vmem"), (extra, "load"), (left, "load")]
    ins += [(right, "load"), (contract, "load")]
    outs = [(shape(256, 2048), "store"), (shape(512, 2048, kind=BF16), "store")]
    outs += [(shape(8, 2048), "vmem"), (shape(512, 2048), "store")]
    outs += [(shape(4, 128, JOB), "store")] * 4
    scratch = list(TensorSum.SCRATCH) + list(RingOne.SCRATCH) * 4

    def body(net, in_refs, out_refs, refs):
        share_ref, late_x, gain_ref, late_extra, late_left, late_right = in_refs.some(6)
        late_contract = in_refs.one()
        rows, lows, gain_sum, out_share, *owns = out_refs.some(8)
        sum_scratch = refs.some(4)
        rings = [
            RingOne(net, late_left.vmem, late_right.vmem, i, i % 2 == 0, owns[i].vmem, refs.some(3))
            for i in range(4)
        ]
        every([late_left, late_right], "start")
        net.greet(NEAR + RING)
        x_ref = late_x.vmem
        work = norm_back_sum(
            net, share_ref, x_ref, gain_ref, late_extra.vmem, rows.vmem, lows.vmem, gain_sum, sum_scratch
        )
        work.begin()
        every([late_contract, late_x, late_extra], "start")
        late_left.ref(), late_right.ref()
        every(rings, "begin")
        work.exchange()
        every(rings, "relay")
        right_ref, contract_ref = late_right.ref(), late_contract.ref()

        def part(at):
            out_share.vmem[:, at] = product(right_ref[...], contract_ref[:, at])

        blocks(8, 256, part)
        late_x.ref(), late_extra.ref()
        joins = jnp.where(net.tensor < 2, 1.0, 0.0)

        def join(i, carry):
            at = pl.ds(pl.multiple_of(i * 16, 16), 16)
            to = pl.ds(pl.multiple_of(net.core * 256 + i * 16, 16), 16)
            out_share.vmem[to, :] += x_ref[at, :] * joins
            return carry

        lax.fori_loop(0, 16, join, 0)
        net.store(out_share)
        work.work()
        net.store(rows)
        work.finish()
        net.store(lows)
        for ring, own in zip(rings, owns):
            ring.close()
            net.store(own)
        every(rings, "done")

    copies, loads = TensorSum.COPIES + 4 * RingOne.COPIES, TensorSum.LOADS
    return call(body, ins, outs, scratch, copies, loads, 2, "backward_first")


def backward_second(share, x_rows, gain, extra, owns, wide, narrow, text, out_share):
    pairs = [wide] + narrow
    ones = [(0, i, i % 2 == 0) for i in range(4)]
    ones += [(1 + i, 0, i % 2 == 0) for i in range(len(narrow))]
    ins = [(share, "hbm"), (x_rows, "load"), (gain, "vmem"), (extra, "load"), (text, "hbm")]
    ins += [(out_share, "hbm")] + [(own, "hbm") for own in owns]
    ins += [(array, "load") for pair in pairs for array in pair]
    outs = [(shape(256, 2048), "store"), (shape(512, 2048, kind=BF16), "store")]
    outs += [(shape(8, 2048), "vmem"), (shape(4, 4, 32, 1024), "vmem")]
    outs += [(shape(512, 2048, kind=BF16), "hbm")]
    outs += [(shape(64, JOB), "vmem")] * len(owns)
    outs += [(shape(4, 128, JOB), "store")] * len(ones)
    scratch = list(TensorSum.SCRATCH) + [TensorSum.SCRATCH[0]]
    scratch += list(RingTwo.SCRATCH + RingTwo.PARTS) * len(owns)
    scratch += list(RingOne.SCRATCH) * len(ones)

    def body(net, in_refs, out_refs, refs):
        share_ref, late_x, gain_ref, late_extra, text_ref, out_share_ref = in_refs.some(6)
        own_refs, late_pairs = in_refs.some(len(owns)), [in_refs.some(2) for _ in pairs]
        rows, lows, gain_sum, all_ref, layer_out = out_refs.some(5)
        final_refs, nexts = out_refs.some(len(owns)), out_refs.some(len(ones))
        mine, got_core, got_z, got_rows = refs.some(4)
        got_z_two = refs.one()
        twos = [
            RingTwo(net, own, i % 2 == 0, final_refs[i], refs.some(2), refs.one())
            for i, own in enumerate(own_refs)
        ]
        rings = [
            RingOne(
                net, *[late.vmem for late in late_pairs[p]], c, x_first, nexts[i].vmem, refs.some(3)
            )
            for i, (p, c, x_first) in enumerate(ones)
        ]
        for pair in late_pairs:
            every(pair, "start")
        net.greet(NEAR + ALL + [("zhi", 1)])
        work = norm_back_sum(
            net,
            share_ref,
            late_x.vmem,
            gain_ref,
            late_extra.vmem,
            rows.vmem,
            lows.vmem,
            gain_sum,
            (mine, got_core, got_z, got_rows),
        )
        layer = TensorSum(
            net,
            out_share_ref,
            lambda at, total: total,
            lows.vmem,
            (mine, got_core, got_z_two, got_rows),
        )
        work.begin()
        kept = net.load(text_ref, all_ref.at[0, 0])
        by_x = [net.push(text_ref, all_ref.at[0, k], "x", k) for k in (1, 2, 3)]
        every([late_x, late_extra], "start")
        for pair in late_pairs:
            every(pair, "ref")
        every(twos, "begin")
        every(rings, "begin")
        work.exchange()
        every(twos, "relay")
        every(rings, "relay")
        kept.wait()
        for copy in by_x:
            copy.wait_recv()
        by_y = [net.push(all_ref.at[0], all_ref.at[k], "y", k) for k in (1, 2, 3)]
        every([late_x, late_extra], "ref")
        work.work()
        net.store(rows)
        work.finish()
        net.release("core")
        lows_copy = net.load(lows.vmem, lows.hbm)
        net.await_release()
        layer.begin()
        layer.exchange()
        every(twos, "third")
        for ring, own in zip(rings[:2] + rings[4:], nexts[:2] + nexts[4:]):
            ring.close()
            net.store(own)
        every(twos, "finish")
        lows_copy.wait()
        layer.work()
        layer.finish()
        net.stores.append(net.load(lows.vmem, layer_out))
        for ring, own in zip(rings[2:4], nexts[2:4]):
            ring.close()
            net.store(own)
        for copy in by_y:
            copy.wait_recv()
        for copy in by_x + by_y:
            copy.wait_send()
        every(rings, "done")

    copies = 2 * TensorSum.COPIES + 6 + len(owns) * RingTwo.COPIES + len(ones) * RingOne.COPIES
    loads = 2 * TensorSum.LOADS + 2 + len(owns) * RingTwo.LOADS
    return call(body, ins, outs, scratch, copies, loads, 3, "backward_second")


def backward_last(
    attention, weights, upstream, normed, x_rows, gain, extra, keep, owns, text_grad, sums
):
    count = 4
    ins = [(array, "load") for array in attention] + [(weights[3], "hbm")]
    ins += [(weight, "load") for weight in weights[:3]]
    ins += [(upstream, "load"), (normed, "load"), (x_rows, "load"), (gain, "vmem"), (extra, "hbm"), (keep, "vmem")]
    ins += [(text_grad, "hbm"), (sums, "vmem")] + [(own, "hbm") for own in owns]
    outs = [(shape(512, 2048, kind=BF16), "store"), (shape(8, 2048), "vmem")]
    outs += [(shape(128, 1024), "vmem")] + [(shape(64, JOB), "vmem")] * (len(owns) + count)
    scratch = list(TensorSum.SCRATCH + TensorSum.HALF) + [((512, 512), BF16)] * 4
    scratch += [((16, 2048), F32), ((128, 1024), F32), ((9, 8, 2048), F32)]
    scratch += list(RingTwo.SCRATCH + RingTwo.PARTS) * len(owns)
    scratch += (list(RingTwo.SCRATCH + RingOne.SCRATCH) + [((4, 128, JOB), F32)]) * count

    def body(net, in_refs, out_refs, refs):
        late_attention, late_output, late_weights = in_refs.some(4), in_refs.one(), in_refs.some(3)
        late_upstream, late_normed = in_refs.some(2)
        late_x, gain_ref, extra_hbm, keep_ref, text_ref, sums_ref = in_refs.some(6)
        own_refs = in_refs.some(len(owns))
        image, small_ref, text_out = out_refs.some(3)
        old_refs, new_refs = out_refs.some(len(owns)), out_refs.some(count)
        sum_scratch, half, grad_mixed, grads = refs.some(4), refs.one(), refs.one(), refs.some(3)
        acc_ref, got_text, got_small = refs.some(3)
        old = [
            RingTwo(net, own, i % 2 == 0, old_refs[i], refs.some(2), refs.one())
            for i, own in enumerate(own_refs)
        ]
        ones, twos = [], []
        for i in range(count):
            two_scratch, one_scratch, own = refs.some(2), refs.some(3), refs.one()
            left = (late_normed if i else late_upstream).vmem
            right = grads[i - 1] if i else late_attention[3].vmem
            ones.append(RingOne(net, left, right, 0, i % 2 == 0, own, one_scratch))
            twos.append(RingTwo(net, own, i % 2 == 0, new_refs[i], two_scratch))
        output_copy = net.load(late_output, image.vmem)
        every([late_upstream, late_attention[3]] + late_attention[:3], "start")
        every(late_weights + [late_normed], "start")
        net.greet(NEAR + ALL + [("zhi", 1)])
        acc_ref[...] = jnp.zeros_like(acc_ref)
        x_ref, extra_ref = late_x.vmem, half

        def epilogue(at, total):
            row_grad, terms = norm_back(x_ref[at, :], gain_ref[...], total)
            result = extra_ref[at, :] + row_grad
            kept = keep_ref[at, :] > 0.5
            acc_ref[0:8, :] += terms
            acc_ref[8:16, :] += jnp.where(kept, 0.0, result)
            return jnp.where(kept, result, 0.0)

        every(old, "begin")
        every([late_upstream, late_attention[3]], "ref")
        ones[0].begin()
        output_copy.wait()
        grad_mixed[...] = low(back_product(late_upstream.vmem[...], image.vmem[...]))
        late_x.start()
        text_rows = lambda z: pl.ds(pl.multiple_of(z * 128, 128), 128)
        text_copy = net.load(text_ref.at[text_rows(net.z)], text_out)
        query_ref, keys_ref, values_ref = [late.ref() for late in late_attention[:3]]
        every(old, "relay")
        for _, at, to in each_head(256, 256):
            found = attend_backward(
                query_ref[at], keys_ref[to], values_ref[to], None, grad_mixed[at]
            )
            for ref, value in zip(grads, found):
                ref[at] = value
        weight_refs = [late.ref() for late in late_weights]

        def share(core, n):
            block, total = pl.ds(n * 512, 512), 0.0
            for ref, weight in zip(grads, weight_refs):
                total = total + back_product(ref[own_rows(core), :], weight[block, :])
            return total

        work = TensorSum(net, share, epilogue, image.vmem, sum_scratch, half)
        work.begin()
        late_normed.ref()
        every(ones[1:], "begin")
        work.exchange()
        work.free_half()
        extra_copy = net.load(extra_hbm, half)
        every(ones, "relay")
        late_x.ref()
        extra_copy.wait()
        work.work()
        got_small[0] = sums_ref[...]
        got_small[0, 0:1, :] = jnp.sum(acc_ref[0:8, :], axis=0, keepdims=True)
        got_small[0, 3:4, :] = jnp.sum(acc_ref[8:16, :], axis=0, keepdims=True)
        by_core = net.push(got_small.at[0], got_small.at[1], "core")
        text_push = net.push(text_ref.at[text_rows(1 - net.z)], got_text, "zhi")
        work.finish()
        net.store(image)
        by_core.wait()
        got_small[0] += got_small[1]
        by_x = [net.push(got_small.at[0], got_small.at[1 + k], "x", k) for k in (1, 2, 3)]
        every(old, "third")
        for one, two in zip(ones, twos):
            one.close()
            two.begin()
        every(old, "finish")
        for copy in by_x:
            copy.wait()
        got_small[0] += got_small[2] + got_small[3] + got_small[4]
        by_y = [net.push(got_small.at[0], got_small.at[4 + k], "y", k) for k in (1, 2, 3)]
        every(twos, "relay")
        for copy in by_y:
            copy.wait()
        got_small[0] += got_small[5] + got_small[6] + got_small[7]
        by_z = net.push(got_small.at[0], got_small.at[8], "zhi")
        every(twos, "third")
        text_copy.wait()
        text_push.wait()
        text_out[...] += got_text[...]
        by_z.wait()
        small_ref[...] = got_small[0] + got_small[8]
        every(twos, "finish")
        every(ones, "done")

    copies = TensorSum.COPIES + 9 + (len(owns) + count) * RingTwo.COPIES + count * RingOne.COPIES
    loads = 3 + len(owns) * RingTwo.LOADS
    return call(body, ins, outs, scratch, copies, loads, 4, "backward_last")


def shards(
    image,
    text,
    masked,
    text_len,
    cotangent,
    self_query,
    self_key,
    self_value,
    self_output,
    text_query,
    text_key,
    text_value,
    text_output,
    expand,
    contract,
    first_gain,
    second_gain,
    third_gain,
    mask_token,
):
    items, length, width = image.shape
    words = text.shape[1]
    count = items * length
    core = lax.axis_index("tensor") % 2
    heads = self_query.shape[1] // HEAD
    split = lambda rows: rows.reshape(items, -1, heads, HEAD)
    flat = lambda value: value.reshape(-1, heads * HEAD)
    gains = [g.reshape(1, width) for g in (first_gain, second_gain, third_gain)]
    own = lambda rows: lax.dynamic_slice_in_dim(rows, core * length, length, axis=0)

    text_rows = text.reshape(items * words, text.shape[2])
    text_blocks = text_rows.astype(F32).reshape(items * words, 4, -1).transpose(1, 0, 2)
    upstream = cotangent.reshape(count, width)

    hidden = masked.reshape(count, 1) == 1
    start = jnp.where(hidden, mask_token[None, :], image.reshape(count, width).astype(F32))
    normed_one = low(layer_norm(start, first_gain))
    weights = (self_query, self_key, self_value, self_output)
    start_own = own(start)
    first, normed_two, text_columns, cross_keys, cross_values, *attention = forward_self(
        normed_one, weights, start_own, gains[1], text_blocks, text_rows, text_key, text_value
    )
    text_columns = low(text_columns.reshape(-1, text_columns.shape[-1]))

    present = (jnp.arange(words)[None, :] < text_len[:, None]).astype(F32)
    second, normed_three, grad_active, cross_query, cross_rows = forward_cross(
        normed_two,
        (text_query, text_output),
        cross_keys,
        cross_values,
        present,
        first,
        gains[2],
        upstream,
        contract,
    )

    raised = product(normed_three, expand)
    gelu, pull = jax.vjp(jax.nn.gelu, raised)
    active = low(gelu)
    grad_raised = low(pull(grad_active)[0])
    grad_second, cross_out_grad, third_sum, out_share, *owns = backward_first(
        back_product(grad_raised, expand),
        second,
        gains[2],
        own(upstream).astype(F32),
        upstream,
        active,
        contract,
    )

    grad_mixed = split(low(back_product(cross_out_grad, text_output)))
    over = jax.vmap(jax.vmap(attend_backward, (1, 1, 1, None, 1), 1), (0, 0, 0, 0, 0))
    grad_q, grad_k, grad_v = over(
        split(cross_query), split(cross_keys), split(cross_values), present[:, None, :], grad_mixed
    )
    grad_cq = flat(grad_q)
    text_kv = jnp.concatenate([flat(grad_k), flat(grad_v)], axis=1).astype(F32)
    grad_first, self_out_grad, second_sum, gathered, layer_out, *rest = backward_second(
        back_product(grad_cq, text_query),
        first,
        gains[1],
        grad_second,
        owns,
        (normed_three, grad_raised),
        [(cross_out_grad, cross_rows), (normed_two, grad_cq)],
        text_kv,
        out_share,
    )
    contract_t, owns = rest[:4], rest[4:]
    gathered = low(gathered.reshape(-1, gathered.shape[-1]))
    text_grads = outer_sum(text_columns, gathered)

    sums = jnp.zeros((8, width), F32)
    sums = sums.at[1].set(jnp.sum(second_sum, axis=0)).at[2].set(jnp.sum(third_sum, axis=0))
    keep = 1.0 - own(masked.reshape(count, 1)).astype(F32)
    image_grad, small, text_grads, *rest = backward_last(
        attention,
        weights,
        self_out_grad,
        normed_one,
        start_own,
        gains[0],
        grad_first,
        keep,
        owns,
        text_grads,
        sums,
    )
    expand_grad, (to, tq, so, sq, sk, sv) = rest[:4], rest[4:]

    share = width // 32
    small = lax.dynamic_slice_in_dim(small, lax.axis_index("dp") * share, share, axis=1)
    cut = text_grads.shape[1] // 2
    joined = lambda parts: jnp.concatenate(parts, axis=1)
    return (
        layer_out.reshape(image.shape),
        image_grad.reshape(image.shape),
        sq,
        sk,
        sv,
        so.T,
        tq,
        text_grads[:, :cut],
        text_grads[:, cut:],
        to.T,
        joined(expand_grad),
        joined(contract_t).T,
        small[0],
        small[1],
        small[2],
        small[3],
    )


def solution(mesh):
    rows, split = P("dp", None, None), P(None, "tensor")
    turned, grads, grads_t = P("tensor", None), P("dp", "tensor"), P("tensor", "dp")
    ins = (rows, rows, P("dp", None), P("dp"), rows, split, split, split, turned)
    ins += (split, split, split, turned, split, turned, P(), P(), P(), P())
    outs = (rows, rows, grads, grads, grads, grads_t, grads, grads, grads, grads_t)
    outs += (grads, grads_t, P("dp"), P("dp"), P("dp"), P("dp"))
    return jax.shard_map(shards, mesh=mesh, in_specs=ins, out_specs=outs, check_vma=False)
```

```python
import functools

import jax
import jax.numpy as jnp
from jax import lax
from jax.experimental import pallas as pl
from jax.experimental.pallas import tpu as pltpu
from jax.sharding import PartitionSpec as P

HEAD = 128
EPS = 1e-05
MESH = pl.DeviceIdType.MESH
F32, BF16 = jnp.float32, jnp.bfloat16
CHUNK = 64
JOB = 512


def product(left, right):
    return jnp.dot(left, right, preferred_element_type=F32)


def outer_sum(left, right):
    return lax.dot_general(left, right, (((0,), (0,)), ((), ())), preferred_element_type=F32)


def back_product(left, right):
    return lax.dot_general(left, right, (((1,), (1,)), ((), ())), preferred_element_type=F32)


def low(value):
    return value.astype(BF16)


def layer_norm(rows, gain):
    mean = jnp.mean(rows, axis=-1, keepdims=True)
    centred = rows - mean
    spread = jnp.mean(centred * centred, axis=-1, keepdims=True)
    return centred * lax.rsqrt(spread + EPS) * gain


def norm_back(rows, gain, grad):
    mean = jnp.mean(rows, axis=-1, keepdims=True)
    centred = rows - mean
    spread = jnp.mean(centred * centred, axis=-1, keepdims=True)
    root = lax.rsqrt(spread + EPS)
    xhat = centred * root
    scaled = grad * gain
    row_grad = root * (
        scaled
        - jnp.mean(scaled, axis=-1, keepdims=True)
        - xhat * jnp.mean(scaled * xhat, axis=-1, keepdims=True)
    )
    return row_grad, grad * xhat


def attend_probs(query, keys, valid):
    scores = back_product(query, keys) * HEAD ** (-0.5)
    if valid is not None:
        scores = jnp.where(valid > 0.5, scores, -1e30)
    raised = jnp.exp(scores - jnp.max(scores, axis=-1, keepdims=True))
    return raised / jnp.sum(raised, axis=-1, keepdims=True)


def attend_backward(query, keys, values, valid, upstream):
    scale = HEAD ** (-0.5)
    probs = attend_probs(query, keys, valid)
    grad_values = outer_sum(low(probs), upstream)
    grad_probs = back_product(upstream, values)
    inner = jnp.sum(grad_probs * probs, axis=-1, keepdims=True)
    grad_scores = low(probs * (grad_probs - inner))
    grad_query = product(grad_scores, keys) * scale
    grad_keys = outer_sum(grad_scores, query) * scale
    return low(grad_query), low(grad_keys), low(grad_values)


class Net:
    def __init__(self, send, recv, local, free):
        dp, tensor = lax.axis_index("dp"), lax.axis_index("tensor")
        self.x, self.y, self.z = dp // 8, (dp // 2) % 4, dp % 2
        self.tensor, self.core = tensor, tensor % 2
        self.send, self.recv, self.local, self.free = send, recv, local, free
        self.sent, self.loads, self.stores = 0, 0, []

    def device(self, kind, step=1):
        x, y, z, tensor = self.x, self.y, self.z, self.tensor
        if kind == "x":
            x = (x + step + 4) % 4
        elif kind == "y":
            y = (y + step + 4) % 4
        elif kind == "zhi":
            z = 1 - z
        elif kind == "zlo":
            tensor = (tensor + 2) % 4
        else:
            tensor = tensor + 1 - 2 * self.core
        return (x * 8 + y * 2 + z, tensor)

    def greet(self, partners):
        barrier = pltpu.get_barrier_semaphore()
        for kind, step in partners:
            pl.semaphore_signal(
                barrier, inc=1, device_id=self.device(kind, step), device_id_type=MESH
            )
        pl.semaphore_wait(barrier, len(partners))

    def release(self, kind):
        pl.semaphore_signal(self.free, inc=1, device_id=self.device(kind), device_id_type=MESH)

    def await_release(self):
        pl.semaphore_wait(self.free, 1)

    def push(self, source, target, kind, step=1):
        copy = pltpu.make_async_remote_copy(
            src_ref=source,
            dst_ref=target,
            send_sem=self.send.at[self.sent],
            recv_sem=self.recv.at[self.sent],
            device_id=self.device(kind, step),
            device_id_type=MESH,
        )
        self.sent += 1
        copy.start()
        return copy

    def load(self, source, target):
        copy = pltpu.make_async_copy(source, target, self.local.at[self.loads])
        self.loads += 1
        copy.start()
        return copy

    def store(self, out):
        self.stores.append(self.load(out.vmem, out.hbm))


class Late:
    def __init__(self, net, hbm, vmem):
        self.net, self.hbm, self.vmem, self.copy, self.here = net, hbm, vmem, None, False

    def start(self):
        self.copy = self.net.load(self.hbm, self.vmem)

    def ref(self):
        if self.copy is None:
            self.start()
        if not self.here:
            self.copy.wait()
            self.here = True
        return self.vmem


class Out:
    def __init__(self, hbm, vmem):
        self.hbm, self.vmem = hbm, vmem


def add_rows(target, *sources):
    rows = target.shape[0]
    step = 16 if target.shape[1] > 1024 else 32

    def body(i, carry):
        at = pl.ds(pl.multiple_of(i * step, step), step)
        value = target[at, :]
        for source in sources:
            value = value + source[at, :]
        target[at, :] = value
        return carry

    lax.fori_loop(0, rows // step, body, 0)


def each_head(rows, other_rows):
    for item in range(2):
        for head in range(4):
            columns = pl.ds(head * HEAD, HEAD)
            yield (
                item,
                (pl.ds(item * rows, rows), columns),
                (pl.ds(item * other_rows, other_rows), columns),
            )


class RingOne:
    SCRATCH = (
        ((2, 2, 128, JOB), F32),
        ((2, 2, 128, JOB), F32),
        ((2, 2, 128, JOB), F32),
    )
    COPIES = 6

    def __init__(self, net, left, right, column, x_first, own, scratch):
        self.net, self.left, self.right, self.own = net, left, right, own
        self.column = column * JOB
        self.x_first = x_first
        self.axis, self.one = ("x", net.x) if x_first else ("y", net.y)
        self.sending, self.got, self.beside = scratch

    def piece(self, step, half, target, add=False):
        at = (self.one + step) % 4
        if self.x_first:
            left = self.left[:, pl.ds(pl.multiple_of(at * 512 + half * 256, 256), 256)]
        else:
            cut = lambda x: self.left[:, pl.ds(pl.multiple_of(x * 512 + at * 128, 128), 128)]
            left = jnp.concatenate([cut(2 * half), cut(2 * half + 1)], axis=1)
        for n in range(JOB // 256):
            value = outer_sum(left, self.right[:, pl.ds(self.column + n * 256, 256)])
            for j in range(2):
                part = value[j * 128 : (j + 1) * 128]
                if add:
                    part = part + target[j, :, pl.ds(n * 256, 256)]
                target[j, :, pl.ds(n * 256, 256)] = part

    def begin(self):
        self.far = []
        for half, step in enumerate((1, -1)):
            self.piece(2, half, self.sending.at[half])
            self.far.append(
                self.net.push(self.sending.at[half], self.got.at[half], self.axis, step)
            )

    def relay(self):
        net, axis = self.net, self.axis
        self.last, self.near = [], []
        for i, (step, at) in enumerate(((1, 1), (-1, 3))):
            self.far[i].wait_recv()
            self.piece(at, i, self.got.at[i], True)
            self.last.append(net.push(self.got.at[i], self.own.at[pl.ds(2 * i, 2)], axis, step))
        for i, (step, at) in enumerate(((1, 1), (-1, 3))):
            self.far[i].wait_send()
            self.piece(at, 1 - i, self.sending.at[i])
            self.near.append(net.push(self.sending.at[i], self.beside.at[1 - i], axis, step))

    def close(self):
        for half in range(2):
            self.near[1 - half].wait_recv()
            self.piece(0, half, self.beside.at[half], True)
        for half in range(2):
            self.last[half].wait_recv()
            for j in range(2):
                add_rows(self.own.at[2 * half + j], self.beside.at[half, j])

    def done(self):
        for copy in self.last + self.near:
            copy.wait_send()


class RingTwo:
    SCRATCH = (((6, 64, JOB), F32), ((64, JOB), F32))
    PARTS = (((4, 64, JOB), F32),)
    COPIES, LOADS = 7, 4

    def __init__(self, net, own, x_first, out, scratch, parts=None):
        self.net, self.own, self.out, self.parts = net, own, out, parts
        self.axis, self.two = ("y", net.y) if x_first else ("x", net.x)
        self.got, self.got_last = scratch

    def part(self, step, half):
        return self.own.at[(self.two + step) % 4, pl.ds(half * 64, 64), :]

    def begin(self):
        net, axis, got = self.net, self.axis, self.got
        self.far = [
            net.push(self.part(2, 0), got.at[0], axis, 1),
            net.push(self.part(2, 1), got.at[1], axis, -1),
        ]
        self.near = [
            net.push(self.part(1, 1), got.at[4], axis, 1),
            net.push(self.part(3, 0), got.at[5], axis, -1),
        ]
        self.read = [self.part(*at) for at in ((1, 0), (3, 1), (0, 0), (0, 1))]
        self.loading = []
        if self.parts is not None:
            self.loading = [net.load(ref, self.parts.at[i]) for i, ref in enumerate(self.read)]
            self.read = [self.parts.at[i] for i in range(4)]

    def relay(self):
        net, axis, got = self.net, self.axis, self.got
        self.last = []
        for copy in self.loading:
            copy.wait()
        for i, step in enumerate((1, -1)):
            self.far[i].wait_recv()
            add_rows(got.at[i], self.read[i])
            self.last.append(net.push(got.at[i], got.at[2 + i], axis, step))

    def third(self):
        net, got = self.net, self.got
        for copy in self.near + self.last:
            copy.wait_recv()
        add_rows(got.at[5], got.at[2], self.read[2])
        add_rows(got.at[4], got.at[3], self.read[3])
        self.final = net.push(got.at[4 + net.z], self.got_last, "zhi")

    def finish(self):
        self.final.wait_recv()
        self.out[...] = self.got[5 - self.net.z] + self.got_last[...]
        for copy in self.far + self.near + self.last + [self.final]:
            copy.wait_send()


class TensorSum:
    SCRATCH = tuple(((256 // CHUNK, CHUNK, 2048), F32) for _ in range(4))
    COPIES, LOADS = 3 * (256 // CHUNK), 256 // CHUNK

    HALF = (((256, 2048), F32),)

    def __init__(self, net, share, epilogue, whole, scratch, half=None):
        self.net, self.share, self.epilogue, self.whole = net, share, epilogue, whole
        self.half = half
        self.mine, self.got_core, self.got_z, self.got_rows = scratch
        self.steps = range(256 // CHUNK)

    def rows(self, core, step):
        return pl.ds(pl.multiple_of(core * 256 + step * CHUNK, CHUNK), CHUNK)

    def free_half(self):
        for copy in self.swaps:
            copy.wait_send()
        self.swaps_sent = True

    def begin(self):
        net = self.net
        self.loading, self.swaps_sent = [], False
        if self.half is not None:
            for n in range(4):
                self.half[:, pl.ds(n * 512, 512)] = self.share(1 - net.core, n)
            self.swaps = [
                net.push(self.half.at[pl.ds(j * CHUNK, CHUNK)], self.got_core.at[j], "core")
                for j in self.steps
            ]
            for n in range(4):
                value = self.share(net.core, n)
                for j in self.steps:
                    rows = value[j * CHUNK : (j + 1) * CHUNK]
                    self.mine[j, :, pl.ds(n * 512, 512)] = rows
            return
        self.swaps = [
            net.push(self.share.at[self.rows(1 - net.core, j)], self.got_core.at[j], "core")
            for j in self.steps
        ]
        self.loading = [
            net.load(self.share.at[self.rows(net.core, j)], self.mine.at[j]) for j in self.steps
        ]

    def exchange(self):
        self.over = []
        for copy in self.loading:
            copy.wait()
        for j in self.steps:
            self.swaps[j].wait_recv()
            add_rows(self.mine.at[j], self.got_core.at[j])
            self.over.append(self.net.push(self.mine.at[j], self.got_z.at[j], "zlo"))

    def work(self):
        net = self.net
        self.spread = []
        for j in self.steps:
            self.over[j].wait_recv()

            def body(i, carry, j=j):
                at = pl.ds(pl.multiple_of(i * 8, 8), 8)
                rows = pl.ds(pl.multiple_of(j * CHUNK + i * 8, 8), 8)
                self.got_core[j, at, :] = self.epilogue(
                    rows, self.mine[j, at, :] + self.got_z[j, at, :]
                )
                return carry

            lax.fori_loop(0, CHUNK // 8, body, 0)
            self.spread.append(net.push(self.got_core.at[j], self.got_rows.at[j], "core"))
            self.round(self.got_core, j, net.core)

    def round(self, source, step, core):
        def body(i, carry):
            at = pl.ds(pl.multiple_of(i * 16, 16), 16)
            rows = pl.ds(pl.multiple_of(core * 256 + step * CHUNK + i * 16, 16), 16)
            self.whole[rows, :] = source[step, at, :].astype(BF16)
            return carry

        lax.fori_loop(0, CHUNK // 16, body, 0)

    def finish(self):
        for j in self.steps:
            self.spread[j].wait_recv()
            self.round(self.got_rows, j, 1 - self.net.core)
        for copy in ([] if self.swaps_sent else self.swaps) + self.over + self.spread:
            copy.wait_send()


NEAR = [("core", 1), ("zlo", 1)]
RING = [("x", 1), ("x", -1), ("y", 1), ("y", -1)]
ALL = [("x", 1), ("x", 2), ("x", 3), ("y", 1), ("y", 2), ("y", 3)]


def vmem(shapes):
    return [pltpu.VMEM(shape, kind) for shape, kind in shapes]


def call(body, ins, outs, scratch, copies, loads, number, name):
    spec = lambda how: pl.BlockSpec(memory_space=pltpu.VMEM if how == "vmem" else pl.ANY)
    late = [(a.shape, a.dtype) for a, how in ins if how == "load"]
    kept = [(o.shape, o.dtype) for o, how in outs if how == "store"]

    def kernel(*refs):
        refs, net = Refs(refs[:-4]), Net(*refs[-4:])
        in_refs, out_refs = refs.some(len(ins)), refs.some(len(outs))
        late_refs, kept_refs = refs.some(len(late)), refs.some(len(kept))
        in_refs = [
            Late(net, ref, late_refs.pop(0)) if how == "load" else ref
            for ref, (_, how) in zip(in_refs, ins)
        ]
        out_refs = [
            Out(ref, kept_refs.pop(0)) if how == "store" else ref
            for ref, (_, how) in zip(out_refs, outs)
        ]
        body(net, Refs(in_refs), Refs(out_refs), refs)
        for copy in net.stores:
            copy.wait()

    return pl.pallas_call(
        kernel,
        name=name,
        out_shape=[o for o, _ in outs],
        in_specs=[spec(how) for _, how in ins],
        out_specs=[spec(how) for _, how in outs],
        scratch_shapes=vmem(late + kept + list(scratch))
        + [
            pltpu.SemaphoreType.DMA((copies,)),
            pltpu.SemaphoreType.DMA((copies,)),
            pltpu.SemaphoreType.DMA((loads + len(late) + len(kept),)),
            pltpu.SemaphoreType.REGULAR,
        ],
        compiler_params=pltpu.CompilerParams(
            collective_id=number, has_side_effects=True, vmem_limit_bytes=60 * 2**20
        ),
    )(*[array for array, _ in ins])


def shape(*dims, kind=F32):
    return jax.ShapeDtypeStruct(dims, kind)


def blocks(count, width, body):
    def step(i, carry):
        body(pl.ds(pl.multiple_of(i * width, width), width))
        return carry

    lax.fori_loop(0, count, step, 0)


class Refs:
    def __init__(self, refs):
        self.refs = list(refs)

    def one(self):
        return self.refs.pop(0)

    def some(self, count):
        return [self.refs.pop(0) for _ in range(count)]


def own_rows(core):
    return pl.ds(pl.multiple_of(core * 256, 256), 256)


def forward_self(normed, weights, rows, gain, text_blocks, text_rows, text_key, text_value):
    ins = [(normed, "load")] + [(weight, "load") for weight in weights]
    ins += [(rows, "load"), (gain, "vmem"), (text_blocks, "hbm")]
    ins += [(text_rows, "load"), (text_key, "load"), (text_value, "load")]
    outs = [(shape(256, 2048), "store"), (shape(512, 2048, kind=BF16), "store")]
    outs += [(shape(4, 4, 32, 256), "vmem")] + [(shape(32, 512, kind=BF16), "vmem")] * 2
    outs += [(shape(512, 512, kind=BF16), "store")] * 4
    scratch = list(TensorSum.SCRATCH + TensorSum.HALF) + [((4, 32, 1024), F32)]

    def body(net, in_refs, out_refs, refs):
        late_normed, late_weights = in_refs.one(), in_refs.some(4)
        late_rows, gain_ref, text_ref, *late_text = in_refs.some(6)
        total, normed, columns_ref, *text_outs = out_refs.some(5)
        attention = out_refs.some(4)
        sum_scratch, half, got = refs.some(4), refs.one(), refs.one()
        every([late_normed] + late_weights, "start")
        net.greet(NEAR + ALL)
        own = net.load(text_ref.at[net.x], got.at[0])
        first = [net.push(text_ref.at[(net.x + k) % 4], got.at[k], "x", k) for k in (1, 2, 3)]
        normed_in = late_normed.ref()
        for late, out in zip(late_weights[:3], attention):
            out.vmem[...] = low(product(normed_in[...], late.ref()[...]))
        query_ref, keys_ref, values_ref, mixed_ref = [out.vmem for out in attention]
        for _, at, to in each_head(256, 256):
            probs = attend_probs(query_ref[at], keys_ref[to], None)
            mixed_ref[at] = low(product(low(probs), values_ref[to]))
        for out in attention:
            net.store(out)
        output_ref = late_weights[3].ref()
        share = lambda core, n: product(
            mixed_ref[own_rows(core), :], output_ref[:, pl.ds(n * 512, 512)]
        )
        rows_ref, total_ref = late_rows.vmem, total.vmem

        def epilogue(at, value):
            value = rows_ref[at, :] + value
            total_ref[at, :] = value
            return layer_norm(value, gain_ref[...])

        work = TensorSum(net, share, epilogue, normed.vmem, sum_scratch, half)
        work.begin()
        late_rows.start()
        every(late_text, "start")
        work.exchange()
        own.wait()
        for copy in first:
            copy.wait_recv()
        cut = lambda y: pl.ds(pl.multiple_of(y * 256, 256), 256)
        kept = net.load(got.at[:, :, cut(net.y)], columns_ref.at[0])
        second = [
            net.push(got.at[:, :, cut((net.y + k) % 4)], columns_ref.at[k], "y", k)
            for k in (1, 2, 3)
        ]
        text_rows_ref = late_text[0].ref()
        for weight, out in zip(late_text[1:], text_outs):
            out[...] = low(product(text_rows_ref[...], weight.ref()[...]))
        late_rows.ref()
        work.work()
        net.store(total)
        work.finish()
        net.store(normed)
        kept.wait()
        for copy in second:
            copy.wait_recv()
        for copy in first + second:
            copy.wait_send()

    copies, loads = TensorSum.COPIES + 6, TensorSum.LOADS + 2
    return call(body, ins, outs, scratch, copies, loads, 0, "forward_self")


def forward_cross(normed, weights, keys, values, present, rows, gain, upstream, contract, expand):
    ins = [(normed, "load")] + [(weight, "load") for weight in weights]
    ins += [(keys, "vmem"), (values, "vmem"), (present, "vmem")]
    ins += [(rows, "load"), (gain, "vmem"), (upstream, "load"), (contract, "load")]
    ins += [(expand, "load")]
    outs = [(shape(256, 2048), "store"), (shape(512, 2048, kind=BF16), "store")]
    outs += [(shape(512, 2048, kind=BF16), "store")] * 2
    outs += [(shape(512, 512, kind=BF16), "store")] * 2
    scratch = list(TensorSum.SCRATCH + TensorSum.HALF) + [((512, 2048), F32)]

    def body(net, in_refs, out_refs, refs):
        late_normed, late_query, late_output = in_refs.some(3)
        keys_ref, values_ref, present_ref = in_refs.some(3)
        late_rows, gain_ref, late_upstream, late_contract, late_expand = in_refs.some(5)
        total, normed, active, grad_raised, query, mixed = out_refs.some(6)
        every([late_normed, late_query, late_output], "start")
        net.greet(NEAR)
        query_ref, mixed_ref = query.vmem, mixed.vmem
        query_ref[...] = low(product(late_normed.ref()[...], late_query.ref()[...]))
        for item, at, to in each_head(256, 16):
            probs = attend_probs(query_ref[at], keys_ref[to], present_ref[pl.ds(item, 1), :])
            mixed_ref[at] = low(product(low(probs), values_ref[to]))
        net.store(query)
        net.store(mixed)
        output_ref = late_output.ref()
        share = lambda core, n: product(
            mixed_ref[own_rows(core), :], output_ref[:, pl.ds(n * 512, 512)]
        )
        rows_ref, total_ref = late_rows.vmem, total.vmem

        def epilogue(at, value):
            value = rows_ref[at, :] + value
            total_ref[at, :] = value
            return layer_norm(value, gain_ref[...])

        work = TensorSum(net, share, epilogue, normed.vmem, refs.some(4), refs.one())
        grad_ref = refs.one()
        work.begin()
        every([late_upstream, late_contract, late_rows, late_expand], "start")
        work.exchange()
        upstream_ref, contract_ref = late_upstream.ref(), late_contract.ref()

        def part(at):
            grad_ref[:, at] = back_product(upstream_ref[...], contract_ref[at, :])

        blocks(8, 256, part)
        late_rows.ref()
        expand_ref = late_expand.ref()

        def hidden(core):
            rows = own_rows(core)

            def part(at):
                raised = product(normed.vmem[rows, :], expand_ref[:, at])
                inner = raised * (0.7978845608028654 + 0.035677408136300125 * raised * raised)
                bend = jnp.tanh(inner)
                active.vmem[rows, at] = low(0.5 * raised * (1.0 + bend))
                slope = 0.7978845608028654 + 0.10703222440890037 * raised * raised
                slope = 0.5 * (1.0 + bend) + 0.5 * raised * (1.0 - bend * bend) * slope
                grad_raised.vmem[rows, at] = low(grad_ref[rows, at] * slope)

            blocks(8, 256, part)

        work.work()
        net.store(total)
        hidden(net.core)
        work.finish()
        net.store(normed)
        hidden(1 - net.core)
        net.store(active)
        net.store(grad_raised)

    return call(
        body, ins, outs, scratch, TensorSum.COPIES, TensorSum.LOADS, 1, "forward_cross"
    )


def norm_back_sum(net, share, x_ref, gain_ref, rows_ref, low_ref, gain_sum, scratch, half):
    gain_sum[...] = jnp.zeros_like(gain_sum)

    def epilogue(at, total):
        row_grad, terms = norm_back(x_ref[at, :], gain_ref[...], total)
        gain_sum[...] += terms
        result = rows_ref[at, :] + row_grad
        rows_ref[at, :] = result
        return result

    return TensorSum(net, share, epilogue, low_ref, scratch, half)


def every(parts, step):
    for part in parts:
        getattr(part, step)()


def backward_first(grad_raised, expand, x_rows, gain, extra, left, right, contract):
    ins = [(grad_raised, "load"), (expand, "load"), (x_rows, "load"), (gain, "vmem")]
    ins += [(extra, "hbm"), (left, "load")]
    ins += [(right, "load"), (contract, "load")]
    outs = [(shape(256, 2048), "hbm"), (shape(512, 2048, kind=BF16), "store")]
    outs += [(shape(8, 2048), "vmem"), (shape(512, 2048), "store")]
    outs += [(shape(4, 128, JOB), "store")] * 4
    scratch = list(TensorSum.SCRATCH + TensorSum.HALF) + list(RingOne.SCRATCH) * 4

    def body(net, in_refs, out_refs, refs):
        late_raised, late_expand, late_x, gain_ref = in_refs.some(4)
        extra_hbm, late_left, late_right = in_refs.some(3)
        late_contract = in_refs.one()
        rows, lows, gain_sum, out_share, *owns = out_refs.some(8)
        sum_scratch, half = refs.some(4), refs.one()
        rings = [
            RingOne(net, late_left.vmem, late_right.vmem, i, i % 2 == 0, owns[i].vmem, refs.some(3))
            for i in range(4)
        ]
        every([late_left, late_right, late_raised, late_expand], "start")
        net.greet(NEAR + RING)
        x_ref, raised_ref, expand_ref = late_x.vmem, late_raised.vmem, late_expand.vmem
        share = lambda core, n: back_product(
            raised_ref[own_rows(core), :], expand_ref[pl.ds(n * 512, 512), :]
        )
        work = norm_back_sum(
            net, share, x_ref, gain_ref, half, lows.vmem, gain_sum, sum_scratch, half
        )
        late_left.ref(), late_right.ref()
        every(rings, "begin")
        late_raised.ref(), late_expand.ref()
        work.begin()
        every([late_contract, late_x], "start")
        work.exchange()
        work.free_half()
        extra_copy = net.load(extra_hbm, half)
        every(rings, "relay")
        right_ref, contract_ref = late_right.ref(), late_contract.ref()

        def part(at):
            out_share.vmem[:, at] = product(right_ref[...], contract_ref[:, at])

        blocks(8, 256, part)
        late_x.ref()
        joins = jnp.where(net.tensor < 2, 1.0, 0.0)

        def join(i, carry):
            at = pl.ds(pl.multiple_of(i * 16, 16), 16)
            to = pl.ds(pl.multiple_of(net.core * 256 + i * 16, 16), 16)
            out_share.vmem[to, :] += x_ref[at, :] * joins
            return carry

        lax.fori_loop(0, 16, join, 0)
        net.store(out_share)
        extra_copy.wait()
        work.work()
        net.stores.append(net.load(half, rows))
        work.finish()
        net.store(lows)
        for ring, own in zip(rings, owns):
            ring.close()
            net.store(own)
        every(rings, "done")

    copies, loads = TensorSum.COPIES + 4 * RingOne.COPIES, 2
    return call(body, ins, outs, scratch, copies, loads, 2, "backward_first")


def backward_second(
    attention, weights, present, x_rows, gain, extra, owns, wide, upstream, mixed, normed, out_share
):
    ones = [(0, i, i % 2 == 0) for i in range(4)] + [(1, 0, True), (2, 0, False)]
    query, keys, values = attention
    ins = [(query, "load"), (keys, "vmem"), (values, "vmem"), (present, "vmem")]
    ins += [(weights[0], "load"), (weights[1], "hbm"), (x_rows, "load"), (gain, "vmem")]
    ins += [(extra, "hbm"), (out_share, "hbm")] + [(own, "hbm") for own in owns]
    ins += [(array, "load") for array in (*wide, upstream, mixed, normed)]
    outs = [(shape(256, 2048), "hbm"), (shape(512, 2048, kind=BF16), "store")]
    outs += [(shape(8, 2048), "vmem")] + [(shape(4, 4, 32, 512), "vmem")] * 2
    outs += [(shape(512, 2048, kind=BF16), "hbm")]
    outs += [(shape(64, JOB), "vmem")] * len(owns)
    outs += [(shape(4, 128, JOB), "store")] * len(ones)
    scratch = list(TensorSum.SCRATCH + TensorSum.HALF) + [TensorSum.SCRATCH[0]]
    scratch += [((512, 512), BF16)]
    scratch += list(RingTwo.SCRATCH + RingTwo.PARTS) * len(owns)
    scratch += list(RingOne.SCRATCH) * len(ones)

    def body(net, in_refs, out_refs, refs):
        late_cross, keys_ref, values_ref, present_ref = in_refs.some(4)
        late_weight, output_hbm, late_x, gain_ref, extra_hbm, out_share_ref = in_refs.some(6)
        own_refs, late_wide, late_narrow = in_refs.some(len(owns)), in_refs.some(2), in_refs.some(3)
        rows, lows, gain_sum, keys_all, values_all, layer_out = out_refs.some(6)
        final_refs, nexts = out_refs.some(len(owns)), out_refs.some(len(ones))
        mine, got_core, got_z, got_rows = refs.some(4)
        half, got_z_two, grad_mixed = refs.some(3)
        grad_cross = late_cross.vmem
        twos = [
            RingTwo(net, own, i % 2 == 0, final_refs[i], refs.some(2), refs.one())
            for i, own in enumerate(own_refs)
        ]
        pairs = [[late.vmem for late in late_wide], [late.vmem for late in late_narrow[:2]]]
        pairs.append([late_narrow[2].vmem, grad_cross])
        rings = [
            RingOne(net, *pairs[p], c, x_first, nexts[i].vmem, refs.some(3))
            for i, (p, c, x_first) in enumerate(ones)
        ]
        every(late_wide + late_narrow[:2], "start")
        output_copy = net.load(output_hbm, lows.vmem)
        every([late_cross, late_weight, late_narrow[2], late_x], "start")
        net.greet(NEAR + ALL + [("zhi", 1)])
        weight_ref = late_weight.vmem
        share = lambda core, n: back_product(
            grad_cross[own_rows(core), :], weight_ref[pl.ds(n * 512, 512), :]
        )
        work = norm_back_sum(
            net,
            share,
            late_x.vmem,
            gain_ref,
            half,
            lows.vmem,
            gain_sum,
            (mine, got_core, got_z, got_rows),
            half,
        )
        layer = TensorSum(
            net,
            out_share_ref,
            lambda at, total: total,
            lows.vmem,
            (mine, got_core, got_z_two, got_rows),
        )
        every(twos, "begin")
        every(late_wide, "ref")
        every(rings[:4], "begin")
        every(late_narrow[:2], "ref")
        output_copy.wait()
        grad_mixed[...] = low(back_product(late_narrow[0].vmem[...], lows.vmem[...]))
        query_ref = late_cross.ref()
        for item, at, to in each_head(256, 16):
            grad_query, grad_keys, grad_values = attend_backward(
                query_ref[at],
                keys_ref[to],
                values_ref[to],
                present_ref[pl.ds(item, 1), :],
                grad_mixed[at],
            )
            grad_cross[at] = grad_query
            keys_all[0, 0, to[0], to[1]] = grad_keys.astype(F32)
            values_all[0, 0, to[0], to[1]] = grad_values.astype(F32)
        late_weight.ref()
        work.begin()
        texts = [
            net.push(ref.at[0, 0], ref.at[0, k], axis, k)
            for ref, axis in ((keys_all, "x"), (values_all, "y"))
            for k in (1, 2, 3)
        ]
        every(rings[4:5], "begin")
        late_narrow[2].ref()
        every(rings[5:], "begin")
        work.exchange()
        work.free_half()
        extra_copy = net.load(extra_hbm, half)
        every(twos, "relay")
        every(rings, "relay")
        for copy in texts:
            copy.wait_recv()
        texts += [
            net.push(ref.at[0], ref.at[k], axis, k)
            for ref, axis in ((keys_all, "y"), (values_all, "x"))
            for k in (1, 2, 3)
        ]
        late_x.ref()
        extra_copy.wait()
        work.work()
        net.stores.append(net.load(half, rows))
        work.finish()
        net.release("core")
        lows_copy = net.load(lows.vmem, lows.hbm)
        net.await_release()
        layer.begin()
        layer.exchange()
        every(twos, "third")
        for ring, own in zip(rings[:2] + rings[4:], nexts[:2] + nexts[4:]):
            ring.close()
            net.store(own)
        every(twos, "finish")
        lows_copy.wait()
        layer.work()
        layer.finish()
        net.stores.append(net.load(lows.vmem, layer_out))
        for ring, own in zip(rings[2:4], nexts[2:4]):
            ring.close()
            net.store(own)
        for copy in texts[6:]:
            copy.wait_recv()
        for copy in texts:
            copy.wait_send()
        every(rings, "done")

    copies = 2 * TensorSum.COPIES + 12 + len(owns) * RingTwo.COPIES + len(ones) * RingOne.COPIES
    loads = TensorSum.LOADS + 5 + len(owns) * RingTwo.LOADS
    return call(body, ins, outs, scratch, copies, loads, 3, "backward_second")


def backward_last(
    attention, weights, upstream, normed, x_rows, gain, extra, keep, owns, text_grad, sums
):
    count = 4
    ins = [(array, "load") for array in attention] + [(weights[3], "hbm")]
    ins += [(weight, "load") for weight in weights[:3]]
    ins += [(upstream, "load"), (normed, "load"), (x_rows, "load"), (gain, "vmem"), (extra, "hbm"), (keep, "vmem")]
    ins += [(text_grad, "hbm"), (sums, "vmem")] + [(own, "hbm") for own in owns]
    outs = [(shape(512, 2048, kind=BF16), "store"), (shape(8, 2048), "vmem")]
    outs += [(shape(128, 1024), "vmem")] + [(shape(64, JOB), "vmem")] * (len(owns) + count)
    scratch = list(TensorSum.SCRATCH + TensorSum.HALF) + [((512, 512), BF16)] * 4
    scratch += [((16, 2048), F32), ((128, 1024), F32), ((9, 8, 2048), F32)]
    scratch += list(RingTwo.SCRATCH + RingTwo.PARTS) * len(owns)
    scratch += (list(RingTwo.SCRATCH + RingOne.SCRATCH) + [((4, 128, JOB), F32)]) * count

    def body(net, in_refs, out_refs, refs):
        late_attention, late_output, late_weights = in_refs.some(4), in_refs.one(), in_refs.some(3)
        late_upstream, late_normed = in_refs.some(2)
        late_x, gain_ref, extra_hbm, keep_ref, text_ref, sums_ref = in_refs.some(6)
        own_refs = in_refs.some(len(owns))
        image, small_ref, text_out = out_refs.some(3)
        old_refs, new_refs = out_refs.some(len(owns)), out_refs.some(count)
        sum_scratch, half, grad_mixed, grads = refs.some(4), refs.one(), refs.one(), refs.some(3)
        acc_ref, got_text, got_small = refs.some(3)
        old = [
            RingTwo(net, own, i % 2 == 0, old_refs[i], refs.some(2), refs.one())
            for i, own in enumerate(own_refs)
        ]
        ones, twos = [], []
        for i in range(count):
            two_scratch, one_scratch, own = refs.some(2), refs.some(3), refs.one()
            left = (late_normed if i else late_upstream).vmem
            right = grads[i - 1] if i else late_attention[3].vmem
            ones.append(RingOne(net, left, right, 0, i % 2 == 0, own, one_scratch))
            twos.append(RingTwo(net, own, i % 2 == 0, new_refs[i], two_scratch))
        output_copy = net.load(late_output, image.vmem)
        every([late_upstream, late_attention[3]] + late_attention[:3], "start")
        every(late_weights + [late_normed], "start")
        net.greet(NEAR + ALL + [("zhi", 1)])
        acc_ref[...] = jnp.zeros_like(acc_ref)
        x_ref, extra_ref = late_x.vmem, half

        def epilogue(at, total):
            row_grad, terms = norm_back(x_ref[at, :], gain_ref[...], total)
            result = extra_ref[at, :] + row_grad
            kept = keep_ref[at, :] > 0.5
            acc_ref[0:8, :] += terms
            acc_ref[8:16, :] += jnp.where(kept, 0.0, result)
            return jnp.where(kept, result, 0.0)

        every(old, "begin")
        every([late_upstream, late_attention[3]], "ref")
        ones[0].begin()
        output_copy.wait()
        grad_mixed[...] = low(back_product(late_upstream.vmem[...], image.vmem[...]))
        late_x.start()
        text_rows = lambda z: pl.ds(pl.multiple_of(z * 128, 128), 128)
        text_copy = net.load(text_ref.at[text_rows(net.z)], text_out)
        query_ref, keys_ref, values_ref = [late.ref() for late in late_attention[:3]]
        every(old, "relay")
        for _, at, to in each_head(256, 256):
            found = attend_backward(
                query_ref[at], keys_ref[to], values_ref[to], None, grad_mixed[at]
            )
            for ref, value in zip(grads, found):
                ref[at] = value
        weight_refs = [late.ref() for late in late_weights]

        def share(core, n):
            block, total = pl.ds(n * 512, 512), 0.0
            for ref, weight in zip(grads, weight_refs):
                total = total + back_product(ref[own_rows(core), :], weight[block, :])
            return total

        work = TensorSum(net, share, epilogue, image.vmem, sum_scratch, half)
        work.begin()
        late_normed.ref()
        every(ones[1:], "begin")
        work.exchange()
        work.free_half()
        extra_copy = net.load(extra_hbm, half)
        every(ones, "relay")
        late_x.ref()
        extra_copy.wait()
        work.work()
        got_small[0] = sums_ref[...]
        got_small[0, 0:1, :] = jnp.sum(acc_ref[0:8, :], axis=0, keepdims=True)
        got_small[0, 3:4, :] = jnp.sum(acc_ref[8:16, :], axis=0, keepdims=True)
        by_core = net.push(got_small.at[0], got_small.at[1], "core")
        text_push = net.push(text_ref.at[text_rows(1 - net.z)], got_text, "zhi")
        work.finish()
        net.store(image)
        by_core.wait()
        got_small[0] += got_small[1]
        by_x = [net.push(got_small.at[0], got_small.at[1 + k], "x", k) for k in (1, 2, 3)]
        every(old, "third")
        for one, two in zip(ones, twos):
            one.close()
            two.begin()
        every(old, "finish")
        for copy in by_x:
            copy.wait()
        got_small[0] += got_small[2] + got_small[3] + got_small[4]
        by_y = [net.push(got_small.at[0], got_small.at[4 + k], "y", k) for k in (1, 2, 3)]
        every(twos, "relay")
        for copy in by_y:
            copy.wait()
        got_small[0] += got_small[5] + got_small[6] + got_small[7]
        by_z = net.push(got_small.at[0], got_small.at[8], "zhi")
        every(twos, "third")
        text_copy.wait()
        text_push.wait()
        text_out[...] += got_text[...]
        by_z.wait()
        small_ref[...] = got_small[0] + got_small[8]
        every(twos, "finish")
        every(ones, "done")

    copies = TensorSum.COPIES + 9 + (len(owns) + count) * RingTwo.COPIES + count * RingOne.COPIES
    loads = 3 + len(owns) * RingTwo.LOADS
    return call(body, ins, outs, scratch, copies, loads, 4, "backward_last")


def shards(
    image,
    text,
    masked,
    text_len,
    cotangent,
    self_query,
    self_key,
    self_value,
    self_output,
    text_query,
    text_key,
    text_value,
    text_output,
    expand,
    contract,
    first_gain,
    second_gain,
    third_gain,
    mask_token,
):
    items, length, width = image.shape
    words = text.shape[1]
    count = items * length
    core = lax.axis_index("tensor") % 2
    gains = [g.reshape(1, width) for g in (first_gain, second_gain, third_gain)]
    own = lambda rows: lax.dynamic_slice_in_dim(rows, core * length, length, axis=0)

    text_rows = text.reshape(items * words, text.shape[2])
    text_blocks = text_rows.astype(F32).reshape(items * words, 4, -1).transpose(1, 0, 2)
    upstream = cotangent.reshape(count, width)

    hidden = masked.reshape(count, 1) == 1
    start = jnp.where(hidden, mask_token[None, :], image.reshape(count, width).astype(F32))
    normed_one = low(layer_norm(start, first_gain))
    weights = (self_query, self_key, self_value, self_output)
    start_own = own(start)
    first, normed_two, text_columns, cross_keys, cross_values, *attention = forward_self(
        normed_one, weights, start_own, gains[1], text_blocks, text_rows, text_key, text_value
    )
    text_columns = low(text_columns.reshape(-1, text_columns.shape[-1]))

    present = (jnp.arange(words)[None, :] < text_len[:, None]).astype(F32)
    second, normed_three, active, grad_raised, cross_query, cross_rows = forward_cross(
        normed_two,
        (text_query, text_output),
        cross_keys,
        cross_values,
        present,
        first,
        gains[2],
        upstream,
        contract,
        expand,
    )
    grad_second, cross_out_grad, third_sum, out_share, *owns = backward_first(
        grad_raised,
        expand,
        second,
        gains[2],
        own(upstream).astype(F32),
        upstream,
        active,
        contract,
    )
    grad_first, self_out_grad, second_sum, text_k, text_v, layer_out, *rest = backward_second(
        (cross_query, cross_keys, cross_values),
        (text_query, text_output),
        present,
        first,
        gains[1],
        grad_second,
        owns,
        (normed_three, grad_raised),
        cross_out_grad,
        cross_rows,
        normed_two,
        out_share,
    )
    contract_t, owns = rest[:4], rest[4:]
    text_v = text_v.transpose(1, 0, 2, 3)
    gathered = low(jnp.concatenate([text_k, text_v], axis=3).reshape(text_columns.shape[0], -1))
    text_grads = outer_sum(text_columns, gathered)

    sums = jnp.zeros((8, width), F32)
    sums = sums.at[1].set(jnp.sum(second_sum, axis=0)).at[2].set(jnp.sum(third_sum, axis=0))
    keep = 1.0 - own(masked.reshape(count, 1)).astype(F32)
    image_grad, small, text_grads, *rest = backward_last(
        attention,
        weights,
        self_out_grad,
        normed_one,
        start_own,
        gains[0],
        grad_first,
        keep,
        owns,
        text_grads,
        sums,
    )
    expand_grad, (to, tq, so, sq, sk, sv) = rest[:4], rest[4:]

    share = width // 32
    small = lax.dynamic_slice_in_dim(small, lax.axis_index("dp") * share, share, axis=1)
    cut = text_grads.shape[1] // 2
    joined = lambda parts: jnp.concatenate(parts, axis=1)
    return (
        layer_out.reshape(image.shape),
        image_grad.reshape(image.shape),
        sq,
        sk,
        sv,
        so.T,
        tq,
        text_grads[:, :cut],
        text_grads[:, cut:],
        to.T,
        joined(expand_grad),
        joined(contract_t).T,
        small[0],
        small[1],
        small[2],
        small[3],
    )


def solution(mesh):
    rows, split = P("dp", None, None), P(None, "tensor")
    turned, grads, grads_t = P("tensor", None), P("dp", "tensor"), P("tensor", "dp")
    ins = (rows, rows, P("dp", None), P("dp"), rows, split, split, split, turned)
    ins += (split, split, split, turned, split, turned, P(), P(), P(), P())
    outs = (rows, rows, grads, grads, grads, grads_t, grads, grads, grads, grads_t)
    outs += (grads, grads_t, P("dp"), P("dp"), P("dp"), P("dp"))
    return jax.shard_map(shards, mesh=mesh, in_specs=ins, out_specs=outs, check_vma=False)
```

```python
import functools

import jax
import jax.numpy as jnp
from jax import lax
from jax.experimental import pallas as pl
from jax.experimental.pallas import tpu as pltpu
from jax.sharding import PartitionSpec as P

HEAD = 128
EPS = 1e-05
MESH = pl.DeviceIdType.MESH
F32, BF16 = jnp.float32, jnp.bfloat16
CHUNK = 64
JOB = 512


def product(left, right):
    return jnp.dot(left, right, preferred_element_type=F32)


def outer_sum(left, right):
    return lax.dot_general(left, right, (((0,), (0,)), ((), ())), preferred_element_type=F32)


def back_product(left, right):
    return lax.dot_general(left, right, (((1,), (1,)), ((), ())), preferred_element_type=F32)


def low(value):
    return value.astype(BF16)


def layer_norm(rows, gain):
    mean = jnp.mean(rows, axis=-1, keepdims=True)
    centred = rows - mean
    spread = jnp.mean(centred * centred, axis=-1, keepdims=True)
    return centred * lax.rsqrt(spread + EPS) * gain


def norm_back(rows, gain, grad):
    mean = jnp.mean(rows, axis=-1, keepdims=True)
    centred = rows - mean
    spread = jnp.mean(centred * centred, axis=-1, keepdims=True)
    root = lax.rsqrt(spread + EPS)
    xhat = centred * root
    scaled = grad * gain
    row_grad = root * (
        scaled
        - jnp.mean(scaled, axis=-1, keepdims=True)
        - xhat * jnp.mean(scaled * xhat, axis=-1, keepdims=True)
    )
    return row_grad, grad * xhat


def attend_probs(query, keys, valid):
    scores = back_product(query, keys) * HEAD ** (-0.5)
    if valid is not None:
        scores = jnp.where(valid > 0.5, scores, -1e30)
    raised = jnp.exp(scores - jnp.max(scores, axis=-1, keepdims=True))
    return raised / jnp.sum(raised, axis=-1, keepdims=True)


def attend_backward(query, keys, values, valid, upstream):
    scale = HEAD ** (-0.5)
    probs = attend_probs(query, keys, valid)
    grad_values = outer_sum(low(probs), upstream)
    grad_probs = back_product(upstream, values)
    inner = jnp.sum(grad_probs * probs, axis=-1, keepdims=True)
    grad_scores = low(probs * (grad_probs - inner))
    grad_query = product(grad_scores, keys) * scale
    grad_keys = outer_sum(grad_scores, query) * scale
    return low(grad_query), low(grad_keys), low(grad_values)


class Net:
    def __init__(self, send, recv, local, free):
        dp, tensor = lax.axis_index("dp"), lax.axis_index("tensor")
        self.x, self.y, self.z = dp // 8, (dp // 2) % 4, dp % 2
        self.tensor, self.core = tensor, tensor % 2
        self.send, self.recv, self.local, self.free = send, recv, local, free
        self.sent, self.loads, self.stores = 0, 0, []

    def device(self, kind, step=1):
        x, y, z, tensor = self.x, self.y, self.z, self.tensor
        if kind == "x":
            x = (x + step + 4) % 4
        elif kind == "y":
            y = (y + step + 4) % 4
        elif kind == "zhi":
            z = 1 - z
        elif kind == "zlo":
            tensor = (tensor + 2) % 4
        else:
            tensor = tensor + 1 - 2 * self.core
        return (x * 8 + y * 2 + z, tensor)

    def greet(self, partners):
        barrier = pltpu.get_barrier_semaphore()
        for kind, step in partners:
            pl.semaphore_signal(
                barrier, inc=1, device_id=self.device(kind, step), device_id_type=MESH
            )
        pl.semaphore_wait(barrier, len(partners))

    def release(self, kind):
        pl.semaphore_signal(self.free, inc=1, device_id=self.device(kind), device_id_type=MESH)

    def await_release(self):
        pl.semaphore_wait(self.free, 1)

    def push(self, source, target, kind, step=1):
        copy = pltpu.make_async_remote_copy(
            src_ref=source,
            dst_ref=target,
            send_sem=self.send.at[self.sent],
            recv_sem=self.recv.at[self.sent],
            device_id=self.device(kind, step),
            device_id_type=MESH,
        )
        self.sent += 1
        copy.start()
        return copy

    def load(self, source, target):
        copy = pltpu.make_async_copy(source, target, self.local.at[self.loads])
        self.loads += 1
        copy.start()
        return copy

    def store(self, out):
        self.stores.append(self.load(out.vmem, out.hbm))


class Late:
    def __init__(self, net, hbm, vmem):
        self.net, self.hbm, self.vmem, self.copy, self.here = net, hbm, vmem, None, False

    def start(self):
        self.copy = self.net.load(self.hbm, self.vmem)

    def ref(self):
        if self.copy is None:
            self.start()
        if not self.here:
            self.copy.wait()
            self.here = True
        return self.vmem


class Out:
    def __init__(self, hbm, vmem):
        self.hbm, self.vmem = hbm, vmem


def add_rows(target, *sources):
    rows = target.shape[0]
    step = 16 if target.shape[1] > 1024 else 32

    def body(i, carry):
        at = pl.ds(pl.multiple_of(i * step, step), step)
        value = target[at, :]
        for source in sources:
            value = value + source[at, :]
        target[at, :] = value
        return carry

    lax.fori_loop(0, rows // step, body, 0)


def each_head(rows, other_rows):
    for item in range(2):
        for head in range(4):
            columns = pl.ds(head * HEAD, HEAD)
            yield (
                item,
                (pl.ds(item * rows, rows), columns),
                (pl.ds(item * other_rows, other_rows), columns),
            )


class RingOne:
    SCRATCH = (
        ((2, 2, 128, JOB), F32),
        ((2, 2, 128, JOB), F32),
        ((2, 2, 128, JOB), F32),
    )
    COPIES = 6

    def __init__(self, net, left, right, column, x_first, own, scratch):
        self.net, self.left, self.right, self.own = net, left, right, own
        self.column = column * JOB
        self.x_first = x_first
        self.axis, self.one = ("x", net.x) if x_first else ("y", net.y)
        self.sending, self.got, self.beside = scratch

    def piece(self, step, half, target, add=False):
        at = (self.one + step) % 4
        if self.x_first:
            left = self.left[:, pl.ds(pl.multiple_of(at * 512 + half * 256, 256), 256)]
        else:
            cut = lambda x: self.left[:, pl.ds(pl.multiple_of(x * 512 + at * 128, 128), 128)]
            left = jnp.concatenate([cut(2 * half), cut(2 * half + 1)], axis=1)
        for n in range(JOB // 256):
            value = outer_sum(left, self.right[:, pl.ds(self.column + n * 256, 256)])
            for j in range(2):
                part = value[j * 128 : (j + 1) * 128]
                if add:
                    part = part + target[j, :, pl.ds(n * 256, 256)]
                target[j, :, pl.ds(n * 256, 256)] = part

    def begin(self):
        self.far = []
        for half, step in enumerate((1, -1)):
            self.piece(2, half, self.sending.at[half])
            self.far.append(
                self.net.push(self.sending.at[half], self.got.at[half], self.axis, step)
            )

    def relay(self):
        net, axis = self.net, self.axis
        self.last, self.near = [], []
        for i, (step, at) in enumerate(((1, 1), (-1, 3))):
            self.far[i].wait_recv()
            self.piece(at, i, self.got.at[i], True)
            self.last.append(net.push(self.got.at[i], self.own.at[pl.ds(2 * i, 2)], axis, step))
        for i, (step, at) in enumerate(((1, 1), (-1, 3))):
            self.far[i].wait_send()
            self.piece(at, 1 - i, self.sending.at[i])
            self.near.append(net.push(self.sending.at[i], self.beside.at[1 - i], axis, step))

    def close(self):
        for half in range(2):
            self.near[1 - half].wait_recv()
            self.piece(0, half, self.beside.at[half], True)
        for half in range(2):
            self.last[half].wait_recv()
            for j in range(2):
                add_rows(self.own.at[2 * half + j], self.beside.at[half, j])

    def done(self):
        for copy in self.last + self.near:
            copy.wait_send()


class RingTwo:
    SCRATCH = (((6, 64, JOB), F32), ((64, JOB), F32))
    PARTS = (((4, 64, JOB), F32),)
    COPIES, LOADS = 7, 4

    def __init__(self, net, own, x_first, out, scratch, parts=None):
        self.net, self.own, self.out, self.parts = net, own, out, parts
        self.axis, self.two = ("y", net.y) if x_first else ("x", net.x)
        self.got, self.got_last = scratch

    def part(self, step, half):
        return self.own.at[(self.two + step) % 4, pl.ds(half * 64, 64), :]

    def begin(self):
        net, axis, got = self.net, self.axis, self.got
        self.far = [
            net.push(self.part(2, 0), got.at[0], axis, 1),
            net.push(self.part(2, 1), got.at[1], axis, -1),
        ]
        self.near = [
            net.push(self.part(1, 1), got.at[4], axis, 1),
            net.push(self.part(3, 0), got.at[5], axis, -1),
        ]
        self.read = [self.part(*at) for at in ((1, 0), (3, 1), (0, 0), (0, 1))]
        self.loading = []
        if self.parts is not None:
            self.loading = [net.load(ref, self.parts.at[i]) for i, ref in enumerate(self.read)]
            self.read = [self.parts.at[i] for i in range(4)]

    def relay(self):
        net, axis, got = self.net, self.axis, self.got
        self.last = []
        for copy in self.loading:
            copy.wait()
        for i, step in enumerate((1, -1)):
            self.far[i].wait_recv()
            add_rows(got.at[i], self.read[i])
            self.last.append(net.push(got.at[i], got.at[2 + i], axis, step))

    def third(self):
        net, got = self.net, self.got
        for copy in self.near + self.last:
            copy.wait_recv()
        add_rows(got.at[5], got.at[2], self.read[2])
        add_rows(got.at[4], got.at[3], self.read[3])
        self.final = net.push(got.at[4 + net.z], self.got_last, "zhi")

    def finish(self):
        self.final.wait_recv()
        self.out[...] = self.got[5 - self.net.z] + self.got_last[...]
        for copy in self.far + self.near + self.last + [self.final]:
            copy.wait_send()


class RingHeads(RingOne):
    WIDTH = 3 * HEAD
    SCRATCH = (((2, 2, 128, WIDTH), F32),) * 3 + (((4, 128, WIDTH), F32),)
    LAST = (((4, 128, WIDTH), F32), ((4, 64, WIDTH), F32))
    COPIES_LAST = 4

    def __init__(self, net, lefts, rights, out, scratch, last):
        self.net, self.lefts, self.rights, self.out = net, lefts, rights, out
        self.axis, self.one = "y", net.y
        self.sending, self.got, self.beside, self.own = scratch
        self.heads, self.got_last = last

    def piece(self, step, half, target, add=False):
        at, total = (self.one + step) % 4, 0.0
        for left, right in zip(self.lefts, self.rights):
            cut = lambda x: left[:, pl.ds(pl.multiple_of(x * 512 + at * 128, 128), 128)]
            both = jnp.concatenate([cut(2 * half), cut(2 * half + 1)], axis=1)
            total = total + outer_sum(both, right[...])
        for j in range(2):
            part = total[j * 128 : (j + 1) * 128]
            if add:
                part = part + target[j]
            target[j] = part

    def swap(self):
        net = self.net
        self.swaps = [
            net.push(self.own.at[(net.x + k) % 4], self.heads.at[k], "x", k) for k in (1, 2, 3)
        ]
        self.heads[0] = self.own[net.x]

    def third(self):
        net = self.net
        for copy in self.swaps:
            copy.wait_recv()
        rows = pl.ds(pl.multiple_of((1 - net.z) * 64, 64), 64)
        self.final = net.push(self.heads.at[:, rows], self.got_last, "zhi")

    def finish(self):
        self.final.wait_recv()
        rows = pl.ds(pl.multiple_of(self.net.z * 64, 64), 64)
        for k in range(4):
            self.out[(self.net.x + 4 - k) % 4] = self.heads[k, rows, :] + self.got_last[k]
        for copy in self.swaps + [self.final]:
            copy.wait_send()


class Gather:
    def __init__(self, net, source, steps, out, got, got_core):
        self.net, self.out, self.got, self.got_core = net, out, got, got_core
        self.slots = range(len(steps))
        self.copies, self.handed = [], []
        for j in range(4):
            at = pl.ds(j * 128, 128)
            self.copies.append(
                [net.push(source.at[at], got.at[i, at], "x", step) for i, step in enumerate(steps)]
            )

    def hand(self, j):
        at = pl.ds(j * 128, 128)
        for i in self.slots:
            self.copies[j][i].wait_recv()
            self.handed.append(
                self.net.push(self.got.at[i, at], self.got_core.at[i, at], "core")
            )

    def keep(self, source, core):
        columns = pl.ds(pl.multiple_of(core * 1024, 1024), 1024)
        for i in self.slots:

            def body(n, carry, i=i):
                at = pl.ds(pl.multiple_of(n * 16, 16), 16)
                self.out[i, at, columns] = source[i, at, :].astype(BF16)
                return carry

            lax.fori_loop(0, 32, body, 0)

    def finish(self):
        self.keep(self.got, self.net.core)
        for copy in self.handed:
            copy.wait_recv()
        self.keep(self.got_core, 1 - self.net.core)
        for copy in [copy for step in self.copies for copy in step] + self.handed:
            copy.wait_send()


class TensorSum:
    SCRATCH = tuple(((256 // CHUNK, CHUNK, 2048), F32) for _ in range(4))
    COPIES, LOADS = 3 * (256 // CHUNK), 256 // CHUNK

    HALF = (((256, 2048), F32),)

    def __init__(self, net, share, epilogue, whole, scratch, half=None):
        self.net, self.share, self.epilogue, self.whole = net, share, epilogue, whole
        self.half = half
        self.mine, self.got_core, self.got_z, self.got_rows = scratch
        self.steps = range(256 // CHUNK)

    def rows(self, core, step):
        return pl.ds(pl.multiple_of(core * 256 + step * CHUNK, CHUNK), CHUNK)

    def free_half(self):
        for copy in self.swaps:
            copy.wait_send()
        self.swaps_sent = True

    def begin(self):
        net = self.net
        self.loading, self.swaps_sent = [], False
        if self.half is not None:
            for n in range(4):
                self.half[:, pl.ds(n * 512, 512)] = self.share(1 - net.core, n)
            self.swaps = [
                net.push(self.half.at[pl.ds(j * CHUNK, CHUNK)], self.got_core.at[j], "core")
                for j in self.steps
            ]
            for n in range(4):
                value = self.share(net.core, n)
                for j in self.steps:
                    rows = value[j * CHUNK : (j + 1) * CHUNK]
                    self.mine[j, :, pl.ds(n * 512, 512)] = rows
            return
        self.swaps = [
            net.push(self.share.at[self.rows(1 - net.core, j)], self.got_core.at[j], "core")
            for j in self.steps
        ]
        self.loading = [
            net.load(self.share.at[self.rows(net.core, j)], self.mine.at[j]) for j in self.steps
        ]

    def exchange(self):
        self.over = []
        for copy in self.loading:
            copy.wait()
        for j in self.steps:
            self.swaps[j].wait_recv()
            add_rows(self.mine.at[j], self.got_core.at[j])
            self.over.append(self.net.push(self.mine.at[j], self.got_z.at[j], "zlo"))

    def work(self, hook=None):
        net = self.net
        self.spread = []
        for j in self.steps:
            if hook is not None:
                hook(j)
            self.over[j].wait_recv()

            def body(i, carry, j=j):
                at = pl.ds(pl.multiple_of(i * 8, 8), 8)
                rows = pl.ds(pl.multiple_of(j * CHUNK + i * 8, 8), 8)
                self.got_core[j, at, :] = self.epilogue(
                    rows, self.mine[j, at, :] + self.got_z[j, at, :]
                )
                return carry

            lax.fori_loop(0, CHUNK // 8, body, 0)
            self.spread.append(net.push(self.got_core.at[j], self.got_rows.at[j], "core"))
            self.round(self.got_core, j, net.core)

    def round(self, source, step, core):
        def body(i, carry):
            at = pl.ds(pl.multiple_of(i * 16, 16), 16)
            rows = pl.ds(pl.multiple_of(core * 256 + step * CHUNK + i * 16, 16), 16)
            self.whole[rows, :] = source[step, at, :].astype(BF16)
            return carry

        lax.fori_loop(0, CHUNK // 16, body, 0)

    def finish(self):
        for j in self.steps:
            self.spread[j].wait_recv()
            self.round(self.got_rows, j, 1 - self.net.core)
        for copy in ([] if self.swaps_sent else self.swaps) + self.over + self.spread:
            copy.wait_send()


NEAR = [("core", 1), ("zlo", 1)]
RING = [("x", 1), ("x", -1), ("y", 1), ("y", -1)]
ALL = [("x", 1), ("x", 2), ("x", 3), ("y", 1), ("y", 2), ("y", 3)]


def vmem(shapes):
    return [pltpu.VMEM(shape, kind) for shape, kind in shapes]


def call(body, ins, outs, scratch, copies, loads, number, name):
    spec = lambda how: pl.BlockSpec(memory_space=pltpu.VMEM if how == "vmem" else pl.ANY)
    late = [(a.shape, a.dtype) for a, how in ins if how == "load"]
    kept = [(o.shape, o.dtype) for o, how in outs if how == "store"]

    def kernel(*refs):
        refs, net = Refs(refs[:-4]), Net(*refs[-4:])
        in_refs, out_refs = refs.some(len(ins)), refs.some(len(outs))
        late_refs, kept_refs = refs.some(len(late)), refs.some(len(kept))
        in_refs = [
            Late(net, ref, late_refs.pop(0)) if how == "load" else ref
            for ref, (_, how) in zip(in_refs, ins)
        ]
        out_refs = [
            Out(ref, kept_refs.pop(0)) if how == "store" else ref
            for ref, (_, how) in zip(out_refs, outs)
        ]
        body(net, Refs(in_refs), Refs(out_refs), refs)
        for copy in net.stores:
            copy.wait()

    return pl.pallas_call(
        kernel,
        name=name,
        out_shape=[o for o, _ in outs],
        in_specs=[spec(how) for _, how in ins],
        out_specs=[spec(how) for _, how in outs],
        scratch_shapes=vmem(late + kept + list(scratch))
        + [
            pltpu.SemaphoreType.DMA((copies,)),
            pltpu.SemaphoreType.DMA((copies,)),
            pltpu.SemaphoreType.DMA((loads + len(late) + len(kept),)),
            pltpu.SemaphoreType.REGULAR,
        ],
        compiler_params=pltpu.CompilerParams(
            collective_id=number, has_side_effects=True, vmem_limit_bytes=60 * 2**20
        ),
    )(*[array for array, _ in ins])


def shape(*dims, kind=F32):
    return jax.ShapeDtypeStruct(dims, kind)


def blocks(count, width, body):
    def step(i, carry):
        body(pl.ds(pl.multiple_of(i * width, width), width))
        return carry

    lax.fori_loop(0, count, step, 0)


class Refs:
    def __init__(self, refs):
        self.refs = list(refs)

    def one(self):
        return self.refs.pop(0)

    def some(self, count):
        return [self.refs.pop(0) for _ in range(count)]


def own_rows(core):
    return pl.ds(pl.multiple_of(core * 256, 256), 256)


def forward_self(
    normed, columns, weights, rows, gain, text_blocks, text_rows, text_key, text_value
):
    ins = [(columns, "hbm"), (normed, "load")] + [(weight, "load") for weight in weights]
    ins += [(rows, "load"), (gain, "vmem"), (text_blocks, "hbm")]
    ins += [(text_rows, "load"), (text_key, "load"), (text_value, "load")]
    outs = [(shape(256, 2048), "store"), (shape(512, 2048, kind=BF16), "store")]
    outs += [(shape(4, 4, 32, 256), "vmem")] + [(shape(32, 512, kind=BF16), "vmem")] * 2
    outs += [(shape(512, 512, kind=BF16), "store")] * 4
    outs += [(shape(2, 512, 2048, kind=BF16), "store")]
    scratch = list(TensorSum.SCRATCH + TensorSum.HALF) + [((4, 32, 1024), F32)]
    scratch += [((2, 512, 1024), F32)] * 2

    def body(net, in_refs, out_refs, refs):
        columns_hbm, late_normed, late_weights = in_refs.one(), in_refs.one(), in_refs.some(4)
        late_rows, gain_ref, text_ref, *late_text = in_refs.some(6)
        total, normed, columns_ref, *text_outs = out_refs.some(5)
        attention, beside = out_refs.some(4), out_refs.one()
        sum_scratch, half, got = refs.some(4), refs.one(), refs.one()
        every([late_normed] + late_weights, "start")
        net.greet(NEAR + ALL)
        own = net.load(text_ref.at[net.x], got.at[0])
        first = [net.push(text_ref.at[(net.x + k) % 4], got.at[k], "x", k) for k in (1, 2, 3)]
        gather = Gather(net, columns_hbm, (1, -1), beside.vmem, refs.one(), refs.one())
        normed_in = late_normed.ref()
        for late, out in zip(late_weights[:3], attention):
            out.vmem[...] = low(product(normed_in[...], late.ref()[...]))
        query_ref, keys_ref, values_ref, mixed_ref = [out.vmem for out in attention]
        for _, at, to in each_head(256, 256):
            probs = attend_probs(query_ref[at], keys_ref[to], None)
            mixed_ref[at] = low(product(low(probs), values_ref[to]))
        for out in attention:
            net.store(out)
        output_ref = late_weights[3].ref()
        share = lambda core, n: product(
            mixed_ref[own_rows(core), :], output_ref[:, pl.ds(n * 512, 512)]
        )
        rows_ref, total_ref = late_rows.vmem, total.vmem

        def epilogue(at, value):
            value = rows_ref[at, :] + value
            total_ref[at, :] = value
            return layer_norm(value, gain_ref[...])

        work = TensorSum(net, share, epilogue, normed.vmem, sum_scratch, half)
        work.begin()
        late_rows.start()
        every(late_text, "start")
        work.exchange()
        own.wait()
        for copy in first:
            copy.wait_recv()
        cut = lambda y: pl.ds(pl.multiple_of(y * 256, 256), 256)
        kept = net.load(got.at[:, :, cut(net.y)], columns_ref.at[0])
        second = [
            net.push(got.at[:, :, cut((net.y + k) % 4)], columns_ref.at[k], "y", k)
            for k in (1, 2, 3)
        ]
        text_rows_ref = late_text[0].ref()
        for weight, out in zip(late_text[1:], text_outs):
            out[...] = low(product(text_rows_ref[...], weight.ref()[...]))
        late_rows.ref()
        work.work(gather.hand)
        net.store(total)
        work.finish()
        net.store(normed)
        gather.finish()
        net.store(beside)
        kept.wait()
        for copy in second:
            copy.wait_recv()
        for copy in first + second:
            copy.wait_send()

    copies, loads = TensorSum.COPIES + 22, TensorSum.LOADS + 2
    return call(body, ins, outs, scratch, copies, loads, 0, "forward_self")


def forward_cross(
    columns, normed, weights, keys, values, present, rows, gain, upstream, contract, expand
):
    ins = [(columns, "hbm"), (normed, "load")] + [(weight, "load") for weight in weights]
    ins += [(keys, "vmem"), (values, "vmem"), (present, "vmem")]
    ins += [(rows, "load"), (gain, "vmem"), (upstream, "load"), (contract, "load")]
    ins += [(expand, "load")]
    outs = [(shape(256, 2048), "store"), (shape(512, 2048, kind=BF16), "store")]
    outs += [(shape(512, 2048, kind=BF16), "store")] * 2
    outs += [(shape(512, 512, kind=BF16), "store")] * 2
    outs += [(shape(1, 512, 2048, kind=BF16), "store")]
    scratch = list(TensorSum.SCRATCH + TensorSum.HALF) + [((512, 2048), F32)]
    scratch += [((1, 512, 1024), F32)] * 2

    def body(net, in_refs, out_refs, refs):
        columns_hbm, late_normed, late_query, late_output = in_refs.some(4)
        keys_ref, values_ref, present_ref = in_refs.some(3)
        late_rows, gain_ref, late_upstream, late_contract, late_expand = in_refs.some(5)
        total, normed, active, grad_raised, query, mixed, beyond = out_refs.some(7)
        every([late_normed, late_query, late_output], "start")
        net.greet(NEAR + [("x", 2)])
        query_ref, mixed_ref = query.vmem, mixed.vmem
        query_ref[...] = low(product(late_normed.ref()[...], late_query.ref()[...]))
        for item, at, to in each_head(256, 16):
            probs = attend_probs(query_ref[at], keys_ref[to], present_ref[pl.ds(item, 1), :])
            mixed_ref[at] = low(product(low(probs), values_ref[to]))
        net.store(query)
        net.store(mixed)
        output_ref = late_output.ref()
        share = lambda core, n: product(
            mixed_ref[own_rows(core), :], output_ref[:, pl.ds(n * 512, 512)]
        )
        rows_ref, total_ref = late_rows.vmem, total.vmem

        def epilogue(at, value):
            value = rows_ref[at, :] + value
            total_ref[at, :] = value
            return layer_norm(value, gain_ref[...])

        work = TensorSum(net, share, epilogue, normed.vmem, refs.some(4), refs.one())
        grad_ref = refs.one()
        gather = Gather(net, columns_hbm, (2,), beyond.vmem, refs.one(), refs.one())
        work.begin()
        every([late_upstream, late_contract, late_rows, late_expand], "start")
        work.exchange()
        upstream_ref, contract_ref = late_upstream.ref(), late_contract.ref()

        def part(at):
            grad_ref[:, at] = back_product(upstream_ref[...], contract_ref[at, :])

        blocks(8, 256, part)
        late_rows.ref()
        expand_ref = late_expand.ref()

        def hidden(core):
            rows = own_rows(core)

            def part(at):
                raised = product(normed.vmem[rows, :], expand_ref[:, at])
                inner = raised * (0.7978845608028654 + 0.035677408136300125 * raised * raised)
                bend = jnp.tanh(inner)
                active.vmem[rows, at] = low(0.5 * raised * (1.0 + bend))
                slope = 0.7978845608028654 + 0.10703222440890037 * raised * raised
                slope = 0.5 * (1.0 + bend) + 0.5 * raised * (1.0 - bend * bend) * slope
                grad_raised.vmem[rows, at] = low(grad_ref[rows, at] * slope)

            blocks(8, 256, part)

        work.work(gather.hand)
        net.store(total)
        hidden(net.core)
        work.finish()
        net.store(normed)
        hidden(1 - net.core)
        net.store(active)
        gather.finish()
        net.store(beyond)
        net.store(grad_raised)

    return call(
        body, ins, outs, scratch, TensorSum.COPIES + 8, TensorSum.LOADS, 1, "forward_cross"
    )


def norm_back_sum(net, share, x_ref, gain_ref, rows_ref, low_ref, gain_sum, scratch, half):
    gain_sum[...] = jnp.zeros_like(gain_sum)

    def epilogue(at, total):
        row_grad, terms = norm_back(x_ref[at, :], gain_ref[...], total)
        gain_sum[...] += terms
        result = rows_ref[at, :] + row_grad
        rows_ref[at, :] = result
        return result

    return TensorSum(net, share, epilogue, low_ref, scratch, half)


def every(parts, step):
    for part in parts:
        getattr(part, step)()


def backward_first(grad_raised, expand, x_rows, gain, extra, left, right, contract):
    ins = [(grad_raised, "load"), (expand, "load"), (x_rows, "load"), (gain, "vmem")]
    ins += [(extra, "hbm"), (left, "load")]
    ins += [(right, "load"), (contract, "load")]
    outs = [(shape(256, 2048), "hbm"), (shape(512, 2048, kind=BF16), "store")]
    outs += [(shape(8, 2048), "vmem"), (shape(512, 2048), "store")]
    outs += [(shape(4, 128, JOB), "store")] * 4
    scratch = list(TensorSum.SCRATCH + TensorSum.HALF) + list(RingOne.SCRATCH) * 4

    def body(net, in_refs, out_refs, refs):
        late_raised, late_expand, late_x, gain_ref = in_refs.some(4)
        extra_hbm, late_left, late_right = in_refs.some(3)
        late_contract = in_refs.one()
        rows, lows, gain_sum, out_share, *owns = out_refs.some(8)
        sum_scratch, half = refs.some(4), refs.one()
        rings = [
            RingOne(net, late_left.vmem, late_right.vmem, i, i % 2 == 0, owns[i].vmem, refs.some(3))
            for i in range(4)
        ]
        every([late_left, late_right, late_raised, late_expand], "start")
        net.greet(NEAR + RING)
        x_ref, raised_ref, expand_ref = late_x.vmem, late_raised.vmem, late_expand.vmem
        share = lambda core, n: back_product(
            raised_ref[own_rows(core), :], expand_ref[pl.ds(n * 512, 512), :]
        )
        work = norm_back_sum(
            net, share, x_ref, gain_ref, half, lows.vmem, gain_sum, sum_scratch, half
        )
        late_left.ref(), late_right.ref()
        every(rings, "begin")
        late_raised.ref(), late_expand.ref()
        work.begin()
        every([late_contract, late_x], "start")
        work.exchange()
        work.free_half()
        extra_copy = net.load(extra_hbm, half)
        every(rings, "relay")
        right_ref, contract_ref = late_right.ref(), late_contract.ref()

        def part(at):
            out_share.vmem[:, at] = product(right_ref[...], contract_ref[:, at])

        blocks(8, 256, part)
        late_x.ref()
        joins = jnp.where(net.tensor < 2, 1.0, 0.0)

        def join(i, carry):
            at = pl.ds(pl.multiple_of(i * 16, 16), 16)
            to = pl.ds(pl.multiple_of(net.core * 256 + i * 16, 16), 16)
            out_share.vmem[to, :] += x_ref[at, :] * joins
            return carry

        lax.fori_loop(0, 16, join, 0)
        net.store(out_share)
        extra_copy.wait()
        work.work()
        net.stores.append(net.load(half, rows))
        work.finish()
        net.store(lows)
        for ring, own in zip(rings, owns):
            ring.close()
            net.store(own)
        every(rings, "done")

    copies, loads = TensorSum.COPIES + 4 * RingOne.COPIES, 2
    return call(body, ins, outs, scratch, copies, loads, 2, "backward_first")


def backward_second(
    attention, weights, present, x_rows, gain, extra, owns, wide, upstream, mixed, normed, out_share
):
    ones = [(0, i, i % 2 == 0) for i in range(4)] + [(1, 0, True), (2, 0, False)]
    query, keys, values = attention
    ins = [(query, "load"), (keys, "vmem"), (values, "vmem"), (present, "vmem")]
    ins += [(weights[0], "load"), (weights[1], "hbm"), (x_rows, "load"), (gain, "vmem")]
    ins += [(extra, "hbm"), (out_share, "hbm")] + [(own, "hbm") for own in owns]
    ins += [(array, "load") for array in (*wide, upstream, mixed, normed)]
    outs = [(shape(256, 2048), "hbm"), (shape(512, 2048, kind=BF16), "store")]
    outs += [(shape(8, 2048), "vmem")] + [(shape(4, 4, 32, 512), "vmem")] * 2
    outs += [(shape(512, 2048, kind=BF16), "hbm")]
    outs += [(shape(64, JOB), "vmem")] * len(owns)
    outs += [(shape(4, 128, JOB), "store")] * len(ones)
    scratch = list(TensorSum.SCRATCH + TensorSum.HALF) + [TensorSum.SCRATCH[0]]
    scratch += [((512, 512), BF16)]
    scratch += list(RingTwo.SCRATCH + RingTwo.PARTS) * len(owns)
    scratch += list(RingOne.SCRATCH) * len(ones)

    def body(net, in_refs, out_refs, refs):
        late_cross, keys_ref, values_ref, present_ref = in_refs.some(4)
        late_weight, output_hbm, late_x, gain_ref, extra_hbm, out_share_ref = in_refs.some(6)
        own_refs, late_wide, late_narrow = in_refs.some(len(owns)), in_refs.some(2), in_refs.some(3)
        rows, lows, gain_sum, keys_all, values_all, layer_out = out_refs.some(6)
        final_refs, nexts = out_refs.some(len(owns)), out_refs.some(len(ones))
        mine, got_core, got_z, got_rows = refs.some(4)
        half, got_z_two, grad_mixed = refs.some(3)
        grad_cross = late_cross.vmem
        twos = [
            RingTwo(net, own, i % 2 == 0, final_refs[i], refs.some(2), refs.one())
            for i, own in enumerate(own_refs)
        ]
        pairs = [[late.vmem for late in late_wide], [late.vmem for late in late_narrow[:2]]]
        pairs.append([late_narrow[2].vmem, grad_cross])
        rings = [
            RingOne(net, *pairs[p], c, x_first, nexts[i].vmem, refs.some(3))
            for i, (p, c, x_first) in enumerate(ones)
        ]
        every(late_wide + late_narrow[:2], "start")
        output_copy = net.load(output_hbm, lows.vmem)
        every([late_cross, late_weight, late_narrow[2], late_x], "start")
        net.greet(NEAR + ALL + [("zhi", 1)])
        weight_ref = late_weight.vmem
        share = lambda core, n: back_product(
            grad_cross[own_rows(core), :], weight_ref[pl.ds(n * 512, 512), :]
        )
        work = norm_back_sum(
            net,
            share,
            late_x.vmem,
            gain_ref,
            half,
            lows.vmem,
            gain_sum,
            (mine, got_core, got_z, got_rows),
            half,
        )
        layer = TensorSum(
            net,
            out_share_ref,
            lambda at, total: total,
            lows.vmem,
            (mine, got_core, got_z_two, got_rows),
        )
        every(twos, "begin")
        every(late_wide, "ref")
        every(rings[:4], "begin")
        every(late_narrow[:2], "ref")
        output_copy.wait()
        grad_mixed[...] = low(back_product(late_narrow[0].vmem[...], lows.vmem[...]))
        query_ref = late_cross.ref()
        for item, at, to in each_head(256, 16):
            grad_query, grad_keys, grad_values = attend_backward(
                query_ref[at],
                keys_ref[to],
                values_ref[to],
                present_ref[pl.ds(item, 1), :],
                grad_mixed[at],
            )
            grad_cross[at] = grad_query
            keys_all[0, 0, to[0], to[1]] = grad_keys.astype(F32)
            values_all[0, 0, to[0], to[1]] = grad_values.astype(F32)
        late_weight.ref()
        work.begin()
        texts = [
            net.push(ref.at[0, 0], ref.at[0, k], axis, k)
            for ref, axis in ((keys_all, "x"), (values_all, "y"))
            for k in (1, 2, 3)
        ]
        every(rings[4:5], "begin")
        late_narrow[2].ref()
        every(rings[5:], "begin")
        work.exchange()
        work.free_half()
        extra_copy = net.load(extra_hbm, half)
        every(twos, "relay")
        every(rings, "relay")
        for copy in texts:
            copy.wait_recv()
        texts += [
            net.push(ref.at[0], ref.at[k], axis, k)
            for ref, axis in ((keys_all, "y"), (values_all, "x"))
            for k in (1, 2, 3)
        ]
        late_x.ref()
        extra_copy.wait()
        work.work()
        net.stores.append(net.load(half, rows))
        work.finish()
        net.release("core")
        lows_copy = net.load(lows.vmem, lows.hbm)
        net.await_release()
        layer.begin()
        layer.exchange()
        every(twos, "third")
        for ring, own in zip(rings[:2] + rings[4:], nexts[:2] + nexts[4:]):
            ring.close()
            net.store(own)
        every(twos, "finish")
        lows_copy.wait()
        layer.work()
        layer.finish()
        net.stores.append(net.load(lows.vmem, layer_out))
        for ring, own in zip(rings[2:4], nexts[2:4]):
            ring.close()
            net.store(own)
        for copy in texts[6:]:
            copy.wait_recv()
        for copy in texts:
            copy.wait_send()
        every(rings, "done")

    copies = 2 * TensorSum.COPIES + 12 + len(owns) * RingTwo.COPIES + len(ones) * RingOne.COPIES
    loads = TensorSum.LOADS + 5 + len(owns) * RingTwo.LOADS
    return call(body, ins, outs, scratch, copies, loads, 3, "backward_second")


def backward_last(
    attention, weights, upstream, normed, beside, beyond, x_rows, gain, extra, keep, owns, text_grad, sums
):
    count = 1
    ins = [(array, "load") for array in attention] + [(weights[3], "hbm")]
    ins += [(weight, "hbm") for weight in weights[:3]]
    ins += [(upstream, "load"), (normed, "load"), (beside, "hbm"), (beyond, "hbm"), (x_rows, "load"), (gain, "vmem"), (extra, "hbm"), (keep, "vmem")]
    ins += [(text_grad, "hbm"), (sums, "vmem")] + [(own, "hbm") for own in owns]
    outs = [(shape(512, 2048, kind=BF16), "store"), (shape(8, 2048), "vmem")]
    outs += [(shape(128, 1024), "vmem")] + [(shape(64, JOB), "vmem")] * (len(owns) + count)
    outs += [(shape(4, 64, RingHeads.WIDTH), "vmem")]
    scratch = list(TensorSum.SCRATCH + TensorSum.HALF) + [((512, 512), BF16)] * 4
    scratch += [((512, 2048), BF16)] * 3 + [((512, RingHeads.WIDTH), BF16)] * 4
    scratch += [((3, 512, RingHeads.WIDTH), F32)] * 2
    scratch += list(RingHeads.SCRATCH + RingHeads.LAST)
    scratch += [((16, 2048), F32), ((128, 1024), F32), ((9, 8, 2048), F32)]
    scratch += list(RingTwo.SCRATCH + RingTwo.PARTS) * len(owns)
    scratch += (list(RingTwo.SCRATCH + RingOne.SCRATCH) + [((4, 128, JOB), F32)]) * count

    def body(net, in_refs, out_refs, refs):
        late_attention, late_output, weights_hbm = in_refs.some(4), in_refs.one(), in_refs.some(3)
        late_upstream, late_normed, beside_hbm, beyond_hbm = in_refs.some(4)
        late_x, gain_ref, extra_hbm, keep_ref, text_ref, sums_ref = in_refs.some(6)
        own_refs = in_refs.some(len(owns))
        image, small_ref, text_out = out_refs.some(3)
        old_refs, new_refs, heads_out = out_refs.some(len(owns)), out_refs.some(count), out_refs.one()
        sum_scratch, half, grad_mixed, grads = refs.some(4), refs.one(), refs.one(), refs.some(3)
        rooms, rights, (leaving, arriving) = refs.some(3), refs.some(4), refs.some(2)
        heads_scratch, heads_last = refs.some(4), refs.some(2)
        acc_ref, got_text, got_small = refs.some(3)
        old = [
            RingTwo(net, own, i % 2 == 0, old_refs[i], refs.some(2), refs.one())
            for i, own in enumerate(own_refs)
        ]
        ones, twos = [], []
        for i in range(count):
            two_scratch, one_scratch, own = refs.some(2), refs.some(3), refs.one()
            left, right = late_upstream.vmem, late_attention[3].vmem
            ones.append(RingOne(net, left, right, 0, False, own, one_scratch))
            twos.append(RingTwo(net, own, False, new_refs[i], two_scratch))
        lefts = [late_normed.vmem] + rooms
        heads = RingHeads(net, lefts, rights, heads_out, heads_scratch, heads_last)
        output_copy = net.load(late_output, image.vmem)
        every([late_upstream, late_attention[3]] + late_attention[:3], "start")
        weight_copies = [
            net.load(weight.at[pl.ds(n * 512, 512)], room.at[:, pl.ds(n * 512, 512)])
            for weight, room in zip(weights_hbm, rooms)
            for n in range(4)
        ]
        late_normed.start()
        net.greet(NEAR + ALL + [("zhi", 1)])
        acc_ref[...] = jnp.zeros_like(acc_ref)
        x_ref, extra_ref = late_x.vmem, half

        def epilogue(at, total):
            row_grad, terms = norm_back(x_ref[at, :], gain_ref[...], total)
            result = extra_ref[at, :] + row_grad
            kept = keep_ref[at, :] > 0.5
            acc_ref[0:8, :] += terms
            acc_ref[8:16, :] += jnp.where(kept, 0.0, result)
            return jnp.where(kept, result, 0.0)

        every(old, "begin")
        every([late_upstream, late_attention[3]], "ref")
        ones[0].begin()
        output_copy.wait()
        grad_mixed[...] = low(back_product(late_upstream.vmem[...], image.vmem[...]))
        late_x.start()
        text_rows = lambda z: pl.ds(pl.multiple_of(z * 128, 128), 128)
        text_copy = net.load(text_ref.at[text_rows(net.z)], text_out)
        query_ref, keys_ref, values_ref = [late.ref() for late in late_attention[:3]]
        every(old, "relay")
        for _, at, to in each_head(256, 256):
            found = attend_backward(
                query_ref[at], keys_ref[to], values_ref[to], None, grad_mixed[at]
            )
            for ref, value in zip(grads, found):
                ref[at] = value
        head = lambda x: pl.ds(pl.multiple_of(x * HEAD, HEAD), HEAD)
        for i, ref in enumerate(grads):
            columns = pl.ds(i * HEAD, HEAD)
            rights[0][:, columns] = ref[:, head(net.x)]
            for k in (1, 2, 3):
                leaving[k - 1, :, columns] = ref[:, head((net.x + k) % 4)].astype(F32)
        spread = [
            net.push(leaving.at[k - 1], arriving.at[k - 1], "x", k) for k in (1, 2, 3)
        ]
        for copy in weight_copies:
            copy.wait()

        def share(core, n):
            block, total = pl.ds(n * 512, 512), 0.0
            for ref, weight in zip(grads, rooms):
                total = total + back_product(ref[own_rows(core), :], weight[:, block])
            return total

        work = TensorSum(net, share, epilogue, image.vmem, sum_scratch, half)
        work.begin()
        others = (beside_hbm.at[0], beyond_hbm.at[0], beside_hbm.at[1])
        left_copies = [net.load(source, room) for source, room in zip(others, rooms)]
        work.exchange()
        work.free_half()
        extra_copy = net.load(extra_hbm, half)
        every(ones, "relay")
        late_normed.ref()
        for copy in left_copies:
            copy.wait()
        for k in range(3):
            spread[k].wait_recv()
            rights[k + 1][...] = low(arriving[k])
        heads.begin()
        late_x.ref()
        extra_copy.wait()
        work.work(lambda j: heads.relay() if j == 3 else None)
        got_small[0] = sums_ref[...]
        got_small[0, 0:1, :] = jnp.sum(acc_ref[0:8, :], axis=0, keepdims=True)
        got_small[0, 3:4, :] = jnp.sum(acc_ref[8:16, :], axis=0, keepdims=True)
        by_core = net.push(got_small.at[0], got_small.at[1], "core")
        text_push = net.push(text_ref.at[text_rows(1 - net.z)], got_text, "zhi")
        work.finish()
        net.store(image)
        by_core.wait()
        got_small[0] += got_small[1]
        by_x = [net.push(got_small.at[0], got_small.at[1 + k], "x", k) for k in (1, 2, 3)]
        every(old, "third")
        for one, two in zip(ones, twos):
            one.close()
            two.begin()
        heads.close()
        heads.swap()
        every(old, "finish")
        for copy in by_x:
            copy.wait()
        got_small[0] += got_small[2] + got_small[3] + got_small[4]
        by_y = [net.push(got_small.at[0], got_small.at[4 + k], "y", k) for k in (1, 2, 3)]
        every(twos, "relay")
        for copy in by_y:
            copy.wait()
        got_small[0] += got_small[5] + got_small[6] + got_small[7]
        by_z = net.push(got_small.at[0], got_small.at[8], "zhi")
        every(twos, "third")
        heads.third()
        text_copy.wait()
        text_push.wait()
        text_out[...] += got_text[...]
        by_z.wait()
        small_ref[...] = got_small[0] + got_small[8]
        every(twos, "finish")
        heads.finish()
        heads.done()
        for copy in spread:
            copy.wait_send()
        every(ones, "done")

    copies = TensorSum.COPIES + 9 + (len(owns) + count) * RingTwo.COPIES + count * RingOne.COPIES
    copies += RingHeads.COPIES + RingHeads.COPIES_LAST + 3
    loads = 18 + len(owns) * RingTwo.LOADS
    return call(body, ins, outs, scratch, copies, loads, 4, "backward_last")


def shards(
    image,
    text,
    masked,
    text_len,
    cotangent,
    self_query,
    self_key,
    self_value,
    self_output,
    text_query,
    text_key,
    text_value,
    text_output,
    expand,
    contract,
    first_gain,
    second_gain,
    third_gain,
    mask_token,
):
    items, length, width = image.shape
    words = text.shape[1]
    count = items * length
    core = lax.axis_index("tensor") % 2
    gains = [g.reshape(1, width) for g in (first_gain, second_gain, third_gain)]
    own = lambda rows: lax.dynamic_slice_in_dim(rows, core * length, length, axis=0)

    text_rows = text.reshape(items * words, text.shape[2])
    text_blocks = text_rows.astype(F32).reshape(items * words, 4, -1).transpose(1, 0, 2)
    upstream = cotangent.reshape(count, width)

    hidden = masked.reshape(count, 1) == 1
    start = jnp.where(hidden, mask_token[None, :], image.reshape(count, width).astype(F32))
    normed_one = low(layer_norm(start, first_gain))
    weights = (self_query, self_key, self_value, self_output)
    start_own = own(start)
    columns = lax.dynamic_slice_in_dim(normed_one, core * (width // 2), width // 2, axis=1)
    columns = columns.astype(F32)
    first, normed_two, text_columns, cross_keys, cross_values, *attention, beside = forward_self(
        normed_one,
        columns,
        weights,
        start_own,
        gains[1],
        text_blocks,
        text_rows,
        text_key,
        text_value,
    )
    text_columns = low(text_columns.reshape(-1, text_columns.shape[-1]))

    present = (jnp.arange(words)[None, :] < text_len[:, None]).astype(F32)
    second, normed_three, active, grad_raised, cross_query, cross_rows, beyond = forward_cross(
        columns,
        normed_two,
        (text_query, text_output),
        cross_keys,
        cross_values,
        present,
        first,
        gains[2],
        upstream,
        contract,
        expand,
    )
    grad_second, cross_out_grad, third_sum, out_share, *owns = backward_first(
        grad_raised,
        expand,
        second,
        gains[2],
        own(upstream).astype(F32),
        upstream,
        active,
        contract,
    )
    grad_first, self_out_grad, second_sum, text_k, text_v, layer_out, *rest = backward_second(
        (cross_query, cross_keys, cross_values),
        (text_query, text_output),
        present,
        first,
        gains[1],
        grad_second,
        owns,
        (normed_three, grad_raised),
        cross_out_grad,
        cross_rows,
        normed_two,
        out_share,
    )
    contract_t, owns = rest[:4], rest[4:]
    text_v = text_v.transpose(1, 0, 2, 3)
    gathered = low(jnp.concatenate([text_k, text_v], axis=3).reshape(text_columns.shape[0], -1))
    text_grads = outer_sum(text_columns, gathered)

    sums = jnp.zeros((8, width), F32)
    sums = sums.at[1].set(jnp.sum(second_sum, axis=0)).at[2].set(jnp.sum(third_sum, axis=0))
    keep = 1.0 - own(masked.reshape(count, 1)).astype(F32)
    image_grad, small, text_grads, *rest = backward_last(
        attention,
        weights,
        self_out_grad,
        normed_one,
        beside,
        beyond,
        start_own,
        gains[0],
        grad_first,
        keep,
        owns,
        text_grads,
        sums,
    )
    expand_grad, (to, tq, so, heads) = rest[:4], rest[4:]
    heads = heads.reshape(4, -1, 3, HEAD).transpose(2, 1, 0, 3)
    sq, sk, sv = heads.reshape(3, heads.shape[1], -1)

    share = width // 32
    small = lax.dynamic_slice_in_dim(small, lax.axis_index("dp") * share, share, axis=1)
    cut = text_grads.shape[1] // 2
    joined = lambda parts: jnp.concatenate(parts, axis=1)
    return (
        layer_out.reshape(image.shape),
        image_grad.reshape(image.shape),
        sq,
        sk,
        sv,
        so.T,
        tq,
        text_grads[:, :cut],
        text_grads[:, cut:],
        to.T,
        joined(expand_grad),
        joined(contract_t).T,
        small[0],
        small[1],
        small[2],
        small[3],
    )


def solution(mesh):
    rows, split = P("dp", None, None), P(None, "tensor")
    turned, grads, grads_t = P("tensor", None), P("dp", "tensor"), P("tensor", "dp")
    ins = (rows, rows, P("dp", None), P("dp"), rows, split, split, split, turned)
    ins += (split, split, split, turned, split, turned, P(), P(), P(), P())
    outs = (rows, rows, grads, grads, grads, grads_t, grads, grads, grads, grads_t)
    outs += (grads, grads_t, P("dp"), P("dp"), P("dp"), P("dp"))
    return jax.shard_map(shards, mesh=mesh, in_specs=ins, out_specs=outs, check_vma=False)
```

```python
import functools

import jax
import jax.numpy as jnp
from jax import lax
from jax.experimental import pallas as pl
from jax.experimental.pallas import tpu as pltpu
from jax.sharding import PartitionSpec as P

HEAD = 128
EPS = 1e-05
MESH = pl.DeviceIdType.MESH
F32, BF16 = jnp.float32, jnp.bfloat16
CHUNK = 64
JOB = 512


def product(left, right):
    return jnp.dot(left, right, preferred_element_type=F32)


def outer_sum(left, right):
    return lax.dot_general(left, right, (((0,), (0,)), ((), ())), preferred_element_type=F32)


def back_product(left, right):
    return lax.dot_general(left, right, (((1,), (1,)), ((), ())), preferred_element_type=F32)


def low(value):
    return value.astype(BF16)


def layer_norm(rows, gain):
    mean = jnp.mean(rows, axis=-1, keepdims=True)
    centred = rows - mean
    spread = jnp.mean(centred * centred, axis=-1, keepdims=True)
    return centred * lax.rsqrt(spread + EPS) * gain


def norm_back(rows, gain, grad):
    mean = jnp.mean(rows, axis=-1, keepdims=True)
    centred = rows - mean
    spread = jnp.mean(centred * centred, axis=-1, keepdims=True)
    root = lax.rsqrt(spread + EPS)
    xhat = centred * root
    scaled = grad * gain
    row_grad = root * (
        scaled
        - jnp.mean(scaled, axis=-1, keepdims=True)
        - xhat * jnp.mean(scaled * xhat, axis=-1, keepdims=True)
    )
    return row_grad, grad * xhat


def attend_probs(query, keys, valid):
    scores = back_product(query, keys) * HEAD ** (-0.5)
    if valid is not None:
        scores = jnp.where(valid > 0.5, scores, -1e30)
    raised = jnp.exp(scores - jnp.max(scores, axis=-1, keepdims=True))
    return raised / jnp.sum(raised, axis=-1, keepdims=True)


def attend_backward(query, keys, values, valid, upstream):
    scale = HEAD ** (-0.5)
    probs = attend_probs(query, keys, valid)
    grad_values = outer_sum(low(probs), upstream)
    grad_probs = back_product(upstream, values)
    inner = jnp.sum(grad_probs * probs, axis=-1, keepdims=True)
    grad_scores = low(probs * (grad_probs - inner))
    grad_query = product(grad_scores, keys) * scale
    grad_keys = outer_sum(grad_scores, query) * scale
    return low(grad_query), low(grad_keys), low(grad_values)


class Net:
    def __init__(self, send, recv, local, free):
        dp, tensor = lax.axis_index("dp"), lax.axis_index("tensor")
        self.x, self.y, self.z = dp // 8, (dp // 2) % 4, dp % 2
        self.tensor, self.core = tensor, tensor % 2
        self.send, self.recv, self.local, self.free = send, recv, local, free
        self.sent, self.loads, self.stores = 0, 0, []

    def device(self, kind, step=1):
        x, y, z, tensor = self.x, self.y, self.z, self.tensor
        if kind == "x":
            x = (x + step + 4) % 4
        elif kind == "y":
            y = (y + step + 4) % 4
        elif kind == "zhi":
            z = 1 - z
        elif kind == "zlo":
            tensor = (tensor + 2) % 4
        else:
            tensor = tensor + 1 - 2 * self.core
        return (x * 8 + y * 2 + z, tensor)

    def greet(self, partners):
        barrier = pltpu.get_barrier_semaphore()
        for kind, step in partners:
            pl.semaphore_signal(
                barrier, inc=1, device_id=self.device(kind, step), device_id_type=MESH
            )
        pl.semaphore_wait(barrier, len(partners))

    def release(self, kind):
        pl.semaphore_signal(self.free, inc=1, device_id=self.device(kind), device_id_type=MESH)

    def await_release(self):
        pl.semaphore_wait(self.free, 1)

    def push(self, source, target, kind, step=1):
        copy = pltpu.make_async_remote_copy(
            src_ref=source,
            dst_ref=target,
            send_sem=self.send.at[self.sent],
            recv_sem=self.recv.at[self.sent],
            device_id=self.device(kind, step),
            device_id_type=MESH,
        )
        self.sent += 1
        copy.start()
        return copy

    def load(self, source, target):
        copy = pltpu.make_async_copy(source, target, self.local.at[self.loads])
        self.loads += 1
        copy.start()
        return copy

    def store(self, out):
        self.stores.append(self.load(out.vmem, out.hbm))


class Late:
    def __init__(self, net, hbm, vmem):
        self.net, self.hbm, self.vmem, self.copy, self.here = net, hbm, vmem, None, False

    def start(self):
        self.copy = self.net.load(self.hbm, self.vmem)

    def ref(self):
        if self.copy is None:
            self.start()
        if not self.here:
            self.copy.wait()
            self.here = True
        return self.vmem


class Out:
    def __init__(self, hbm, vmem):
        self.hbm, self.vmem = hbm, vmem


def add_rows(target, *sources):
    rows = target.shape[0]
    step = 16 if target.shape[1] > 1024 else 32

    def body(i, carry):
        at = pl.ds(pl.multiple_of(i * step, step), step)
        value = target[at, :]
        for source in sources:
            value = value + source[at, :]
        target[at, :] = value
        return carry

    lax.fori_loop(0, rows // step, body, 0)


def each_head(rows, other_rows):
    for item in range(2):
        for head in range(4):
            columns = pl.ds(head * HEAD, HEAD)
            yield (
                item,
                (pl.ds(item * rows, rows), columns),
                (pl.ds(item * other_rows, other_rows), columns),
            )


class RingOne:
    SCRATCH = (
        ((2, 2, 128, JOB), F32),
        ((2, 2, 128, JOB), F32),
        ((2, 2, 128, JOB), F32),
    )
    COPIES = 6

    def __init__(self, net, left, right, column, x_first, own, scratch):
        self.net, self.left, self.right, self.own = net, left, right, own
        self.column = column * JOB
        self.x_first = x_first
        self.axis, self.one = ("x", net.x) if x_first else ("y", net.y)
        self.sending, self.got, self.beside = scratch

    def piece(self, step, half, target, add=False):
        at = (self.one + step) % 4
        if self.x_first:
            left = self.left[:, pl.ds(pl.multiple_of(at * 512 + half * 256, 256), 256)]
        else:
            cut = lambda x: self.left[:, pl.ds(pl.multiple_of(x * 512 + at * 128, 128), 128)]
            left = jnp.concatenate([cut(2 * half), cut(2 * half + 1)], axis=1)
        for n in range(JOB // 256):
            value = outer_sum(left, self.right[:, pl.ds(self.column + n * 256, 256)])
            for j in range(2):
                part = value[j * 128 : (j + 1) * 128]
                if add:
                    part = part + target[j, :, pl.ds(n * 256, 256)]
                target[j, :, pl.ds(n * 256, 256)] = part

    def begin(self):
        self.far = []
        for half, step in enumerate((1, -1)):
            self.piece(2, half, self.sending.at[half])
            self.far.append(
                self.net.push(self.sending.at[half], self.got.at[half], self.axis, step)
            )

    def relay(self):
        net, axis = self.net, self.axis
        self.last, self.near = [], []
        for i, (step, at) in enumerate(((1, 1), (-1, 3))):
            self.far[i].wait_recv()
            self.piece(at, i, self.got.at[i], True)
            self.last.append(net.push(self.got.at[i], self.own.at[pl.ds(2 * i, 2)], axis, step))
        for i, (step, at) in enumerate(((1, 1), (-1, 3))):
            self.far[i].wait_send()
            self.piece(at, 1 - i, self.sending.at[i])
            self.near.append(net.push(self.sending.at[i], self.beside.at[1 - i], axis, step))

    def close(self):
        for half in range(2):
            self.near[1 - half].wait_recv()
            self.piece(0, half, self.beside.at[half], True)
        for half in range(2):
            self.last[half].wait_recv()
            for j in range(2):
                add_rows(self.own.at[2 * half + j], self.beside.at[half, j])

    def done(self):
        for copy in self.last + self.near:
            copy.wait_send()


class RingTwo:
    SCRATCH = (((6, 64, JOB), F32), ((64, JOB), F32))
    PARTS = (((4, 64, JOB), F32),)
    COPIES, LOADS = 7, 4

    def __init__(self, net, own, x_first, out, scratch, parts=None):
        self.net, self.own, self.out, self.parts = net, own, out, parts
        self.axis, self.two = ("y", net.y) if x_first else ("x", net.x)
        self.got, self.got_last = scratch

    def part(self, step, half):
        return self.own.at[(self.two + step) % 4, pl.ds(half * 64, 64), :]

    def begin(self):
        net, axis, got = self.net, self.axis, self.got
        self.far = [
            net.push(self.part(2, 0), got.at[0], axis, 1),
            net.push(self.part(2, 1), got.at[1], axis, -1),
        ]
        self.near = [
            net.push(self.part(1, 1), got.at[4], axis, 1),
            net.push(self.part(3, 0), got.at[5], axis, -1),
        ]
        self.read = [self.part(*at) for at in ((1, 0), (3, 1), (0, 0), (0, 1))]
        self.loading = []
        if self.parts is not None:
            self.loading = [net.load(ref, self.parts.at[i]) for i, ref in enumerate(self.read)]
            self.read = [self.parts.at[i] for i in range(4)]

    def relay(self):
        net, axis, got = self.net, self.axis, self.got
        self.last = []
        for copy in self.loading:
            copy.wait()
        for i, step in enumerate((1, -1)):
            self.far[i].wait_recv()
            add_rows(got.at[i], self.read[i])
            self.last.append(net.push(got.at[i], got.at[2 + i], axis, step))

    def third(self):
        net, got = self.net, self.got
        for copy in self.near + self.last:
            copy.wait_recv()
        add_rows(got.at[5], got.at[2], self.read[2])
        add_rows(got.at[4], got.at[3], self.read[3])
        self.final = net.push(got.at[4 + net.z], self.got_last, "zhi")

    def finish(self):
        self.final.wait_recv()
        self.out[...] = self.got[5 - self.net.z] + self.got_last[...]
        for copy in self.far + self.near + self.last + [self.final]:
            copy.wait_send()


class RingHeads(RingOne):
    WIDTH = 3 * HEAD
    SCRATCH = (((2, 2, 128, WIDTH), F32),) * 3 + (((4, 128, WIDTH), F32),)
    LAST = (((4, 128, WIDTH), F32), ((4, 64, WIDTH), F32))
    COPIES_LAST = 4

    def __init__(self, net, lefts, rights, out, scratch, last):
        self.net, self.lefts, self.rights, self.out = net, lefts, rights, out
        self.axis, self.one = "y", net.y
        self.sending, self.got, self.beside, self.own = scratch
        self.heads, self.got_last = last

    def piece(self, step, half, target, add=False):
        at, total = (self.one + step) % 4, 0.0
        for left, right in zip(self.lefts, self.rights):
            cut = lambda x: left[:, pl.ds(pl.multiple_of(x * 512 + at * 128, 128), 128)]
            both = jnp.concatenate([cut(2 * half), cut(2 * half + 1)], axis=1)
            total = total + outer_sum(both, right[...])
        for j in range(2):
            part = total[j * 128 : (j + 1) * 128]
            if add:
                part = part + target[j]
            target[j] = part

    def swap(self):
        net = self.net
        self.swaps = [
            net.push(self.own.at[(net.x + k) % 4], self.heads.at[k], "x", k) for k in (1, 2, 3)
        ]
        self.heads[0] = self.own[net.x]

    def third(self):
        net = self.net
        for copy in self.swaps:
            copy.wait_recv()
        rows = pl.ds(pl.multiple_of((1 - net.z) * 64, 64), 64)
        self.final = net.push(self.heads.at[:, rows], self.got_last, "zhi")

    def finish(self):
        self.final.wait_recv()
        rows = pl.ds(pl.multiple_of(self.net.z * 64, 64), 64)
        for k in range(4):
            self.out[(self.net.x + 4 - k) % 4] = self.heads[k, rows, :] + self.got_last[k]
        for copy in self.swaps + [self.final]:
            copy.wait_send()


class Gather:
    def __init__(self, net, source, steps, out, got, got_core):
        self.net, self.out, self.got, self.got_core = net, out, got, got_core
        self.slots = range(len(steps))
        self.copies, self.handed = [], []
        for j in range(4):
            at = pl.ds(j * 128, 128)
            self.copies.append(
                [net.push(source.at[at], got.at[i, at], "x", step) for i, step in enumerate(steps)]
            )

    def hand(self, j):
        at = pl.ds(j * 128, 128)
        for i in self.slots:
            self.copies[j][i].wait_recv()
            self.handed.append(
                self.net.push(self.got.at[i, at], self.got_core.at[i, at], "core")
            )

    def keep(self, source, core):
        columns = pl.ds(pl.multiple_of(core * 1024, 1024), 1024)
        for i in self.slots:

            def body(n, carry, i=i):
                at = pl.ds(pl.multiple_of(n * 16, 16), 16)
                self.out[i, at, columns] = source[i, at, :].astype(BF16)
                return carry

            lax.fori_loop(0, 32, body, 0)

    def finish(self):
        self.keep(self.got, self.net.core)
        for copy in self.handed:
            copy.wait_recv()
        self.keep(self.got_core, 1 - self.net.core)
        for copy in [copy for step in self.copies for copy in step] + self.handed:
            copy.wait_send()


class TensorSum:
    SCRATCH = tuple(((256 // CHUNK, CHUNK, 2048), F32) for _ in range(4))
    COPIES, LOADS = 3 * (256 // CHUNK), 256 // CHUNK

    HALF = (((256, 2048), F32),)

    def __init__(self, net, share, epilogue, whole, scratch, half=None):
        self.net, self.share, self.epilogue, self.whole = net, share, epilogue, whole
        self.half = half
        self.mine, self.got_core, self.got_z, self.got_rows = scratch
        self.steps = range(256 // CHUNK)

    def rows(self, core, step):
        return pl.ds(pl.multiple_of(core * 256 + step * CHUNK, CHUNK), CHUNK)

    def free_half(self):
        for copy in self.swaps:
            copy.wait_send()
        self.swaps_sent = True

    def begin(self):
        net = self.net
        self.loading, self.swaps_sent = [], False
        if self.half is not None:
            for n in range(4):
                self.half[:, pl.ds(n * 512, 512)] = self.share(1 - net.core, n)
            self.swaps = [
                net.push(self.half.at[pl.ds(j * CHUNK, CHUNK)], self.got_core.at[j], "core")
                for j in self.steps
            ]
            for n in range(4):
                value = self.share(net.core, n)
                for j in self.steps:
                    rows = value[j * CHUNK : (j + 1) * CHUNK]
                    self.mine[j, :, pl.ds(n * 512, 512)] = rows
            return
        self.swaps = [
            net.push(self.share.at[self.rows(1 - net.core, j)], self.got_core.at[j], "core")
            for j in self.steps
        ]
        self.loading = [
            net.load(self.share.at[self.rows(net.core, j)], self.mine.at[j]) for j in self.steps
        ]

    def exchange(self):
        self.over = []
        for copy in self.loading:
            copy.wait()
        for j in self.steps:
            self.swaps[j].wait_recv()
            add_rows(self.mine.at[j], self.got_core.at[j])
            self.over.append(self.net.push(self.mine.at[j], self.got_z.at[j], "zlo"))

    def work(self, hook=None):
        net = self.net
        self.spread = []
        for j in self.steps:
            if hook is not None:
                hook(j)
            self.over[j].wait_recv()

            def body(i, carry, j=j):
                at = pl.ds(pl.multiple_of(i * 8, 8), 8)
                rows = pl.ds(pl.multiple_of(j * CHUNK + i * 8, 8), 8)
                self.got_core[j, at, :] = self.epilogue(
                    rows, self.mine[j, at, :] + self.got_z[j, at, :]
                )
                return carry

            lax.fori_loop(0, CHUNK // 8, body, 0)
            self.spread.append(net.push(self.got_core.at[j], self.got_rows.at[j], "core"))
            self.round(self.got_core, j, net.core)

    def round(self, source, step, core):
        def body(i, carry):
            at = pl.ds(pl.multiple_of(i * 16, 16), 16)
            rows = pl.ds(pl.multiple_of(core * 256 + step * CHUNK + i * 16, 16), 16)
            self.whole[rows, :] = source[step, at, :].astype(BF16)
            return carry

        lax.fori_loop(0, CHUNK // 16, body, 0)

    def finish(self):
        for j in self.steps:
            self.spread[j].wait_recv()
            self.round(self.got_rows, j, 1 - self.net.core)
        for copy in ([] if self.swaps_sent else self.swaps) + self.over + self.spread:
            copy.wait_send()


NEAR = [("core", 1), ("zlo", 1)]
RING = [("x", 1), ("x", -1), ("y", 1), ("y", -1)]
ALL = [("x", 1), ("x", 2), ("x", 3), ("y", 1), ("y", 2), ("y", 3)]


def vmem(shapes):
    return [pltpu.VMEM(shape, kind) for shape, kind in shapes]


def call(body, ins, outs, scratch, copies, loads, number, name):
    spec = lambda how: pl.BlockSpec(memory_space=pltpu.VMEM if how == "vmem" else pl.ANY)
    late = [(a.shape, a.dtype) for a, how in ins if how == "load"]
    kept = [(o.shape, o.dtype) for o, how in outs if how == "store"]

    def kernel(*refs):
        refs, net = Refs(refs[:-4]), Net(*refs[-4:])
        in_refs, out_refs = refs.some(len(ins)), refs.some(len(outs))
        late_refs, kept_refs = refs.some(len(late)), refs.some(len(kept))
        in_refs = [
            Late(net, ref, late_refs.pop(0)) if how == "load" else ref
            for ref, (_, how) in zip(in_refs, ins)
        ]
        out_refs = [
            Out(ref, kept_refs.pop(0)) if how == "store" else ref
            for ref, (_, how) in zip(out_refs, outs)
        ]
        body(net, Refs(in_refs), Refs(out_refs), refs)
        for copy in net.stores:
            copy.wait()

    return pl.pallas_call(
        kernel,
        name=name,
        out_shape=[o for o, _ in outs],
        in_specs=[spec(how) for _, how in ins],
        out_specs=[spec(how) for _, how in outs],
        scratch_shapes=vmem(late + kept + list(scratch))
        + [
            pltpu.SemaphoreType.DMA((copies,)),
            pltpu.SemaphoreType.DMA((copies,)),
            pltpu.SemaphoreType.DMA((loads + len(late) + len(kept),)),
            pltpu.SemaphoreType.REGULAR,
        ],
        compiler_params=pltpu.CompilerParams(
            collective_id=number, has_side_effects=True, vmem_limit_bytes=60 * 2**20
        ),
    )(*[array for array, _ in ins])


def shape(*dims, kind=F32):
    return jax.ShapeDtypeStruct(dims, kind)


def blocks(count, width, body):
    def step(i, carry):
        body(pl.ds(pl.multiple_of(i * width, width), width))
        return carry

    lax.fori_loop(0, count, step, 0)


class Refs:
    def __init__(self, refs):
        self.refs = list(refs)

    def one(self):
        return self.refs.pop(0)

    def some(self, count):
        return [self.refs.pop(0) for _ in range(count)]


def own_rows(core):
    return pl.ds(pl.multiple_of(core * 256, 256), 256)


def forward_self(
    normed, columns, weights, rows, gain, text_blocks, text_rows, text_key, text_value
):
    ins = [(columns, "hbm"), (normed, "load")] + [(weight, "load") for weight in weights]
    ins += [(rows, "load"), (gain, "vmem"), (text_blocks, "hbm")]
    ins += [(text_rows, "load"), (text_key, "load"), (text_value, "load")]
    outs = [(shape(256, 2048), "store"), (shape(512, 2048, kind=BF16), "store")]
    outs += [(shape(4, 4, 32, 256), "vmem")] + [(shape(32, 512, kind=BF16), "vmem")] * 2
    outs += [(shape(512, 512, kind=BF16), "store")] * 4
    outs += [(shape(2, 512, 2048, kind=BF16), "store")]
    scratch = list(TensorSum.SCRATCH + TensorSum.HALF) + [((4, 32, 1024), F32)]
    scratch += [((2, 512, 1024), F32)] * 2

    def body(net, in_refs, out_refs, refs):
        columns_hbm, late_normed, late_weights = in_refs.one(), in_refs.one(), in_refs.some(4)
        late_rows, gain_ref, text_ref, *late_text = in_refs.some(6)
        total, normed, columns_ref, *text_outs = out_refs.some(5)
        attention, beside = out_refs.some(4), out_refs.one()
        sum_scratch, half, got = refs.some(4), refs.one(), refs.one()
        every([late_normed] + late_weights, "start")
        net.greet(NEAR + ALL)
        own = net.load(text_ref.at[net.x], got.at[0])
        first = [net.push(text_ref.at[(net.x + k) % 4], got.at[k], "x", k) for k in (1, 2, 3)]
        gather = Gather(net, columns_hbm, (1, -1), beside.vmem, refs.one(), refs.one())
        normed_in = late_normed.ref()
        for late, out in zip(late_weights[:3], attention):
            out.vmem[...] = low(product(normed_in[...], late.ref()[...]))
        query_ref, keys_ref, values_ref, mixed_ref = [out.vmem for out in attention]
        for _, at, to in each_head(256, 256):
            probs = attend_probs(query_ref[at], keys_ref[to], None)
            mixed_ref[at] = low(product(low(probs), values_ref[to]))
        for out in attention:
            net.store(out)
        output_ref = late_weights[3].ref()
        share = lambda core, n: product(
            mixed_ref[own_rows(core), :], output_ref[:, pl.ds(n * 512, 512)]
        )
        rows_ref, total_ref = late_rows.vmem, total.vmem

        def epilogue(at, value):
            value = rows_ref[at, :] + value
            total_ref[at, :] = value
            return layer_norm(value, gain_ref[...])

        work = TensorSum(net, share, epilogue, normed.vmem, sum_scratch, half)
        work.begin()
        late_rows.start()
        every(late_text, "start")
        work.exchange()
        own.wait()
        for copy in first:
            copy.wait_recv()
        cut = lambda y: pl.ds(pl.multiple_of(y * 256, 256), 256)
        kept = net.load(got.at[:, :, cut(net.y)], columns_ref.at[0])
        second = [
            net.push(got.at[:, :, cut((net.y + k) % 4)], columns_ref.at[k], "y", k)
            for k in (1, 2, 3)
        ]
        text_rows_ref = late_text[0].ref()
        for weight, out in zip(late_text[1:], text_outs):
            out[...] = low(product(text_rows_ref[...], weight.ref()[...]))
        late_rows.ref()
        work.work(gather.hand)
        net.store(total)
        work.finish()
        net.store(normed)
        gather.finish()
        net.store(beside)
        kept.wait()
        for copy in second:
            copy.wait_recv()
        for copy in first + second:
            copy.wait_send()

    copies, loads = TensorSum.COPIES + 22, TensorSum.LOADS + 2
    return call(body, ins, outs, scratch, copies, loads, 0, "forward_self")


def forward_cross(
    columns, normed, weights, keys, values, present, rows, gain, upstream, contract, expand
):
    ins = [(columns, "hbm"), (normed, "load")] + [(weight, "load") for weight in weights]
    ins += [(keys, "vmem"), (values, "vmem"), (present, "vmem")]
    ins += [(rows, "load"), (gain, "vmem"), (upstream, "load"), (contract, "load")]
    ins += [(expand, "load")]
    outs = [(shape(256, 2048), "store"), (shape(512, 2048, kind=BF16), "store")]
    outs += [(shape(512, 2048, kind=BF16), "store")] * 2
    outs += [(shape(512, 512, kind=BF16), "store")] * 2
    outs += [(shape(1, 512, 2048, kind=BF16), "store")]
    scratch = list(TensorSum.SCRATCH + TensorSum.HALF) + [((512, 2048), F32)]
    scratch += [((1, 512, 1024), F32)] * 2

    def body(net, in_refs, out_refs, refs):
        columns_hbm, late_normed, late_query, late_output = in_refs.some(4)
        keys_ref, values_ref, present_ref = in_refs.some(3)
        late_rows, gain_ref, late_upstream, late_contract, late_expand = in_refs.some(5)
        total, normed, active, grad_raised, query, mixed, beyond = out_refs.some(7)
        every([late_normed, late_query, late_output], "start")
        net.greet(NEAR + [("x", 2)])
        query_ref, mixed_ref = query.vmem, mixed.vmem
        query_ref[...] = low(product(late_normed.ref()[...], late_query.ref()[...]))
        for item, at, to in each_head(256, 16):
            probs = attend_probs(query_ref[at], keys_ref[to], present_ref[pl.ds(item, 1), :])
            mixed_ref[at] = low(product(low(probs), values_ref[to]))
        net.store(query)
        net.store(mixed)
        output_ref = late_output.ref()
        share = lambda core, n: product(
            mixed_ref[own_rows(core), :], output_ref[:, pl.ds(n * 512, 512)]
        )
        rows_ref, total_ref = late_rows.vmem, total.vmem

        def epilogue(at, value):
            value = rows_ref[at, :] + value
            total_ref[at, :] = value
            return layer_norm(value, gain_ref[...])

        work = TensorSum(net, share, epilogue, normed.vmem, refs.some(4), refs.one())
        grad_ref = refs.one()
        gather = Gather(net, columns_hbm, (2,), beyond.vmem, refs.one(), refs.one())
        work.begin()
        every([late_upstream, late_contract, late_rows, late_expand], "start")
        work.exchange()
        upstream_ref, contract_ref = late_upstream.ref(), late_contract.ref()

        def part(at):
            grad_ref[:, at] = back_product(upstream_ref[...], contract_ref[at, :])

        blocks(8, 256, part)
        late_rows.ref()
        expand_ref = late_expand.ref()

        def hidden(core):
            rows = own_rows(core)

            def part(at):
                raised = product(normed.vmem[rows, :], expand_ref[:, at])
                inner = raised * (0.7978845608028654 + 0.035677408136300125 * raised * raised)
                bend = jnp.tanh(inner)
                active.vmem[rows, at] = low(0.5 * raised * (1.0 + bend))
                slope = 0.7978845608028654 + 0.10703222440890037 * raised * raised
                slope = 0.5 * (1.0 + bend) + 0.5 * raised * (1.0 - bend * bend) * slope
                grad_raised.vmem[rows, at] = low(grad_ref[rows, at] * slope)

            blocks(8, 256, part)

        work.work(gather.hand)
        net.store(total)
        hidden(net.core)
        work.finish()
        net.store(normed)
        hidden(1 - net.core)
        net.store(active)
        gather.finish()
        net.store(beyond)
        net.store(grad_raised)

    return call(
        body, ins, outs, scratch, TensorSum.COPIES + 8, TensorSum.LOADS, 1, "forward_cross"
    )


def norm_back_sum(net, share, x_ref, gain_ref, rows_ref, low_ref, gain_sum, scratch, half):
    gain_sum[...] = jnp.zeros_like(gain_sum)

    def epilogue(at, total):
        row_grad, terms = norm_back(x_ref[at, :], gain_ref[...], total)
        gain_sum[...] += terms
        result = rows_ref[at, :] + row_grad
        rows_ref[at, :] = result
        return result

    return TensorSum(net, share, epilogue, low_ref, scratch, half)


def every(parts, step):
    for part in parts:
        getattr(part, step)()


def backward_first(grad_raised, expand, x_rows, gain, extra, left, right, contract):
    ins = [(grad_raised, "load"), (expand, "load"), (x_rows, "load"), (gain, "vmem")]
    ins += [(extra, "hbm"), (left, "load")]
    ins += [(right, "load"), (contract, "load")]
    outs = [(shape(256, 2048), "hbm"), (shape(512, 2048, kind=BF16), "store")]
    outs += [(shape(8, 2048), "vmem"), (shape(512, 2048), "store")]
    outs += [(shape(4, 128, JOB), "store")] * 4
    scratch = list(TensorSum.SCRATCH + TensorSum.HALF) + list(RingOne.SCRATCH) * 4

    def body(net, in_refs, out_refs, refs):
        late_raised, late_expand, late_x, gain_ref = in_refs.some(4)
        extra_hbm, late_left, late_right = in_refs.some(3)
        late_contract = in_refs.one()
        rows, lows, gain_sum, out_share, *owns = out_refs.some(8)
        sum_scratch, half = refs.some(4), refs.one()
        rings = [
            RingOne(net, late_left.vmem, late_right.vmem, i, i % 2 == 0, owns[i].vmem, refs.some(3))
            for i in range(4)
        ]
        every([late_left, late_right, late_raised, late_expand], "start")
        net.greet(NEAR + RING)
        x_ref, raised_ref, expand_ref = late_x.vmem, late_raised.vmem, late_expand.vmem
        share = lambda core, n: back_product(
            raised_ref[own_rows(core), :], expand_ref[pl.ds(n * 512, 512), :]
        )
        work = norm_back_sum(
            net, share, x_ref, gain_ref, half, lows.vmem, gain_sum, sum_scratch, half
        )
        late_left.ref(), late_right.ref()
        every(rings, "begin")
        late_raised.ref(), late_expand.ref()
        work.begin()
        every([late_contract, late_x], "start")
        work.exchange()
        work.free_half()
        extra_copy = net.load(extra_hbm, half)
        every(rings, "relay")
        right_ref, contract_ref = late_right.ref(), late_contract.ref()

        def part(at):
            out_share.vmem[:, at] = product(right_ref[...], contract_ref[:, at])

        blocks(8, 256, part)
        late_x.ref()
        joins = jnp.where(net.tensor < 2, 1.0, 0.0)

        def join(i, carry):
            at = pl.ds(pl.multiple_of(i * 16, 16), 16)
            to = pl.ds(pl.multiple_of(net.core * 256 + i * 16, 16), 16)
            out_share.vmem[to, :] += x_ref[at, :] * joins
            return carry

        lax.fori_loop(0, 16, join, 0)
        net.store(out_share)
        extra_copy.wait()
        work.work()
        net.stores.append(net.load(half, rows))
        work.finish()
        net.store(lows)
        for ring, own in zip(rings, owns):
            ring.close()
            net.store(own)
        every(rings, "done")

    copies, loads = TensorSum.COPIES + 4 * RingOne.COPIES, 2
    return call(body, ins, outs, scratch, copies, loads, 2, "backward_first")


def backward_second(
    attention, weights, present, x_rows, gain, extra, owns, wide, upstream, mixed, normed, out_share
):
    ones = [(0, i, i % 2 == 0) for i in range(4)] + [(1, 0, True), (2, 0, False)]
    query, keys, values = attention
    ins = [(query, "load"), (keys, "vmem"), (values, "vmem"), (present, "vmem")]
    ins += [(weights[0], "load"), (weights[1], "hbm"), (x_rows, "load"), (gain, "vmem")]
    ins += [(extra, "hbm"), (out_share, "hbm")] + [(own, "hbm") for own in owns]
    ins += [(array, "load") for array in (*wide, upstream, mixed, normed)]
    outs = [(shape(256, 2048), "hbm"), (shape(512, 2048, kind=BF16), "store")]
    outs += [(shape(8, 2048), "vmem")] + [(shape(4, 4, 32, 512), "vmem")] * 2
    outs += [(shape(512, 2048, kind=BF16), "hbm")]
    outs += [(shape(64, JOB), "vmem")] * len(owns)
    outs += [(shape(4, 128, JOB), "store")] * len(ones)
    scratch = list(TensorSum.SCRATCH + TensorSum.HALF) + [TensorSum.SCRATCH[0]]
    scratch += [((512, 512), BF16)]
    scratch += list(RingTwo.SCRATCH + RingTwo.PARTS) * len(owns)
    scratch += list(RingOne.SCRATCH) * len(ones)

    def body(net, in_refs, out_refs, refs):
        late_cross, keys_ref, values_ref, present_ref = in_refs.some(4)
        late_weight, output_hbm, late_x, gain_ref, extra_hbm, out_share_ref = in_refs.some(6)
        own_refs, late_wide, late_narrow = in_refs.some(len(owns)), in_refs.some(2), in_refs.some(3)
        rows, lows, gain_sum, keys_all, values_all, layer_out = out_refs.some(6)
        final_refs, nexts = out_refs.some(len(owns)), out_refs.some(len(ones))
        mine, got_core, got_z, got_rows = refs.some(4)
        half, got_z_two, grad_mixed = refs.some(3)
        grad_cross = late_cross.vmem
        twos = [
            RingTwo(net, own, i % 2 == 0, final_refs[i], refs.some(2), refs.one())
            for i, own in enumerate(own_refs)
        ]
        pairs = [[late.vmem for late in late_wide], [late.vmem for late in late_narrow[:2]]]
        pairs.append([late_narrow[2].vmem, grad_cross])
        rings = [
            RingOne(net, *pairs[p], c, x_first, nexts[i].vmem, refs.some(3))
            for i, (p, c, x_first) in enumerate(ones)
        ]
        every(late_wide + late_narrow[:2], "start")
        output_copy = net.load(output_hbm, lows.vmem)
        every([late_cross, late_weight, late_narrow[2], late_x], "start")
        net.greet(NEAR + ALL + [("zhi", 1)])
        weight_ref = late_weight.vmem
        share = lambda core, n: back_product(
            grad_cross[own_rows(core), :], weight_ref[pl.ds(n * 512, 512), :]
        )
        work = norm_back_sum(
            net,
            share,
            late_x.vmem,
            gain_ref,
            half,
            lows.vmem,
            gain_sum,
            (mine, got_core, got_z, got_rows),
            half,
        )
        layer = TensorSum(
            net,
            out_share_ref,
            lambda at, total: total,
            lows.vmem,
            (mine, got_core, got_z_two, got_rows),
        )
        every(twos, "begin")
        every(late_wide, "ref")
        every(rings[:4], "begin")
        every(late_narrow[:2], "ref")
        output_copy.wait()
        grad_mixed[...] = low(back_product(late_narrow[0].vmem[...], lows.vmem[...]))
        query_ref = late_cross.ref()
        for item, at, to in each_head(256, 16):
            grad_query, grad_keys, grad_values = attend_backward(
                query_ref[at],
                keys_ref[to],
                values_ref[to],
                present_ref[pl.ds(item, 1), :],
                grad_mixed[at],
            )
            grad_cross[at] = grad_query
            keys_all[0, 0, to[0], to[1]] = grad_keys.astype(F32)
            values_all[0, 0, to[0], to[1]] = grad_values.astype(F32)
        late_weight.ref()
        work.begin()
        texts = [
            net.push(ref.at[0, 0], ref.at[0, k], axis, k)
            for ref, axis in ((keys_all, "x"), (values_all, "y"))
            for k in (1, 2, 3)
        ]
        every(rings[4:5], "begin")
        late_narrow[2].ref()
        every(rings[5:], "begin")
        work.exchange()
        work.free_half()
        extra_copy = net.load(extra_hbm, half)
        every(twos, "relay")
        every(rings, "relay")
        for copy in texts:
            copy.wait_recv()
        texts += [
            net.push(ref.at[0], ref.at[k], axis, k)
            for ref, axis in ((keys_all, "y"), (values_all, "x"))
            for k in (1, 2, 3)
        ]
        late_x.ref()
        extra_copy.wait()
        work.work()
        net.stores.append(net.load(half, rows))
        work.finish()
        net.release("core")
        lows_copy = net.load(lows.vmem, lows.hbm)
        net.await_release()
        layer.begin()
        layer.exchange()
        every(twos, "third")
        for ring, own in zip(rings[:2] + rings[4:], nexts[:2] + nexts[4:]):
            ring.close()
            net.store(own)
        every(twos, "finish")
        lows_copy.wait()
        layer.work()
        layer.finish()
        net.stores.append(net.load(lows.vmem, layer_out))
        for ring, own in zip(rings[2:4], nexts[2:4]):
            ring.close()
            net.store(own)
        for copy in texts[6:]:
            copy.wait_recv()
        for copy in texts:
            copy.wait_send()
        every(rings, "done")

    copies = 2 * TensorSum.COPIES + 12 + len(owns) * RingTwo.COPIES + len(ones) * RingOne.COPIES
    loads = TensorSum.LOADS + 5 + len(owns) * RingTwo.LOADS
    return call(body, ins, outs, scratch, copies, loads, 3, "backward_second")


def backward_last(
    attention, weights, upstream, normed, beside, beyond, x_rows, gain, extra, keep, owns, text_grad, sums
):
    count = 1
    ins = [(array, "load") for array in attention] + [(weights[3], "hbm")]
    ins += [(weight, "hbm") for weight in weights[:3]]
    ins += [(upstream, "load"), (normed, "load"), (beside, "hbm"), (beyond, "hbm"), (x_rows, "load"), (gain, "vmem"), (extra, "hbm"), (keep, "vmem")]
    ins += [(text_grad, "hbm"), (sums, "vmem")] + [(own, "hbm") for own in owns]
    outs = [(shape(512, 2048, kind=BF16), "store"), (shape(8, 2048), "vmem")]
    outs += [(shape(128, 1024), "vmem")] + [(shape(64, JOB), "vmem")] * (len(owns) + count)
    outs += [(shape(4, 64, RingHeads.WIDTH), "vmem")]
    scratch = list(TensorSum.SCRATCH + TensorSum.HALF) + [((512, 512), BF16)] * 4
    scratch += [((512, 2048), BF16)] * 3 + [((512, RingHeads.WIDTH), BF16)] * 4
    scratch += [((3, 512, RingHeads.WIDTH), F32)] * 2
    scratch += list(RingHeads.SCRATCH + RingHeads.LAST)
    scratch += [((16, 2048), F32), ((128, 1024), F32), ((9, 8, 2048), F32)]
    scratch += list(RingTwo.SCRATCH + RingTwo.PARTS) * len(owns)
    scratch += (list(RingTwo.SCRATCH + RingOne.SCRATCH) + [((4, 128, JOB), F32)]) * count

    def body(net, in_refs, out_refs, refs):
        late_attention, late_output, weights_hbm = in_refs.some(4), in_refs.one(), in_refs.some(3)
        late_upstream, late_normed, beside_hbm, beyond_hbm = in_refs.some(4)
        late_x, gain_ref, extra_hbm, keep_ref, text_ref, sums_ref = in_refs.some(6)
        own_refs = in_refs.some(len(owns))
        image, small_ref, text_out = out_refs.some(3)
        old_refs, new_refs, heads_out = out_refs.some(len(owns)), out_refs.some(count), out_refs.one()
        sum_scratch, half, grad_mixed, grads = refs.some(4), refs.one(), refs.one(), refs.some(3)
        rooms, rights, (leaving, arriving) = refs.some(3), refs.some(4), refs.some(2)
        heads_scratch, heads_last = refs.some(4), refs.some(2)
        acc_ref, got_text, got_small = refs.some(3)
        old = [
            RingTwo(net, own, i % 2 == 0, old_refs[i], refs.some(2), refs.one())
            for i, own in enumerate(own_refs)
        ]
        ones, twos = [], []
        for i in range(count):
            two_scratch, one_scratch, own = refs.some(2), refs.some(3), refs.one()
            left, right = late_upstream.vmem, late_attention[3].vmem
            ones.append(RingOne(net, left, right, 0, False, own, one_scratch))
            twos.append(RingTwo(net, own, False, new_refs[i], two_scratch))
        lefts = [late_normed.vmem] + rooms
        heads = RingHeads(net, lefts, rights, heads_out, heads_scratch, heads_last)
        output_copy = net.load(late_output, image.vmem)
        every([late_upstream, late_attention[3]] + late_attention[:3], "start")
        weight_copies = [
            net.load(weight.at[pl.ds(n * 512, 512)], room.at[:, pl.ds(n * 512, 512)])
            for weight, room in zip(weights_hbm, rooms)
            for n in range(4)
        ]
        late_normed.start()
        net.greet(NEAR + ALL + [("zhi", 1)])
        acc_ref[...] = jnp.zeros_like(acc_ref)
        x_ref, extra_ref = late_x.vmem, half

        def epilogue(at, total):
            row_grad, terms = norm_back(x_ref[at, :], gain_ref[...], total)
            result = extra_ref[at, :] + row_grad
            kept = keep_ref[at, :] > 0.5
            acc_ref[0:8, :] += terms
            acc_ref[8:16, :] += jnp.where(kept, 0.0, result)
            return jnp.where(kept, result, 0.0)

        text_rows = lambda z: pl.ds(pl.multiple_of(z * 128, 128), 128)
        text_push = net.push(text_ref.at[text_rows(1 - net.z)], got_text, "zhi")
        every(old, "begin")
        every([late_upstream, late_attention[3]], "ref")
        ones[0].begin()
        output_copy.wait()
        grad_mixed[...] = low(back_product(late_upstream.vmem[...], image.vmem[...]))
        late_x.start()
        text_copy = net.load(text_ref.at[text_rows(net.z)], text_out)
        query_ref, keys_ref, values_ref = [late.ref() for late in late_attention[:3]]
        every(old, "relay")
        for _, at, to in each_head(256, 256):
            found = attend_backward(
                query_ref[at], keys_ref[to], values_ref[to], None, grad_mixed[at]
            )
            for ref, value in zip(grads, found):
                ref[at] = value
        head = lambda x: pl.ds(pl.multiple_of(x * HEAD, HEAD), HEAD)
        for i, ref in enumerate(grads):
            columns = pl.ds(i * HEAD, HEAD)
            rights[0][:, columns] = ref[:, head(net.x)]
            for k in (1, 2, 3):
                leaving[k - 1, :, columns] = ref[:, head((net.x + k) % 4)].astype(F32)
        spread = [
            net.push(leaving.at[k - 1], arriving.at[k - 1], "x", k) for k in (1, 2, 3)
        ]
        for copy in weight_copies:
            copy.wait()

        def share(core, n):
            block, total = pl.ds(n * 512, 512), 0.0
            for ref, weight in zip(grads, rooms):
                total = total + back_product(ref[own_rows(core), :], weight[:, block])
            return total

        work = TensorSum(net, share, epilogue, image.vmem, sum_scratch, half)
        work.begin()
        others = (beside_hbm.at[0], beyond_hbm.at[0], beside_hbm.at[1])
        left_copies = [net.load(source, room) for source, room in zip(others, rooms)]
        work.exchange()
        work.free_half()
        extra_copy = net.load(extra_hbm, half)
        every(ones, "relay")
        late_normed.ref()
        for copy in left_copies:
            copy.wait()
        for k in range(3):
            spread[k].wait_recv()
            rights[k + 1][...] = low(arriving[k])
        heads.begin()
        late_x.ref()
        extra_copy.wait()
        work.work(lambda j: heads.relay() if j == 3 else every(old[3 * j : 3 * j + 3], "third"))
        got_small[0] = sums_ref[...]
        got_small[0, 0:1, :] = jnp.sum(acc_ref[0:8, :], axis=0, keepdims=True)
        got_small[0, 3:4, :] = jnp.sum(acc_ref[8:16, :], axis=0, keepdims=True)
        by_core = net.push(got_small.at[0], got_small.at[1], "core")
        work.finish()
        net.store(image)
        by_core.wait()
        got_small[0] += got_small[1]
        by_x = [net.push(got_small.at[0], got_small.at[1 + k], "x", k) for k in (1, 2, 3)]
        for one, two in zip(ones, twos):
            one.close()
            two.begin()
        heads.close()
        heads.swap()
        every(old, "finish")
        for copy in by_x:
            copy.wait()
        got_small[0] += got_small[2] + got_small[3] + got_small[4]
        by_y = [net.push(got_small.at[0], got_small.at[4 + k], "y", k) for k in (1, 2, 3)]
        every(twos, "relay")
        for copy in by_y:
            copy.wait()
        got_small[0] += got_small[5] + got_small[6] + got_small[7]
        by_z = net.push(got_small.at[0], got_small.at[8], "zhi")
        every(twos, "third")
        heads.third()
        text_copy.wait()
        text_push.wait()
        text_out[...] += got_text[...]
        by_z.wait()
        small_ref[...] = got_small[0] + got_small[8]
        every(twos, "finish")
        heads.finish()
        heads.done()
        for copy in spread:
            copy.wait_send()
        every(ones, "done")

    copies = TensorSum.COPIES + 9 + (len(owns) + count) * RingTwo.COPIES + count * RingOne.COPIES
    copies += RingHeads.COPIES + RingHeads.COPIES_LAST + 3
    loads = 18 + len(owns) * RingTwo.LOADS
    return call(body, ins, outs, scratch, copies, loads, 4, "backward_last")


def shards(
    image,
    text,
    masked,
    text_len,
    cotangent,
    self_query,
    self_key,
    self_value,
    self_output,
    text_query,
    text_key,
    text_value,
    text_output,
    expand,
    contract,
    first_gain,
    second_gain,
    third_gain,
    mask_token,
):
    items, length, width = image.shape
    words = text.shape[1]
    count = items * length
    core = lax.axis_index("tensor") % 2
    gains = [g.reshape(1, width) for g in (first_gain, second_gain, third_gain)]
    own = lambda rows: lax.dynamic_slice_in_dim(rows, core * length, length, axis=0)

    text_rows = text.reshape(items * words, text.shape[2])
    text_blocks = text_rows.astype(F32).reshape(items * words, 4, -1).transpose(1, 0, 2)
    upstream = cotangent.reshape(count, width)

    hidden = masked.reshape(count, 1) == 1
    start = jnp.where(hidden, mask_token[None, :], image.reshape(count, width).astype(F32))
    normed_one = low(layer_norm(start, first_gain))
    weights = (self_query, self_key, self_value, self_output)
    start_own = own(start)
    columns = lax.dynamic_slice_in_dim(normed_one, core * (width // 2), width // 2, axis=1)
    columns = columns.astype(F32)
    first, normed_two, text_columns, cross_keys, cross_values, *attention, beside = forward_self(
        normed_one,
        columns,
        weights,
        start_own,
        gains[1],
        text_blocks,
        text_rows,
        text_key,
        text_value,
    )
    text_columns = low(text_columns.reshape(-1, text_columns.shape[-1]))

    present = (jnp.arange(words)[None, :] < text_len[:, None]).astype(F32)
    second, normed_three, active, grad_raised, cross_query, cross_rows, beyond = forward_cross(
        columns,
        normed_two,
        (text_query, text_output),
        cross_keys,
        cross_values,
        present,
        first,
        gains[2],
        upstream,
        contract,
        expand,
    )
    grad_second, cross_out_grad, third_sum, out_share, *owns = backward_first(
        grad_raised,
        expand,
        second,
        gains[2],
        own(upstream).astype(F32),
        upstream,
        active,
        contract,
    )
    grad_first, self_out_grad, second_sum, text_k, text_v, layer_out, *rest = backward_second(
        (cross_query, cross_keys, cross_values),
        (text_query, text_output),
        present,
        first,
        gains[1],
        grad_second,
        owns,
        (normed_three, grad_raised),
        cross_out_grad,
        cross_rows,
        normed_two,
        out_share,
    )
    contract_t, owns = rest[:4], rest[4:]
    text_v = text_v.transpose(1, 0, 2, 3)
    gathered = low(jnp.concatenate([text_k, text_v], axis=3).reshape(text_columns.shape[0], -1))
    text_grads = outer_sum(text_columns, gathered)

    sums = jnp.zeros((8, width), F32)
    sums = sums.at[1].set(jnp.sum(second_sum, axis=0)).at[2].set(jnp.sum(third_sum, axis=0))
    keep = 1.0 - own(masked.reshape(count, 1)).astype(F32)
    image_grad, small, text_grads, *rest = backward_last(
        attention,
        weights,
        self_out_grad,
        normed_one,
        beside,
        beyond,
        start_own,
        gains[0],
        grad_first,
        keep,
        owns,
        text_grads,
        sums,
    )
    expand_grad, (to, tq, so, heads) = rest[:4], rest[4:]
    heads = heads.reshape(4, -1, 3, HEAD).transpose(2, 1, 0, 3)
    sq, sk, sv = heads.reshape(3, heads.shape[1], -1)

    share = width // 32
    small = lax.dynamic_slice_in_dim(small, lax.axis_index("dp") * share, share, axis=1)
    cut = text_grads.shape[1] // 2
    joined = lambda parts: jnp.concatenate(parts, axis=1)
    return (
        layer_out.reshape(image.shape),
        image_grad.reshape(image.shape),
        sq,
        sk,
        sv,
        so.T,
        tq,
        text_grads[:, :cut],
        text_grads[:, cut:],
        to.T,
        joined(expand_grad),
        joined(contract_t).T,
        small[0],
        small[1],
        small[2],
        small[3],
    )


def solution(mesh):
    rows, split = P("dp", None, None), P(None, "tensor")
    turned, grads, grads_t = P("tensor", None), P("dp", "tensor"), P("tensor", "dp")
    ins = (rows, rows, P("dp", None), P("dp"), rows, split, split, split, turned)
    ins += (split, split, split, turned, split, turned, P(), P(), P(), P())
    outs = (rows, rows, grads, grads, grads, grads_t, grads, grads, grads, grads_t)
    outs += (grads, grads_t, P("dp"), P("dp"), P("dp"), P("dp"))
    return jax.shard_map(shards, mesh=mesh, in_specs=ins, out_specs=outs, check_vma=False)
```

```python
import functools

import jax
import jax.numpy as jnp
from jax import lax
from jax.experimental import pallas as pl
from jax.experimental.pallas import tpu as pltpu
from jax.sharding import PartitionSpec as P

HEAD = 128
EPS = 1e-05
MESH = pl.DeviceIdType.MESH
F32, BF16 = jnp.float32, jnp.bfloat16
CHUNK = 64
JOB = 512


def product(left, right):
    return jnp.dot(left, right, preferred_element_type=F32)


def outer_sum(left, right):
    return lax.dot_general(left, right, (((0,), (0,)), ((), ())), preferred_element_type=F32)


def back_product(left, right):
    return lax.dot_general(left, right, (((1,), (1,)), ((), ())), preferred_element_type=F32)


def low(value):
    return value.astype(BF16)


def layer_norm(rows, gain):
    mean = jnp.mean(rows, axis=-1, keepdims=True)
    centred = rows - mean
    spread = jnp.mean(centred * centred, axis=-1, keepdims=True)
    return centred * lax.rsqrt(spread + EPS) * gain


def norm_back(rows, gain, grad):
    mean = jnp.mean(rows, axis=-1, keepdims=True)
    centred = rows - mean
    spread = jnp.mean(centred * centred, axis=-1, keepdims=True)
    root = lax.rsqrt(spread + EPS)
    xhat = centred * root
    scaled = grad * gain
    row_grad = root * (
        scaled
        - jnp.mean(scaled, axis=-1, keepdims=True)
        - xhat * jnp.mean(scaled * xhat, axis=-1, keepdims=True)
    )
    return row_grad, grad * xhat


def attend_probs(query, keys, valid):
    scores = back_product(query, keys) * HEAD ** (-0.5)
    if valid is not None:
        scores = jnp.where(valid > 0.5, scores, -1e30)
    raised = jnp.exp(scores - jnp.max(scores, axis=-1, keepdims=True))
    return raised / jnp.sum(raised, axis=-1, keepdims=True)


def attend_backward(query, keys, values, valid, upstream):
    scale = HEAD ** (-0.5)
    probs = attend_probs(query, keys, valid)
    grad_values = outer_sum(low(probs), upstream)
    grad_probs = back_product(upstream, values)
    inner = jnp.sum(grad_probs * probs, axis=-1, keepdims=True)
    grad_scores = low(probs * (grad_probs - inner))
    grad_query = product(grad_scores, keys) * scale
    grad_keys = outer_sum(grad_scores, query) * scale
    return low(grad_query), low(grad_keys), low(grad_values)


class Net:
    def __init__(self, send, recv, local, free):
        dp, tensor = lax.axis_index("dp"), lax.axis_index("tensor")
        self.x, self.y, self.z = dp // 8, (dp // 2) % 4, dp % 2
        self.tensor, self.core = tensor, tensor % 2
        self.send, self.recv, self.local, self.free = send, recv, local, free
        self.sent, self.loads, self.stores = 0, 0, []

    def device(self, kind, step=1):
        x, y, z, tensor = self.x, self.y, self.z, self.tensor
        if kind == "x":
            x = (x + step + 4) % 4
        elif kind == "y":
            y = (y + step + 4) % 4
        elif kind == "zhi":
            z = 1 - z
        elif kind == "zlo":
            tensor = (tensor + 2) % 4
        else:
            tensor = tensor + 1 - 2 * self.core
        return (x * 8 + y * 2 + z, tensor)

    def greet(self, partners):
        barrier = pltpu.get_barrier_semaphore()
        for kind, step in partners:
            pl.semaphore_signal(
                barrier, inc=1, device_id=self.device(kind, step), device_id_type=MESH
            )
        pl.semaphore_wait(barrier, len(partners))

    def release(self, kind):
        pl.semaphore_signal(self.free, inc=1, device_id=self.device(kind), device_id_type=MESH)

    def await_release(self):
        pl.semaphore_wait(self.free, 1)

    def push(self, source, target, kind, step=1):
        copy = pltpu.make_async_remote_copy(
            src_ref=source,
            dst_ref=target,
            send_sem=self.send.at[self.sent],
            recv_sem=self.recv.at[self.sent],
            device_id=self.device(kind, step),
            device_id_type=MESH,
        )
        self.sent += 1
        copy.start()
        return copy

    def load(self, source, target):
        copy = pltpu.make_async_copy(source, target, self.local.at[self.loads])
        self.loads += 1
        copy.start()
        return copy

    def store(self, out):
        self.stores.append(self.load(out.vmem, out.hbm))


class Late:
    def __init__(self, net, hbm, vmem):
        self.net, self.hbm, self.vmem, self.copy, self.here = net, hbm, vmem, None, False

    def start(self):
        self.copy = self.net.load(self.hbm, self.vmem)

    def ref(self):
        if self.copy is None:
            self.start()
        if not self.here:
            self.copy.wait()
            self.here = True
        return self.vmem


class Out:
    def __init__(self, hbm, vmem):
        self.hbm, self.vmem = hbm, vmem


def add_rows(target, *sources):
    rows = target.shape[0]
    step = 16 if target.shape[1] > 1024 else 32

    def body(i, carry):
        at = pl.ds(pl.multiple_of(i * step, step), step)
        value = target[at, :]
        for source in sources:
            value = value + source[at, :]
        target[at, :] = value
        return carry

    lax.fori_loop(0, rows // step, body, 0)


def each_head(rows, other_rows):
    for item in range(2):
        for head in range(4):
            columns = pl.ds(head * HEAD, HEAD)
            yield (
                item,
                (pl.ds(item * rows, rows), columns),
                (pl.ds(item * other_rows, other_rows), columns),
            )


class RingOne:
    SCRATCH = (
        ((2, 2, 128, JOB), F32),
        ((2, 2, 128, JOB), F32),
        ((2, 2, 128, JOB), F32),
    )
    COPIES = 6

    def __init__(self, net, left, right, column, x_first, own, scratch):
        self.net, self.left, self.right, self.own = net, left, right, own
        self.column = column * JOB
        self.x_first = x_first
        self.axis, self.one = ("x", net.x) if x_first else ("y", net.y)
        self.sending, self.got, self.beside = scratch

    def piece(self, step, half, target, add=False):
        at = (self.one + step) % 4
        if self.x_first:
            left = self.left[:, pl.ds(pl.multiple_of(at * 512 + half * 256, 256), 256)]
        else:
            cut = lambda x: self.left[:, pl.ds(pl.multiple_of(x * 512 + at * 128, 128), 128)]
            left = jnp.concatenate([cut(2 * half), cut(2 * half + 1)], axis=1)
        for n in range(JOB // 256):
            value = outer_sum(left, self.right[:, pl.ds(self.column + n * 256, 256)])
            for j in range(2):
                part = value[j * 128 : (j + 1) * 128]
                if add:
                    part = part + target[j, :, pl.ds(n * 256, 256)]
                target[j, :, pl.ds(n * 256, 256)] = part

    def begin(self):
        self.far = []
        for half, step in enumerate((1, -1)):
            self.piece(2, half, self.sending.at[half])
            self.far.append(
                self.net.push(self.sending.at[half], self.got.at[half], self.axis, step)
            )

    def relay(self):
        net, axis = self.net, self.axis
        self.last, self.near = [], []
        for i, (step, at) in enumerate(((1, 1), (-1, 3))):
            self.far[i].wait_recv()
            self.piece(at, i, self.got.at[i], True)
            self.last.append(net.push(self.got.at[i], self.own.at[pl.ds(2 * i, 2)], axis, step))
        for i, (step, at) in enumerate(((1, 1), (-1, 3))):
            self.far[i].wait_send()
            self.piece(at, 1 - i, self.sending.at[i])
            self.near.append(net.push(self.sending.at[i], self.beside.at[1 - i], axis, step))

    def close(self):
        for half in range(2):
            self.near[1 - half].wait_recv()
            self.piece(0, half, self.beside.at[half], True)
        for half in range(2):
            self.last[half].wait_recv()
            for j in range(2):
                add_rows(self.own.at[2 * half + j], self.beside.at[half, j])

    def done(self):
        for copy in self.last + self.near:
            copy.wait_send()


class RingTwo:
    SCRATCH = (((6, 64, JOB), F32), ((64, JOB), F32))
    PARTS = (((4, 64, JOB), F32),)
    COPIES, LOADS = 7, 4

    def __init__(self, net, own, x_first, out, scratch, parts=None):
        self.net, self.own, self.out, self.parts = net, own, out, parts
        self.axis, self.two = ("y", net.y) if x_first else ("x", net.x)
        self.got, self.got_last = scratch

    def part(self, step, half):
        return self.own.at[(self.two + step) % 4, pl.ds(half * 64, 64), :]

    def begin(self):
        net, axis, got = self.net, self.axis, self.got
        self.far = [
            net.push(self.part(2, 0), got.at[0], axis, 1),
            net.push(self.part(2, 1), got.at[1], axis, -1),
        ]
        self.near = [
            net.push(self.part(1, 1), got.at[4], axis, 1),
            net.push(self.part(3, 0), got.at[5], axis, -1),
        ]
        self.read = [self.part(*at) for at in ((1, 0), (3, 1), (0, 0), (0, 1))]
        self.loading = []
        if self.parts is not None:
            self.loading = [net.load(ref, self.parts.at[i]) for i, ref in enumerate(self.read)]
            self.read = [self.parts.at[i] for i in range(4)]

    def relay(self):
        net, axis, got = self.net, self.axis, self.got
        self.last = []
        for copy in self.loading:
            copy.wait()
        for i, step in enumerate((1, -1)):
            self.far[i].wait_recv()
            add_rows(got.at[i], self.read[i])
            self.last.append(net.push(got.at[i], got.at[2 + i], axis, step))

    def third(self):
        net, got = self.net, self.got
        for copy in self.near + self.last:
            copy.wait_recv()
        add_rows(got.at[5], got.at[2], self.read[2])
        add_rows(got.at[4], got.at[3], self.read[3])
        self.final = net.push(got.at[4 + net.z], self.got_last, "zhi")

    def finish(self):
        self.final.wait_recv()
        self.out[...] = self.got[5 - self.net.z] + self.got_last[...]
        for copy in self.far + self.near + self.last + [self.final]:
            copy.wait_send()


class RingHeads(RingOne):
    WIDTH = 3 * HEAD
    SCRATCH = (((2, 2, 128, WIDTH), F32),) * 3 + (((4, 128, WIDTH), F32),)
    LAST = (((4, 128, WIDTH), F32), ((4, 64, WIDTH), F32))
    COPIES_LAST = 4

    def __init__(self, net, lefts, rights, out, scratch, last):
        self.net, self.lefts, self.rights, self.out = net, lefts, rights, out
        self.axis, self.one = "y", net.y
        self.sending, self.got, self.beside, self.own = scratch
        self.heads, self.got_last = last

    def piece(self, step, half, target, add=False):
        at, total = (self.one + step) % 4, 0.0
        for left, right in zip(self.lefts, self.rights):
            cut = lambda x: left[:, pl.ds(pl.multiple_of(x * 512 + at * 128, 128), 128)]
            both = jnp.concatenate([cut(2 * half), cut(2 * half + 1)], axis=1)
            total = total + outer_sum(both, right[...])
        for j in range(2):
            part = total[j * 128 : (j + 1) * 128]
            if add:
                part = part + target[j]
            target[j] = part

    def swap(self):
        net = self.net
        self.swaps = [
            net.push(self.own.at[(net.x + k) % 4], self.heads.at[k], "x", k) for k in (1, 2, 3)
        ]
        self.heads[0] = self.own[net.x]

    def third(self):
        net = self.net
        for copy in self.swaps:
            copy.wait_recv()
        rows = pl.ds(pl.multiple_of((1 - net.z) * 64, 64), 64)
        self.final = net.push(self.heads.at[:, rows], self.got_last, "zhi")

    def finish(self):
        self.final.wait_recv()
        rows = pl.ds(pl.multiple_of(self.net.z * 64, 64), 64)
        for k in range(4):
            self.out[(self.net.x + 4 - k) % 4] = self.heads[k, rows, :] + self.got_last[k]
        for copy in self.swaps + [self.final]:
            copy.wait_send()


class Gather:
    def __init__(self, net, source, steps, out, got, got_core):
        self.net, self.out, self.got, self.got_core = net, out, got, got_core
        self.slots = range(len(steps))
        self.copies, self.handed = [], []
        for j in range(4):
            at = pl.ds(j * 128, 128)
            self.copies.append(
                [net.push(source.at[at], got.at[i, at], "x", step) for i, step in enumerate(steps)]
            )

    def hand(self, j):
        at = pl.ds(j * 128, 128)
        for i in self.slots:
            self.copies[j][i].wait_recv()
            self.handed.append(
                self.net.push(self.got.at[i, at], self.got_core.at[i, at], "core")
            )

    def keep(self, source, core):
        columns = pl.ds(pl.multiple_of(core * 1024, 1024), 1024)
        for i in self.slots:

            def body(n, carry, i=i):
                at = pl.ds(pl.multiple_of(n * 16, 16), 16)
                self.out[i, at, columns] = source[i, at, :].astype(BF16)
                return carry

            lax.fori_loop(0, 32, body, 0)

    def finish(self):
        self.keep(self.got, self.net.core)
        for copy in self.handed:
            copy.wait_recv()
        self.keep(self.got_core, 1 - self.net.core)
        for copy in [copy for step in self.copies for copy in step] + self.handed:
            copy.wait_send()


class TensorSum:
    SCRATCH = tuple(((256 // CHUNK, CHUNK, 2048), F32) for _ in range(4))
    COPIES, LOADS = 3 * (256 // CHUNK), 256 // CHUNK

    HALF = (((256, 2048), F32),)

    def __init__(self, net, share, epilogue, whole, scratch, half=None):
        self.net, self.share, self.epilogue, self.whole = net, share, epilogue, whole
        self.half = half
        self.mine, self.got_core, self.got_z, self.got_rows = scratch
        self.steps = range(256 // CHUNK)

    def rows(self, core, step):
        return pl.ds(pl.multiple_of(core * 256 + step * CHUNK, CHUNK), CHUNK)

    def free_half(self):
        for copy in self.swaps:
            copy.wait_send()
        self.swaps_sent = True

    def begin(self):
        net = self.net
        self.loading, self.swaps_sent = [], False
        if self.half is not None:
            for n in range(4):
                self.half[:, pl.ds(n * 512, 512)] = self.share(1 - net.core, n)
            self.swaps = [
                net.push(self.half.at[pl.ds(j * CHUNK, CHUNK)], self.got_core.at[j], "core")
                for j in self.steps
            ]
            for n in range(4):
                value = self.share(net.core, n)
                for j in self.steps:
                    rows = value[j * CHUNK : (j + 1) * CHUNK]
                    self.mine[j, :, pl.ds(n * 512, 512)] = rows
            return
        self.swaps = [
            net.push(self.share.at[self.rows(1 - net.core, j)], self.got_core.at[j], "core")
            for j in self.steps
        ]
        self.loading = [
            net.load(self.share.at[self.rows(net.core, j)], self.mine.at[j]) for j in self.steps
        ]

    def exchange(self):
        self.over = []
        for copy in self.loading:
            copy.wait()
        for j in self.steps:
            self.swaps[j].wait_recv()
            add_rows(self.mine.at[j], self.got_core.at[j])
            self.over.append(self.net.push(self.mine.at[j], self.got_z.at[j], "zlo"))

    def work(self, hook=None):
        net = self.net
        self.spread = []
        for j in self.steps:
            if hook is not None:
                hook(j)
            self.over[j].wait_recv()

            def body(i, carry, j=j):
                at = pl.ds(pl.multiple_of(i * 8, 8), 8)
                rows = pl.ds(pl.multiple_of(j * CHUNK + i * 8, 8), 8)
                self.got_core[j, at, :] = self.epilogue(
                    rows, self.mine[j, at, :] + self.got_z[j, at, :]
                )
                return carry

            lax.fori_loop(0, CHUNK // 8, body, 0)
            self.spread.append(net.push(self.got_core.at[j], self.got_rows.at[j], "core"))
            self.round(self.got_core, j, net.core)

    def round(self, source, step, core):
        def body(i, carry):
            at = pl.ds(pl.multiple_of(i * 16, 16), 16)
            rows = pl.ds(pl.multiple_of(core * 256 + step * CHUNK + i * 16, 16), 16)
            self.whole[rows, :] = source[step, at, :].astype(BF16)
            return carry

        lax.fori_loop(0, CHUNK // 16, body, 0)

    def finish(self):
        for j in self.steps:
            self.spread[j].wait_recv()
            self.round(self.got_rows, j, 1 - self.net.core)
        for copy in ([] if self.swaps_sent else self.swaps) + self.over + self.spread:
            copy.wait_send()


NEAR = [("core", 1), ("zlo", 1)]
RING = [("x", 1), ("x", -1), ("y", 1), ("y", -1)]
ALL = [("x", 1), ("x", 2), ("x", 3), ("y", 1), ("y", 2), ("y", 3)]


def vmem(shapes):
    return [pltpu.VMEM(shape, kind) for shape, kind in shapes]


def call(body, ins, outs, scratch, copies, loads, number, name):
    spec = lambda how: pl.BlockSpec(memory_space=pltpu.VMEM if how == "vmem" else pl.ANY)
    late = [(a.shape, a.dtype) for a, how in ins if how == "load"]
    kept = [(o.shape, o.dtype) for o, how in outs if how == "store"]

    def kernel(*refs):
        refs, net = Refs(refs[:-4]), Net(*refs[-4:])
        in_refs, out_refs = refs.some(len(ins)), refs.some(len(outs))
        late_refs, kept_refs = refs.some(len(late)), refs.some(len(kept))
        in_refs = [
            Late(net, ref, late_refs.pop(0)) if how == "load" else ref
            for ref, (_, how) in zip(in_refs, ins)
        ]
        out_refs = [
            Out(ref, kept_refs.pop(0)) if how == "store" else ref
            for ref, (_, how) in zip(out_refs, outs)
        ]
        body(net, Refs(in_refs), Refs(out_refs), refs)
        for copy in net.stores:
            copy.wait()

    return pl.pallas_call(
        kernel,
        name=name,
        out_shape=[o for o, _ in outs],
        in_specs=[spec(how) for _, how in ins],
        out_specs=[spec(how) for _, how in outs],
        scratch_shapes=vmem(late + kept + list(scratch))
        + [
            pltpu.SemaphoreType.DMA((copies,)),
            pltpu.SemaphoreType.DMA((copies,)),
            pltpu.SemaphoreType.DMA((loads + len(late) + len(kept),)),
            pltpu.SemaphoreType.REGULAR,
        ],
        compiler_params=pltpu.CompilerParams(
            collective_id=number, has_side_effects=True, vmem_limit_bytes=60 * 2**20
        ),
    )(*[array for array, _ in ins])


def shape(*dims, kind=F32):
    return jax.ShapeDtypeStruct(dims, kind)


def blocks(count, width, body):
    def step(i, carry):
        body(pl.ds(pl.multiple_of(i * width, width), width))
        return carry

    lax.fori_loop(0, count, step, 0)


class Refs:
    def __init__(self, refs):
        self.refs = list(refs)

    def one(self):
        return self.refs.pop(0)

    def some(self, count):
        return [self.refs.pop(0) for _ in range(count)]


def own_rows(core):
    return pl.ds(pl.multiple_of(core * 256, 256), 256)


def forward_self(
    normed, columns, weights, rows, gain, text_blocks, text_rows, text_key, text_value
):
    ins = [(columns, "hbm"), (normed, "load")] + [(weight, "load") for weight in weights]
    ins += [(rows, "load"), (gain, "vmem"), (text_blocks, "hbm")]
    ins += [(text_rows, "load"), (text_key, "load"), (text_value, "load")]
    outs = [(shape(256, 2048), "store"), (shape(512, 2048, kind=BF16), "store")]
    outs += [(shape(4, 4, 32, 256), "vmem")] + [(shape(32, 512, kind=BF16), "vmem")] * 2
    outs += [(shape(512, 512, kind=BF16), "store")] * 4
    outs += [(shape(2, 512, 2048, kind=BF16), "store")]
    scratch = list(TensorSum.SCRATCH + TensorSum.HALF) + [((4, 32, 1024), F32)]
    scratch += [((2, 512, 1024), F32)] * 2

    def body(net, in_refs, out_refs, refs):
        columns_hbm, late_normed, late_weights = in_refs.one(), in_refs.one(), in_refs.some(4)
        late_rows, gain_ref, text_ref, *late_text = in_refs.some(6)
        total, normed, columns_ref, *text_outs = out_refs.some(5)
        attention, beside = out_refs.some(4), out_refs.one()
        sum_scratch, half, got = refs.some(4), refs.one(), refs.one()
        every([late_normed] + late_weights, "start")
        net.greet(NEAR + ALL)
        own = net.load(text_ref.at[net.x], got.at[0])
        first = [net.push(text_ref.at[(net.x + k) % 4], got.at[k], "x", k) for k in (1, 2, 3)]
        gather = Gather(net, columns_hbm, (1, -1), beside.vmem, refs.one(), refs.one())
        normed_in = late_normed.ref()
        for late, out in zip(late_weights[:3], attention):
            out.vmem[...] = low(product(normed_in[...], late.ref()[...]))
        query_ref, keys_ref, values_ref, mixed_ref = [out.vmem for out in attention]
        for _, at, to in each_head(256, 256):
            probs = attend_probs(query_ref[at], keys_ref[to], None)
            mixed_ref[at] = low(product(low(probs), values_ref[to]))
        for out in attention:
            net.store(out)
        output_ref = late_weights[3].ref()
        share = lambda core, n: product(
            mixed_ref[own_rows(core), :], output_ref[:, pl.ds(n * 512, 512)]
        )
        rows_ref, total_ref = late_rows.vmem, total.vmem

        def epilogue(at, value):
            value = rows_ref[at, :] + value
            total_ref[at, :] = value
            return layer_norm(value, gain_ref[...])

        work = TensorSum(net, share, epilogue, normed.vmem, sum_scratch, half)
        work.begin()
        late_rows.start()
        every(late_text, "start")
        work.exchange()
        own.wait()
        for copy in first:
            copy.wait_recv()
        cut = lambda y: pl.ds(pl.multiple_of(y * 256, 256), 256)
        kept = net.load(got.at[:, :, cut(net.y)], columns_ref.at[0])
        second = [
            net.push(got.at[:, :, cut((net.y + k) % 4)], columns_ref.at[k], "y", k)
            for k in (1, 2, 3)
        ]
        text_rows_ref = late_text[0].ref()
        for weight, out in zip(late_text[1:], text_outs):
            out[...] = low(product(text_rows_ref[...], weight.ref()[...]))
        late_rows.ref()
        work.work(gather.hand)
        net.store(total)
        gather.finish()
        net.store(beside)
        work.finish()
        net.store(normed)
        kept.wait()
        for copy in second:
            copy.wait_recv()
        for copy in first + second:
            copy.wait_send()

    copies, loads = TensorSum.COPIES + 22, TensorSum.LOADS + 2
    return call(body, ins, outs, scratch, copies, loads, 0, "forward_self")


def forward_cross(
    columns, normed, weights, keys, values, present, rows, gain, upstream, contract, expand
):
    ins = [(columns, "hbm"), (normed, "load")] + [(weight, "load") for weight in weights]
    ins += [(keys, "vmem"), (values, "vmem"), (present, "vmem")]
    ins += [(rows, "load"), (gain, "vmem"), (upstream, "load"), (contract, "load")]
    ins += [(expand, "load")]
    outs = [(shape(256, 2048), "store"), (shape(512, 2048, kind=BF16), "store")]
    outs += [(shape(512, 2048, kind=BF16), "store")] * 2
    outs += [(shape(512, 512, kind=BF16), "store")] * 2
    outs += [(shape(1, 512, 2048, kind=BF16), "store")]
    scratch = list(TensorSum.SCRATCH + TensorSum.HALF) + [((512, 2048), F32)]
    scratch += [((1, 512, 1024), F32)] * 2

    def body(net, in_refs, out_refs, refs):
        columns_hbm, late_normed, late_query, late_output = in_refs.some(4)
        keys_ref, values_ref, present_ref = in_refs.some(3)
        late_rows, gain_ref, late_upstream, late_contract, late_expand = in_refs.some(5)
        total, normed, active, grad_raised, query, mixed, beyond = out_refs.some(7)
        every([late_normed, late_query, late_output], "start")
        net.greet(NEAR + [("x", 2)])
        query_ref, mixed_ref = query.vmem, mixed.vmem
        query_ref[...] = low(product(late_normed.ref()[...], late_query.ref()[...]))
        for item, at, to in each_head(256, 16):
            probs = attend_probs(query_ref[at], keys_ref[to], present_ref[pl.ds(item, 1), :])
            mixed_ref[at] = low(product(low(probs), values_ref[to]))
        net.store(query)
        net.store(mixed)
        output_ref = late_output.ref()
        share = lambda core, n: product(
            mixed_ref[own_rows(core), :], output_ref[:, pl.ds(n * 512, 512)]
        )
        rows_ref, total_ref = late_rows.vmem, total.vmem

        def epilogue(at, value):
            value = rows_ref[at, :] + value
            total_ref[at, :] = value
            return layer_norm(value, gain_ref[...])

        work = TensorSum(net, share, epilogue, normed.vmem, refs.some(4), refs.one())
        grad_ref = refs.one()
        gather = Gather(net, columns_hbm, (2,), beyond.vmem, refs.one(), refs.one())
        work.begin()
        every([late_upstream, late_contract, late_rows, late_expand], "start")
        work.exchange()
        upstream_ref, contract_ref = late_upstream.ref(), late_contract.ref()

        def part(at):
            grad_ref[:, at] = back_product(upstream_ref[...], contract_ref[at, :])

        blocks(8, 256, part)
        late_rows.ref()
        expand_ref = late_expand.ref()

        def hidden(core):
            rows = own_rows(core)

            def part(at):
                raised = product(normed.vmem[rows, :], expand_ref[:, at])
                inner = raised * (0.7978845608028654 + 0.035677408136300125 * raised * raised)
                bend = jnp.tanh(inner)
                active.vmem[rows, at] = low(0.5 * raised * (1.0 + bend))
                slope = 0.7978845608028654 + 0.10703222440890037 * raised * raised
                slope = 0.5 * (1.0 + bend) + 0.5 * raised * (1.0 - bend * bend) * slope
                grad_raised.vmem[rows, at] = low(grad_ref[rows, at] * slope)

            blocks(8, 256, part)

        work.work(gather.hand)
        net.store(total)
        gather.finish()
        net.store(beyond)
        hidden(net.core)
        work.finish()
        net.store(normed)
        hidden(1 - net.core)
        net.store(active)
        net.store(grad_raised)

    return call(
        body, ins, outs, scratch, TensorSum.COPIES + 8, TensorSum.LOADS, 1, "forward_cross"
    )


def norm_back_sum(net, share, x_ref, gain_ref, rows_ref, low_ref, gain_sum, scratch, half):
    gain_sum[...] = jnp.zeros_like(gain_sum)

    def epilogue(at, total):
        row_grad, terms = norm_back(x_ref[at, :], gain_ref[...], total)
        gain_sum[...] += terms
        result = rows_ref[at, :] + row_grad
        rows_ref[at, :] = result
        return result

    return TensorSum(net, share, epilogue, low_ref, scratch, half)


def every(parts, step):
    for part in parts:
        getattr(part, step)()


def backward_first(grad_raised, expand, x_rows, gain, extra, left, right, contract):
    ins = [(grad_raised, "load"), (expand, "load"), (x_rows, "load"), (gain, "vmem")]
    ins += [(extra, "hbm"), (left, "load")]
    ins += [(right, "load"), (contract, "load")]
    outs = [(shape(256, 2048), "hbm"), (shape(512, 2048, kind=BF16), "store")]
    outs += [(shape(8, 2048), "vmem"), (shape(512, 2048), "store")]
    outs += [(shape(4, 128, JOB), "store")] * 4
    scratch = list(TensorSum.SCRATCH + TensorSum.HALF) + list(RingOne.SCRATCH) * 4

    def body(net, in_refs, out_refs, refs):
        late_raised, late_expand, late_x, gain_ref = in_refs.some(4)
        extra_hbm, late_left, late_right = in_refs.some(3)
        late_contract = in_refs.one()
        rows, lows, gain_sum, out_share, *owns = out_refs.some(8)
        sum_scratch, half = refs.some(4), refs.one()
        rings = [
            RingOne(net, late_left.vmem, late_right.vmem, i, i % 2 == 0, owns[i].vmem, refs.some(3))
            for i in range(4)
        ]
        every([late_left, late_right, late_raised, late_expand], "start")
        net.greet(NEAR + RING)
        x_ref, raised_ref, expand_ref = late_x.vmem, late_raised.vmem, late_expand.vmem
        share = lambda core, n: back_product(
            raised_ref[own_rows(core), :], expand_ref[pl.ds(n * 512, 512), :]
        )
        work = norm_back_sum(
            net, share, x_ref, gain_ref, half, lows.vmem, gain_sum, sum_scratch, half
        )
        late_left.ref(), late_right.ref()
        every(rings, "begin")
        late_raised.ref(), late_expand.ref()
        work.begin()
        every([late_contract, late_x], "start")
        work.exchange()
        work.free_half()
        extra_copy = net.load(extra_hbm, half)
        every(rings, "relay")
        right_ref, contract_ref = late_right.ref(), late_contract.ref()

        def part(at):
            out_share.vmem[:, at] = product(right_ref[...], contract_ref[:, at])

        blocks(8, 256, part)
        late_x.ref()
        joins = jnp.where(net.tensor < 2, 1.0, 0.0)

        def join(i, carry):
            at = pl.ds(pl.multiple_of(i * 16, 16), 16)
            to = pl.ds(pl.multiple_of(net.core * 256 + i * 16, 16), 16)
            out_share.vmem[to, :] += x_ref[at, :] * joins
            return carry

        lax.fori_loop(0, 16, join, 0)
        net.store(out_share)
        extra_copy.wait()
        work.work()
        net.stores.append(net.load(half, rows))
        work.finish()
        net.store(lows)
        for ring, own in zip(rings, owns):
            ring.close()
            net.store(own)
        every(rings, "done")

    copies, loads = TensorSum.COPIES + 4 * RingOne.COPIES, 2
    return call(body, ins, outs, scratch, copies, loads, 2, "backward_first")


def backward_second(
    attention, weights, present, x_rows, gain, extra, owns, wide, upstream, mixed, normed, out_share
):
    ones = [(0, i, i % 2 == 0) for i in range(4)] + [(1, 0, True), (2, 0, False)]
    query, keys, values = attention
    ins = [(query, "load"), (keys, "vmem"), (values, "vmem"), (present, "vmem")]
    ins += [(weights[0], "load"), (weights[1], "hbm"), (x_rows, "load"), (gain, "vmem")]
    ins += [(extra, "hbm"), (out_share, "hbm")] + [(own, "hbm") for own in owns]
    ins += [(array, "load") for array in (*wide, upstream, mixed, normed)]
    outs = [(shape(256, 2048), "hbm"), (shape(512, 2048, kind=BF16), "store")]
    outs += [(shape(8, 2048), "vmem")] + [(shape(4, 4, 32, 512), "vmem")] * 2
    outs += [(shape(512, 2048, kind=BF16), "hbm")]
    outs += [(shape(64, JOB), "vmem")] * len(owns)
    outs += [(shape(4, 128, JOB), "store")] * len(ones)
    scratch = list(TensorSum.SCRATCH + TensorSum.HALF) + [TensorSum.SCRATCH[0]]
    scratch += [((512, 512), BF16)]
    scratch += list(RingTwo.SCRATCH + RingTwo.PARTS) * len(owns)
    scratch += list(RingOne.SCRATCH) * len(ones)

    def body(net, in_refs, out_refs, refs):
        late_cross, keys_ref, values_ref, present_ref = in_refs.some(4)
        late_weight, output_hbm, late_x, gain_ref, extra_hbm, out_share_ref = in_refs.some(6)
        own_refs, late_wide, late_narrow = in_refs.some(len(owns)), in_refs.some(2), in_refs.some(3)
        rows, lows, gain_sum, keys_all, values_all, layer_out = out_refs.some(6)
        final_refs, nexts = out_refs.some(len(owns)), out_refs.some(len(ones))
        mine, got_core, got_z, got_rows = refs.some(4)
        half, got_z_two, grad_mixed = refs.some(3)
        grad_cross = late_cross.vmem
        twos = [
            RingTwo(net, own, i % 2 == 0, final_refs[i], refs.some(2), refs.one())
            for i, own in enumerate(own_refs)
        ]
        pairs = [[late.vmem for late in late_wide], [late.vmem for late in late_narrow[:2]]]
        pairs.append([late_narrow[2].vmem, grad_cross])
        rings = [
            RingOne(net, *pairs[p], c, x_first, nexts[i].vmem, refs.some(3))
            for i, (p, c, x_first) in enumerate(ones)
        ]
        every(late_wide + late_narrow[:2], "start")
        output_copy = net.load(output_hbm, lows.vmem)
        every([late_cross, late_weight, late_narrow[2], late_x], "start")
        net.greet(NEAR + ALL + [("zhi", 1)])
        weight_ref = late_weight.vmem
        share = lambda core, n: back_product(
            grad_cross[own_rows(core), :], weight_ref[pl.ds(n * 512, 512), :]
        )
        work = norm_back_sum(
            net,
            share,
            late_x.vmem,
            gain_ref,
            half,
            lows.vmem,
            gain_sum,
            (mine, got_core, got_z, got_rows),
            half,
        )
        layer = TensorSum(
            net,
            out_share_ref,
            lambda at, total: total,
            lows.vmem,
            (mine, got_core, got_z_two, got_rows),
        )
        every(twos, "begin")
        every(late_wide, "ref")
        every(rings[:4], "begin")
        every(late_narrow[:2], "ref")
        output_copy.wait()
        grad_mixed[...] = low(back_product(late_narrow[0].vmem[...], lows.vmem[...]))
        query_ref = late_cross.ref()
        for item, at, to in each_head(256, 16):
            grad_query, grad_keys, grad_values = attend_backward(
                query_ref[at],
                keys_ref[to],
                values_ref[to],
                present_ref[pl.ds(item, 1), :],
                grad_mixed[at],
            )
            grad_cross[at] = grad_query
            keys_all[0, 0, to[0], to[1]] = grad_keys.astype(F32)
            values_all[0, 0, to[0], to[1]] = grad_values.astype(F32)
        late_weight.ref()
        work.begin()
        texts = [
            net.push(ref.at[0, 0], ref.at[0, k], axis, k)
            for ref, axis in ((keys_all, "x"), (values_all, "y"))
            for k in (1, 2, 3)
        ]
        every(rings[4:5], "begin")
        late_narrow[2].ref()
        every(rings[5:], "begin")
        work.exchange()
        work.free_half()
        extra_copy = net.load(extra_hbm, half)
        every(twos, "relay")
        every(rings, "relay")
        for copy in texts:
            copy.wait_recv()
        texts += [
            net.push(ref.at[0], ref.at[k], axis, k)
            for ref, axis in ((keys_all, "y"), (values_all, "x"))
            for k in (1, 2, 3)
        ]
        late_x.ref()
        extra_copy.wait()
        work.work()
        net.stores.append(net.load(half, rows))
        work.finish()
        net.release("core")
        lows_copy = net.load(lows.vmem, lows.hbm)
        net.await_release()
        layer.begin()
        layer.exchange()
        every(twos, "third")
        for ring, own in zip(rings[:2] + rings[4:], nexts[:2] + nexts[4:]):
            ring.close()
            net.store(own)
        every(twos, "finish")
        lows_copy.wait()
        layer.work()
        layer.finish()
        net.stores.append(net.load(lows.vmem, layer_out))
        for ring, own in zip(rings[2:4], nexts[2:4]):
            ring.close()
            net.store(own)
        for copy in texts[6:]:
            copy.wait_recv()
        for copy in texts:
            copy.wait_send()
        every(rings, "done")

    copies = 2 * TensorSum.COPIES + 12 + len(owns) * RingTwo.COPIES + len(ones) * RingOne.COPIES
    loads = TensorSum.LOADS + 5 + len(owns) * RingTwo.LOADS
    return call(body, ins, outs, scratch, copies, loads, 3, "backward_second")


def backward_last(
    attention, weights, upstream, normed, beside, beyond, x_rows, gain, extra, keep, owns, text_grad, sums
):
    count = 1
    ins = [(array, "load") for array in attention] + [(weights[3], "hbm")]
    ins += [(weight, "hbm") for weight in weights[:3]]
    ins += [(upstream, "load"), (normed, "load"), (beside, "hbm"), (beyond, "hbm"), (x_rows, "load"), (gain, "vmem"), (extra, "hbm"), (keep, "vmem")]
    ins += [(text_grad, "hbm"), (sums, "vmem")] + [(own, "hbm") for own in owns]
    outs = [(shape(512, 2048, kind=BF16), "store"), (shape(8, 2048), "vmem")]
    outs += [(shape(128, 1024), "vmem")] + [(shape(64, JOB), "vmem")] * (len(owns) + count)
    outs += [(shape(4, 64, RingHeads.WIDTH), "vmem")]
    scratch = list(TensorSum.SCRATCH + TensorSum.HALF) + [((512, 512), BF16)] * 4
    scratch += [((512, 2048), BF16)] * 3 + [((512, RingHeads.WIDTH), BF16)] * 4
    scratch += [((3, 512, RingHeads.WIDTH), F32)] * 2
    scratch += list(RingHeads.SCRATCH + RingHeads.LAST)
    scratch += [((16, 2048), F32), ((128, 1024), F32), ((9, 8, 2048), F32)]
    scratch += list(RingTwo.SCRATCH + RingTwo.PARTS) * len(owns)
    scratch += (list(RingTwo.SCRATCH + RingOne.SCRATCH) + [((4, 128, JOB), F32)]) * count

    def body(net, in_refs, out_refs, refs):
        late_attention, late_output, weights_hbm = in_refs.some(4), in_refs.one(), in_refs.some(3)
        late_upstream, late_normed, beside_hbm, beyond_hbm = in_refs.some(4)
        late_x, gain_ref, extra_hbm, keep_ref, text_ref, sums_ref = in_refs.some(6)
        own_refs = in_refs.some(len(owns))
        image, small_ref, text_out = out_refs.some(3)
        old_refs, new_refs, heads_out = out_refs.some(len(owns)), out_refs.some(count), out_refs.one()
        sum_scratch, half, grad_mixed, grads = refs.some(4), refs.one(), refs.one(), refs.some(3)
        rooms, rights, (leaving, arriving) = refs.some(3), refs.some(4), refs.some(2)
        heads_scratch, heads_last = refs.some(4), refs.some(2)
        acc_ref, got_text, got_small = refs.some(3)
        old = [
            RingTwo(net, own, i % 2 == 0, old_refs[i], refs.some(2), refs.one())
            for i, own in enumerate(own_refs)
        ]
        ones, twos = [], []
        for i in range(count):
            two_scratch, one_scratch, own = refs.some(2), refs.some(3), refs.one()
            left, right = late_upstream.vmem, late_attention[3].vmem
            ones.append(RingOne(net, left, right, 0, False, own, one_scratch))
            twos.append(RingTwo(net, own, False, new_refs[i], two_scratch))
        lefts = [late_normed.vmem] + rooms
        heads = RingHeads(net, lefts, rights, heads_out, heads_scratch, heads_last)
        output_copy = net.load(late_output, image.vmem)
        every([late_upstream, late_attention[3]] + late_attention[:3], "start")
        weight_copies = [
            net.load(weight.at[pl.ds(n * 512, 512)], room.at[:, pl.ds(n * 512, 512)])
            for weight, room in zip(weights_hbm, rooms)
            for n in range(4)
        ]
        late_normed.start()
        net.greet(NEAR + ALL + [("zhi", 1)])
        acc_ref[...] = jnp.zeros_like(acc_ref)
        x_ref, extra_ref = late_x.vmem, half

        def epilogue(at, total):
            row_grad, terms = norm_back(x_ref[at, :], gain_ref[...], total)
            result = extra_ref[at, :] + row_grad
            kept = keep_ref[at, :] > 0.5
            acc_ref[0:8, :] += terms
            acc_ref[8:16, :] += jnp.where(kept, 0.0, result)
            return jnp.where(kept, result, 0.0)

        text_rows = lambda z: pl.ds(pl.multiple_of(z * 128, 128), 128)
        text_push = net.push(text_ref.at[text_rows(1 - net.z)], got_text, "zhi")
        every(old, "begin")
        every([late_upstream, late_attention[3]], "ref")
        ones[0].begin()
        output_copy.wait()
        grad_mixed[...] = low(back_product(late_upstream.vmem[...], image.vmem[...]))
        late_x.start()
        text_copy = net.load(text_ref.at[text_rows(net.z)], text_out)
        query_ref, keys_ref, values_ref = [late.ref() for late in late_attention[:3]]
        every(old, "relay")
        for _, at, to in each_head(256, 256):
            found = attend_backward(
                query_ref[at], keys_ref[to], values_ref[to], None, grad_mixed[at]
            )
            for ref, value in zip(grads, found):
                ref[at] = value
        head = lambda x: pl.ds(pl.multiple_of(x * HEAD, HEAD), HEAD)
        for i, ref in enumerate(grads):
            columns = pl.ds(i * HEAD, HEAD)
            rights[0][:, columns] = ref[:, head(net.x)]
            for k in (1, 2, 3):
                leaving[k - 1, :, columns] = ref[:, head((net.x + k) % 4)].astype(F32)
        spread = [
            net.push(leaving.at[k - 1], arriving.at[k - 1], "x", k) for k in (1, 2, 3)
        ]
        for copy in weight_copies:
            copy.wait()

        def share(core, n):
            block, total = pl.ds(n * 512, 512), 0.0
            for ref, weight in zip(grads, rooms):
                total = total + back_product(ref[own_rows(core), :], weight[:, block])
            return total

        work = TensorSum(net, share, epilogue, image.vmem, sum_scratch, half)
        work.begin()
        others = (beside_hbm.at[0], beyond_hbm.at[0], beside_hbm.at[1])
        left_copies = [net.load(source, room) for source, room in zip(others, rooms)]
        work.exchange()
        work.free_half()
        extra_copy = net.load(extra_hbm, half)
        every(ones, "relay")
        late_normed.ref()
        for copy in left_copies:
            copy.wait()
        for k in range(3):
            spread[k].wait_recv()
            rights[k + 1][...] = low(arriving[k])
        heads.begin()
        late_x.ref()
        extra_copy.wait()
        work.work(lambda j: heads.relay() if j == 3 else every(old[3 * j : 3 * j + 3], "third"))
        got_small[0] = sums_ref[...]
        got_small[0, 0:1, :] = jnp.sum(acc_ref[0:8, :], axis=0, keepdims=True)
        got_small[0, 3:4, :] = jnp.sum(acc_ref[8:16, :], axis=0, keepdims=True)
        by_core = net.push(got_small.at[0], got_small.at[1], "core")
        work.finish()
        net.store(image)
        by_core.wait()
        got_small[0] += got_small[1]
        by_x = [net.push(got_small.at[0], got_small.at[1 + k], "x", k) for k in (1, 2, 3)]
        for one, two in zip(ones, twos):
            one.close()
            two.begin()
        heads.close()
        heads.swap()
        every(old, "finish")
        for copy in by_x:
            copy.wait()
        got_small[0] += got_small[2] + got_small[3] + got_small[4]
        by_y = [net.push(got_small.at[0], got_small.at[4 + k], "y", k) for k in (1, 2, 3)]
        every(twos, "relay")
        for copy in by_y:
            copy.wait()
        got_small[0] += got_small[5] + got_small[6] + got_small[7]
        by_z = net.push(got_small.at[0], got_small.at[8], "zhi")
        every(twos, "third")
        heads.third()
        text_copy.wait()
        text_push.wait()
        text_out[...] += got_text[...]
        by_z.wait()
        small_ref[...] = got_small[0] + got_small[8]
        every(twos, "finish")
        heads.finish()
        heads.done()
        for copy in spread:
            copy.wait_send()
        every(ones, "done")

    copies = TensorSum.COPIES + 9 + (len(owns) + count) * RingTwo.COPIES + count * RingOne.COPIES
    copies += RingHeads.COPIES + RingHeads.COPIES_LAST + 3
    loads = 18 + len(owns) * RingTwo.LOADS
    return call(body, ins, outs, scratch, copies, loads, 4, "backward_last")


def shards(
    image,
    text,
    masked,
    text_len,
    cotangent,
    self_query,
    self_key,
    self_value,
    self_output,
    text_query,
    text_key,
    text_value,
    text_output,
    expand,
    contract,
    first_gain,
    second_gain,
    third_gain,
    mask_token,
):
    items, length, width = image.shape
    words = text.shape[1]
    count = items * length
    core = lax.axis_index("tensor") % 2
    gains = [g.reshape(1, width) for g in (first_gain, second_gain, third_gain)]
    own = lambda rows: lax.dynamic_slice_in_dim(rows, core * length, length, axis=0)

    text_rows = text.reshape(items * words, text.shape[2])
    text_blocks = text_rows.astype(F32).reshape(items * words, 4, -1).transpose(1, 0, 2)
    upstream = cotangent.reshape(count, width)

    hidden = masked.reshape(count, 1) == 1
    start = jnp.where(hidden, mask_token[None, :], image.reshape(count, width).astype(F32))
    normed_one = low(layer_norm(start, first_gain))
    weights = (self_query, self_key, self_value, self_output)
    start_own = own(start)
    columns = lax.dynamic_slice_in_dim(normed_one, core * (width // 2), width // 2, axis=1)
    columns = columns.astype(F32)
    first, normed_two, text_columns, cross_keys, cross_values, *attention, beside = forward_self(
        normed_one,
        columns,
        weights,
        start_own,
        gains[1],
        text_blocks,
        text_rows,
        text_key,
        text_value,
    )
    text_columns = low(text_columns.reshape(-1, text_columns.shape[-1]))

    present = (jnp.arange(words)[None, :] < text_len[:, None]).astype(F32)
    second, normed_three, active, grad_raised, cross_query, cross_rows, beyond = forward_cross(
        columns,
        normed_two,
        (text_query, text_output),
        cross_keys,
        cross_values,
        present,
        first,
        gains[2],
        upstream,
        contract,
        expand,
    )
    grad_second, cross_out_grad, third_sum, out_share, *owns = backward_first(
        grad_raised,
        expand,
        second,
        gains[2],
        own(upstream).astype(F32),
        upstream,
        active,
        contract,
    )
    grad_first, self_out_grad, second_sum, text_k, text_v, layer_out, *rest = backward_second(
        (cross_query, cross_keys, cross_values),
        (text_query, text_output),
        present,
        first,
        gains[1],
        grad_second,
        owns,
        (normed_three, grad_raised),
        cross_out_grad,
        cross_rows,
        normed_two,
        out_share,
    )
    contract_t, owns = rest[:4], rest[4:]
    text_v = text_v.transpose(1, 0, 2, 3)
    gathered = low(jnp.concatenate([text_k, text_v], axis=3).reshape(text_columns.shape[0], -1))
    text_grads = outer_sum(text_columns, gathered)

    sums = jnp.zeros((8, width), F32)
    sums = sums.at[1].set(jnp.sum(second_sum, axis=0)).at[2].set(jnp.sum(third_sum, axis=0))
    keep = 1.0 - own(masked.reshape(count, 1)).astype(F32)
    image_grad, small, text_grads, *rest = backward_last(
        attention,
        weights,
        self_out_grad,
        normed_one,
        beside,
        beyond,
        start_own,
        gains[0],
        grad_first,
        keep,
        owns,
        text_grads,
        sums,
    )
    expand_grad, (to, tq, so, heads) = rest[:4], rest[4:]
    heads = heads.reshape(4, -1, 3, HEAD).transpose(2, 1, 0, 3)
    sq, sk, sv = heads.reshape(3, heads.shape[1], -1)

    share = width // 32
    small = lax.dynamic_slice_in_dim(small, lax.axis_index("dp") * share, share, axis=1)
    cut = text_grads.shape[1] // 2
    joined = lambda parts: jnp.concatenate(parts, axis=1)
    return (
        layer_out.reshape(image.shape),
        image_grad.reshape(image.shape),
        sq,
        sk,
        sv,
        so.T,
        tq,
        text_grads[:, :cut],
        text_grads[:, cut:],
        to.T,
        joined(expand_grad),
        joined(contract_t).T,
        small[0],
        small[1],
        small[2],
        small[3],
    )


def solution(mesh):
    rows, split = P("dp", None, None), P(None, "tensor")
    turned, grads, grads_t = P("tensor", None), P("dp", "tensor"), P("tensor", "dp")
    ins = (rows, rows, P("dp", None), P("dp"), rows, split, split, split, turned)
    ins += (split, split, split, turned, split, turned, P(), P(), P(), P())
    outs = (rows, rows, grads, grads, grads, grads_t, grads, grads, grads, grads_t)
    outs += (grads, grads_t, P("dp"), P("dp"), P("dp"), P("dp"))
    return jax.shard_map(shards, mesh=mesh, in_specs=ins, out_specs=outs, check_vma=False)
```
